32 devices in a mesh: tm: 4 (over z), chan: 8 (over y, x, core).
Axes of the slice: x: 2, y: 2, z: 4, core: 2. Of those that a mesh axis runs over, the one named last changes fastest.
Arguments:
- record: float32 [4096, 1024], P('tm', 'chan'), may hold values from -6 to 6
- fk_mask: int32 [512, 1024], P('chan'), may hold values from 0 to 1, as said below
- tap_table: bfloat16 [8, 8], replicated, may hold values from -0.1875 to 0.1875
- delay_whole: int32 [128, 128], replicated, may hold values from -16 to 16
- tap_index: int32 [128, 128], replicated, may hold values from 0 to 7
Outputs:
- beams: bfloat16 [16, 128, 4096], P('chan', None, 'tm')
The draws below stay inside these ranges and needn't reach their ends.
Inputs may be any that keep to these rules, and one draw needn't show every extreme that they name: `fk_mask`: 0 or 1; in each row the ones form one contiguous band of signed wavenumbers (k, or k - 1024 for k >= 512) that contains zero.
All inputs are finite; a program needn't handle non-finite values.
Results may differ from the reference program's by a relative error of at most 0.0049.
Values may be sent and summed in bfloat16 or wider, within the bound.
A program may use at most 128 MiB of HBM per device.

```python
import jax
import jax.numpy as jnp
from jax import lax

CHANNELS = 1024
BLOCK = 1024
HALF_T = 512
SAMPLES = 4096
SLOW = 128
SUBARRAY = 128
STRIDE = 64
SUBARRAYS = 16
TAPS = 8
FRACS = 8
LAG = 16
RIM = 20
LAGS = 40
N_TM = 4


def draw_fk_mask(key, part):
    low_key, high_key = jax.random.split(jax.random.fold_in(key, 3))
    lowest = -jax.random.randint(low_key, (HALF_T, 1), CHANNELS // 8, CHANNELS // 2, dtype=jnp.int32)
    highest = jax.random.randint(high_key, (HALF_T, 1), CHANNELS // 8, CHANNELS // 2, dtype=jnp.int32)
    wavenumber = jnp.arange(CHANNELS, dtype=jnp.int32)
    signed = jnp.where(wavenumber < CHANNELS // 2, wavenumber, wavenumber - CHANNELS)[None, :]
    return ((signed >= lowest) & (signed <= highest)).astype(jnp.int32)


def delay_units(key):
    base_key = jax.random.fold_in(key, 7)
    slope_key, order_key, jitter_key = jax.random.split(base_key, 3)
    steepest = LAG * FRACS // (SUBARRAY // 2)
    slopes = jax.random.randint(slope_key, (SLOW,), -steepest, steepest + 1, dtype=jnp.int32)
    chosen = jax.random.permutation(order_key, SLOW)
    row_ids = jnp.arange(SLOW, dtype=jnp.int32)
    slopes = jnp.where(row_ids == chosen[0], steepest, slopes)
    slopes = jnp.where(row_ids == chosen[1], -steepest, slopes)
    jitter = jax.random.randint(jitter_key, (SLOW, SUBARRAY), 0, FRACS, dtype=jnp.int32)
    offset = jnp.arange(SUBARRAY, dtype=jnp.int32) - SUBARRAY // 2
    return slopes[:, None] * offset[None, :] + jitter


def draw_delay_whole(key, part):
    return jnp.floor_divide(delay_units(key), FRACS)


def draw_tap_index(key, part):
    return jnp.remainder(delay_units(key), FRACS)


def steps_of(rng, extent, cuts, smallest, largest):
    def one(position, blocks):
        draws = jax.random.uniform(jax.random.fold_in(jax.random.fold_in(rng, 6), position), (blocks,), jnp.float32, smallest / len(cuts), largest / len(cuts))
        return jnp.repeat(jnp.exp(draws), extent[position] // blocks).reshape((-1,) + (1,) * (len(extent) - position - 1))

    factor_of = one(*cuts[0])
    for cut in cuts[1:]:
        factor_of = factor_of * one(*cut)
    return factor_of


def scatter_about(own_key, dims, spread, bound, cuts=(), held_as=jnp.bfloat16):
    loudness = steps_of(own_key, dims, cuts, -0.22, 0.18) if cuts else 1.0
    result = jax.random.normal(own_key, dims, jnp.float32) * spread * loudness
    return jnp.minimum(jnp.maximum(result, -bound), bound).astype(held_as)


def setup_inputs(seed: int = 0) -> dict:
    seeds = jax.random.split(jax.random.key(seed), 6)
    return {
        "record": scatter_about(seeds[0], (SAMPLES, CHANNELS), 1.0, 6.0, ((0, 4), (1, 8)), jnp.float32),
        "fk_mask": draw_fk_mask(jax.random.fold_in(seeds[5], 71), 0),
        "tap_table": scatter_about(seeds[2], (FRACS, TAPS), (SUBARRAY * TAPS) ** -0.5, 0.1875),
        "delay_whole": draw_delay_whole(jax.random.fold_in(seeds[5], 71), 0),
        "tap_index": draw_tap_index(jax.random.fold_in(seeds[5], 71), 0),
    }


def flip_wavenumbers(rows_table):
    return jnp.roll(rows_table[:, ::-1], 1, axis=1)


def lag_weights(tap_table, delay_whole, tap_index):
    fractions = jnp.arange(FRACS, dtype=jnp.int32)
    one_hot = (tap_index[:, :, None] == fractions[None, None, :]).astype(jnp.float32)
    coeffs = jnp.einsum("sjr,rp->sjp", one_hot, tap_table.astype(jnp.float32))
    lag_ids = jnp.arange(LAGS, dtype=jnp.int32)
    weights = jnp.zeros((delay_whole.shape[0], LAGS, delay_whole.shape[1]), jnp.float32)
    for tap_pos in range(TAPS):
        target = delay_whole + (tap_pos + LAG)
        weights = weights + jnp.where(lag_ids[None, :, None] == target[:, None, :], coeffs[:, None, :, tap_pos], 0.0)
    return weights.astype(jnp.bfloat16)


def reference(record, fk_mask, tap_table, delay_whole, tap_index):
    half_band = fk_mask.astype(jnp.float32)
    flipped = flip_wavenumbers(half_band)
    zero_row = (half_band[0] * flipped[0])[None, :]
    nyquist = jnp.zeros((1, CHANNELS), jnp.float32)
    full_band = jnp.concatenate([zero_row, half_band[1:], nyquist, flipped[1:][::-1]], axis=0)
    pieces = []
    for block_id in range(N_TM):
        segment = record[block_id * BLOCK:(block_id + 1) * BLOCK]
        spectrum = jnp.fft.fft2(segment) * full_band
        pieces.append(jnp.real(jnp.fft.ifft2(spectrum)))
    filtered = jnp.concatenate(pieces, axis=0).astype(jnp.bfloat16)
    weights = lag_weights(tap_table, delay_whole, tap_index)
    columns = jnp.pad(filtered.T, ((0, STRIDE), (RIM, RIM)))
    time_span = SAMPLES + 2 * RIM
    groups = columns.reshape(SUBARRAYS + 1, STRIDE, time_span)
    subarrays = jnp.concatenate([groups[:-1], groups[1:]], axis=1)
    by_channel = jnp.transpose(subarrays, (1, 0, 2)).astype(jnp.float32)

    def add_lag(beam_sum, lag_id):
        window = lax.dynamic_slice_in_dim(by_channel, lag_id + 1, SAMPLES, 2).reshape(SUBARRAY, SUBARRAYS * SAMPLES)
        chosen = lax.dynamic_index_in_dim(weights, lag_id, 1, keepdims=False).astype(jnp.float32)
        return beam_sum + jnp.dot(chosen, window, precision=lax.Precision.HIGHEST, preferred_element_type=jnp.float32), None

    beam_sum = lax.scan(add_lag, jnp.zeros((SLOW, SUBARRAYS * SAMPLES), jnp.float32), jnp.arange(LAGS, dtype=jnp.int32))[0]
    return jnp.transpose(beam_sum.reshape(SLOW, SUBARRAYS, SAMPLES), (1, 0, 2)).astype(jnp.bfloat16)
```

```python
import functools
import math

import jax
import jax.numpy as jnp
import ml_dtypes
import numpy as np
from jax import lax
from jax.experimental import pallas as pl
from jax.experimental.pallas import tpu as pltpu
from jax.sharding import PartitionSpec as P

SUBARRAY = 128
STRIDE = 64
TAPS = 8
FRACS = 8
LAG = 16
RIM = 20
LAGS = 40
GROUPS = 5
SHIFTS = LAGS // GROUPS


def split_table(table):
    high = table.astype(ml_dtypes.bfloat16)
    low = (table - high.astype(np.float64)).astype(ml_dtypes.bfloat16)
    return high, low


def time_table(block_len, devices):
    half_len = block_len // 2
    freq = np.arange(half_len)
    phase = (freq[:, None] * np.arange(block_len)[None, :] % block_len) * (2.0 * math.pi / block_len)
    both = np.stack([np.cos(phase), -np.sin(phase)])
    both = both.reshape(2, devices, half_len // devices, block_len).transpose(1, 0, 2, 3)
    return split_table(both.reshape(block_len, block_len))


def local_table(local_ch):
    ids = np.arange(local_ch)
    phase = (ids[:, None] * ids[None, :] % local_ch) * (2.0 * math.pi / local_ch)
    c, s = np.cos(phase), np.sin(phase)
    return np.block([[c, -s], [s, c]]).astype(np.float32)


def twist_tables(devices, local_ch):
    phase = np.arange(devices)[:, None] * np.arange(local_ch)[None, :] * (2.0 * math.pi / (devices * local_ch))
    return np.cos(phase).astype(np.float32), np.sin(phase).astype(np.float32)


def small_dft(re, im, sign):
    count = len(re)
    if count == 1:
        return re, im
    even_re, even_im = small_dft(re[0::2], im[0::2], sign)
    odd_re, odd_im = small_dft(re[1::2], im[1::2], sign)
    out_re, out_im = [None] * count, [None] * count
    half = count // 2
    for k in range(half):
        if k == 0:
            tr, ti = odd_re[k], odd_im[k]
        elif 4 * k == count:
            tr, ti = -sign * odd_im[k], sign * odd_re[k]
        else:
            c = math.cos(2.0 * math.pi * k / count)
            s = sign * math.sin(2.0 * math.pi * k / count)
            tr = odd_re[k] * c - odd_im[k] * s
            ti = odd_im[k] * c + odd_re[k] * s
        out_re[k], out_im[k] = even_re[k] + tr, even_im[k] + ti
        out_re[k + half], out_im[k + half] = even_re[k] - tr, even_im[k] - ti
    return out_re, out_im


def flip_wavenumbers(rows_table):
    return jnp.roll(rows_table[:, ::-1], 1, axis=1)


def grouped_weights(tap_table, delay_whole, tap_index):
    table = tap_table.astype(jnp.float32)
    coeffs = []
    for tap_pos in range(TAPS):
        value = jnp.zeros(tap_index.shape, jnp.float32)
        for frac in range(FRACS):
            value = jnp.where(tap_index == frac, table[frac, tap_pos], value)
        coeffs.append(value)
    lag = (
        SHIFTS * jnp.arange(GROUPS, dtype=jnp.int32)[:, None, None, None]
        + jnp.arange(SHIFTS, dtype=jnp.int32)[None, None, :, None]
    )
    tap = lag - (delay_whole + LAG)[None, :, None, :]
    weights = jnp.zeros(tap.shape, jnp.float32)
    for tap_pos in range(TAPS):
        weights = jnp.where(tap == tap_pos, coeffs[tap_pos][None, :, None, :], weights)
    rows = GROUPS * delay_whole.shape[0]
    return weights.astype(jnp.bfloat16).reshape(rows, SHIFTS * delay_whole.shape[1])


def dot_f32(left_op, right_op, precision=None):
    return jnp.dot(left_op, right_op, precision=precision, preferred_element_type=jnp.float32)


def body(record, fk_mask, tap_table, delay_whole, tap_index):
    block_len, local_ch = record.shape
    devices = lax.axis_size("chan")
    band_rows, channels = fk_mask.shape
    slow_count = delay_whole.shape[0]
    table_hi, table_lo = time_table(block_len, devices)
    table_hi, table_lo = jnp.asarray(table_hi), jnp.asarray(table_lo)

    rec_hi = record.astype(jnp.bfloat16)
    rec_lo = (record - rec_hi.astype(jnp.float32)).astype(jnp.bfloat16)
    first = dot_f32(table_hi, jnp.concatenate([rec_hi, rec_lo], axis=1))
    spectrum = first[:, :local_ch] + first[:, local_ch:] + dot_f32(table_lo, rec_hi)
    sent = spectrum.astype(jnp.bfloat16).reshape(devices, 2 * band_rows, local_ch)
    got = lax.all_to_all(sent, "chan", split_axis=0, concat_axis=0, tiled=True)

    own_band = fk_mask.astype(jnp.float32)
    freq = lax.axis_index("chan") * band_rows + jnp.arange(band_rows, dtype=jnp.int32)
    at_zero = (freq == 0)[:, None]
    band = jnp.where(at_zero, own_band * flip_wavenumbers(own_band), own_band)
    scale = jnp.where(at_zero, 1.0, 2.0) / (block_len * channels)
    band = (band * scale).reshape(band_rows, local_ch, devices).transpose(2, 0, 1)
    band = band.reshape(devices * band_rows, local_ch)

    cos_twist, sin_twist = twist_tables(devices, local_ch)
    mix = local_table(local_ch)
    parts = got.astype(jnp.float32)
    re, im = small_dft(
        [parts[d, :band_rows] for d in range(devices)],
        [parts[d, band_rows:] for d in range(devices)],
        -1.0,
    )
    turned = []
    for d in range(devices):
        c, s = cos_twist[d][None], sin_twist[d][None]
        turned.append(jnp.concatenate([re[d] * c + im[d] * s, im[d] * c - re[d] * s], axis=1))
    wave = dot_f32(jnp.concatenate(turned, axis=0), mix, lax.Precision.HIGH)
    kept = wave * jnp.concatenate([band, band], axis=1)
    back = dot_f32(kept, mix.T, lax.Precision.HIGH).reshape(devices, band_rows, 2 * local_ch)
    re, im = [], []
    for d in range(devices):
        c, s = cos_twist[d][None], sin_twist[d][None]
        b_re, b_im = back[d, :, :local_ch], back[d, :, local_ch:]
        re.append(b_re * c - b_im * s)
        im.append(b_im * c + b_re * s)
    re, im = small_dft(re, im, 1.0)
    reach = SUBARRAY - STRIDE
    slabs = []
    for d in range(devices):
        if d + 1 < devices:
            rim = jnp.concatenate([re[d + 1][:, :reach], im[d + 1][:, :reach]], axis=1)
        else:
            rim = jnp.zeros((band_rows, 2 * reach), jnp.float32)
        slabs.append(jnp.concatenate([re[d], im[d], rim], axis=0).astype(jnp.bfloat16))
    back_got = lax.all_to_all(jnp.stack(slabs), "chan", split_axis=0, concat_axis=0, tiled=True)
    own = back_got[:, : 2 * band_rows].reshape(block_len, local_ch)
    rim = back_got[:, 2 * band_rows :].reshape(devices, band_rows, 2, reach)
    rim = rim.transpose(0, 2, 1, 3).reshape(block_len, reach)
    rows = jnp.concatenate([own, rim], axis=1)
    contract = (((0,), (0,)), ((), ()))
    field = lax.dot_general(rows, table_hi, contract, preferred_element_type=jnp.float32)
    field = field + lax.dot_general(rows, table_lo, contract, preferred_element_type=jnp.float32)
    filtered = field.astype(jnp.bfloat16)

    count = lax.axis_size("tm")
    forward = [(i, i + 1) for i in range(count - 1)]
    backward = [(i + 1, i) for i in range(count - 1)]
    low = lax.ppermute(filtered[:, block_len - RIM :], "tm", forward)
    high = lax.ppermute(filtered[:, :RIM], "tm", backward)
    extended = jnp.concatenate([low, filtered, high], axis=1)

    weights = grouped_weights(tap_table, delay_whole, tap_index)
    span = block_len + SHIFTS * (GROUPS - 1)
    shifted = jnp.stack([extended[:, r + 1 : r + 1 + span] for r in range(SHIFTS)])
    beams = []
    for a in range(local_ch // STRIDE):
        chosen = shifted[:, a * STRIDE : a * STRIDE + SUBARRAY].reshape(SHIFTS * SUBARRAY, span)
        sums = dot_f32(weights, chosen).reshape(GROUPS, slow_count, span)
        total = sums[0, :, :block_len]
        for g in range(1, GROUPS):
            total = total + sums[g, :, SHIFTS * g : SHIFTS * g + block_len]
        beams.append(total)
    return jnp.stack(beams).astype(jnp.bfloat16)


TILE = 128
EXTRA = 128
MESH = pl.DeviceIdType.MESH


def flipped_bits(number, mask, count):
    result, bit = 0, 1
    while bit < count:
        digit = number // bit % 2
        result = result + (1 - digit if mask // bit % 2 else digit) * bit
        bit *= 2
    return result


def triple(table):
    high, low = split_table(table.astype(np.float64))
    return np.concatenate([high, high, low], axis=0)


def split_dot(left_op, right_ref):
    high = left_op.astype(jnp.bfloat16)
    low = (left_op - high.astype(jnp.float32)).astype(jnp.bfloat16)
    return dot_f32(jnp.concatenate([high, low, high], axis=1), right_ref[...])


def fused(
    devices,
    blocks,
    tap_ref,
    rec_hbm,
    mask_hbm,
    delay_hbm,
    index_hbm,
    mix_hbm,
    unmix_hbm,
    cos_hbm,
    sin_hbm,
    high_hbm,
    low_hbm,
    out_ref,
    rec_ref,
    mask_ref,
    delay_ref,
    index_ref,
    mix_ref,
    unmix_ref,
    cos_ref,
    sin_ref,
    high,
    low,
    rec_pair,
    sent,
    got,
    wave,
    band,
    back_sent,
    back_got,
    rows_t,
    ext,
    weights,
    shifted,
    sums,
    load_sem,
    table_sem,
    send_sem,
    recv_sem,
    halo_send,
    halo_recv,
):
    me = lax.axis_index("chan")
    blk = lax.axis_index("tm")
    block_len, local_ch = rec_ref.shape
    band_rows, channels = mask_ref.shape
    slow_count = delay_ref.shape[0]
    reach = SUBARRAY - STRIDE
    slab = 2 * band_rows
    has_low = jnp.where(blk > 0, 1, 0)
    has_high = jnp.where(blk < blocks - 1, 1, 0)
    order = list(range(devices - 1, 0, -1)) + [0]
    peer = {k: flipped_bits(me, k, devices) for k in order}

    loads = [
        pltpu.make_async_copy(source, target, load_sem.at[place])
        for place, (source, target) in enumerate(
            (
                (rec_hbm, rec_ref),
                (mask_hbm, mask_ref),
                (delay_hbm, delay_ref),
                (index_hbm, index_ref),
                (mix_hbm, mix_ref),
                (unmix_hbm, unmix_ref),
                (cos_hbm, cos_ref),
                (sin_hbm, sin_ref),
            )
        )
    ]
    loads[0].start()
    table_copies = {}
    for k in order:
        rows = pl.ds(pl.multiple_of(peer[k] * slab, slab), slab)
        table_copies[k] = (
            pltpu.make_async_copy(high_hbm.at[rows], high.at[rows], table_sem.at[0, k]),
            pltpu.make_async_copy(low_hbm.at[rows], low.at[rows], table_sem.at[1, k]),
        )
        for copy in table_copies[k]:
            copy.start()

    for load in loads[1:]:
        load.start()

    barrier = pltpu.get_barrier_semaphore()
    for k in order[:-1]:
        pl.semaphore_signal(barrier, inc=1, device_id=(blk, peer[k]), device_id_type=MESH)

    @pl.when(blk > 0)
    def _():
        pl.semaphore_signal(barrier, inc=1, device_id=(blk - 1, me), device_id_type=MESH)

    @pl.when(blk < blocks - 1)
    def _():
        pl.semaphore_signal(barrier, inc=1, device_id=(blk + 1, me), device_id_type=MESH)

    loads[0].wait()
    record = rec_ref[...]
    rec_high = record.astype(jnp.bfloat16)
    rec_pair[:, :local_ch] = rec_high
    rec_pair[:, local_ch:] = (record - rec_high.astype(jnp.float32)).astype(jnp.bfloat16)
    pl.semaphore_wait(barrier, devices - 1 + has_low + has_high)

    copies = {}
    for k in order:
        for copy in table_copies[k]:
            copy.wait()
        rows = pl.ds(pl.multiple_of(peer[k] * slab, slab), slab)
        first = dot_f32(high[rows, :], rec_pair[...])
        part = first[:, :local_ch] + first[:, local_ch:]
        part = part + dot_f32(low[rows, :], rec_pair[:, :local_ch])
        if k == 0:
            got[me] = part.astype(jnp.bfloat16)
        else:
            sent[k] = part.astype(jnp.bfloat16)
            copies[k] = pltpu.make_async_remote_copy(
                src_ref=sent.at[k],
                dst_ref=got.at[me],
                send_sem=send_sem.at[0, k],
                recv_sem=recv_sem.at[0, k],
                device_id=(blk, peer[k]),
                device_id_type=MESH,
            )
            copies[k].start()

    for load in loads[1:]:
        load.wait()
    mask = mask_ref[...].astype(jnp.float32).astype(jnp.bfloat16)
    wave_id = lax.broadcasted_iota(jnp.int32, (channels, local_ch), 0)
    lane_id = lax.broadcasted_iota(jnp.int32, (channels, local_ch), 1)
    bands = []
    for k1 in range(devices):
        pick = jnp.where(wave_id == lane_id * devices + k1, 1.0, 0.0).astype(jnp.bfloat16)
        bands.append(dot_f32(mask, pick))
    from_id = lax.broadcasted_iota(jnp.int32, (local_ch, local_ch), 0)
    to_id = lax.broadcasted_iota(jnp.int32, (local_ch, local_ch), 1)
    freq = lax.broadcasted_iota(jnp.int32, (band_rows, local_ch), 0) + me * band_rows
    scale = jnp.where(freq == 0, 1.0, 2.0) / (block_len * channels)
    for k1 in range(devices):
        total = from_id + to_id
        if k1 == 0:
            turn = jnp.where((total == local_ch) | (total == 0), 1.0, 0.0)
        else:
            turn = jnp.where(total == local_ch - 1, 1.0, 0.0)
        mirror = dot_f32(bands[(devices - k1) % devices].astype(jnp.bfloat16), turn.astype(jnp.bfloat16))
        own = jnp.where(freq == 0, bands[k1] * mirror, bands[k1]) * scale
        band[k1 * band_rows : (k1 + 1) * band_rows] = own

    table = tap_ref[...].astype(jnp.float32)
    for half in range(0, slow_count, 32):
        some = slice(half, half + 32)
        start = delay_ref[some] + LAG
        index = index_ref[some]
        coeffs = []
        for tap_pos in range(TAPS):
            value = jnp.zeros(index.shape, jnp.float32)
            for frac in range(FRACS):
                value = jnp.where(index == frac, table[frac : frac + 1, tap_pos : tap_pos + 1], value)
            coeffs.append(value)
        for lag in range(LAGS):
            value = jnp.zeros(index.shape, jnp.float32)
            for tap_pos in range(TAPS):
                value = jnp.where(start == lag - tap_pos, coeffs[tap_pos], value)
            g, r = divmod(lag, SHIFTS)
            weights[
                g * slow_count + half : g * slow_count + half + 32, r * SUBARRAY : (r + 1) * SUBARRAY
            ] = value.astype(jnp.bfloat16)

    for k in order[:-1]:
        copies[k].wait_recv()

    step = 16
    for low_row in range(0, band_rows, step):
        re = [got[d, low_row : low_row + step].astype(jnp.float32) for d in range(devices)]
        im = [
            got[d, band_rows + low_row : band_rows + low_row + step].astype(jnp.float32)
            for d in range(devices)
        ]
        re, im = small_dft(re, im, -1.0)
        for d in range(devices):
            c, s = cos_ref[d : d + 1], sin_ref[d : d + 1]
            rows = slice(d * band_rows + low_row, d * band_rows + low_row + step)
            wave[rows, :local_ch] = re[d] * c + im[d] * s
            wave[rows, local_ch:] = im[d] * c - re[d] * s
    spread = split_dot(wave[...], mix_ref)
    kept = spread * jnp.concatenate([band[...], band[...]], axis=1)
    wave[...] = split_dot(kept, unmix_ref)
    for low_row in range(0, band_rows, step):
        re, im = [], []
        for d in range(devices):
            c, s = cos_ref[d : d + 1], sin_ref[d : d + 1]
            rows = slice(d * band_rows + low_row, d * band_rows + low_row + step)
            b_re, b_im = wave[rows, :local_ch], wave[rows, local_ch:]
            re.append(b_re * c - b_im * s)
            im.append(b_im * c + b_re * s)
        re, im = small_dft(re, im, 1.0)
        for d in range(devices):
            if d + 1 < devices:
                rim = jnp.concatenate([re[d + 1][:, :reach], im[d + 1][:, :reach]], axis=1)
            else:
                rim = jnp.zeros((step, 2 * reach), jnp.float32)
            for place, part in enumerate((re[d], im[d], rim)):
                rows = slice(place * band_rows + low_row, place * band_rows + low_row + step)
                back_sent[d, rows] = part.astype(jnp.bfloat16)

    back_copies = {}
    for k in order[:-1]:
        back_copies[k] = pltpu.make_async_remote_copy(
            src_ref=back_sent.at[peer[k]],
            dst_ref=back_got.at[me],
            send_sem=send_sem.at[1, k],
            recv_sem=recv_sem.at[1, k],
            device_id=(blk, peer[k]),
            device_id_type=MESH,
        )
        back_copies[k].start()
    back_got[me] = back_sent[me]
    for k in order[::-1]:
        if k:
            back_copies[k].wait_recv()
        source = peer[k]
        piece = back_got[source].astype(jnp.float32)
        lanes = pl.ds(pl.multiple_of(source * slab, slab), slab)
        rows_t[:local_ch, lanes] = piece[:slab].T.astype(jnp.bfloat16)
        rim = piece[slab:].T
        rim = jnp.concatenate([rim[:reach], rim[reach:]], axis=1)
        rows_t[local_ch:, lanes] = rim.astype(jnp.bfloat16)

    def back_in_time(first, width):
        left_op = rows_t[...]
        field = dot_f32(left_op, high[:, first : first + width])
        field = field + dot_f32(left_op, low[:, first : first + width])
        ext[:, EXTRA + first : EXTRA + first + width] = field.astype(jnp.bfloat16)

    chunk = 2 * TILE
    back_in_time(0, chunk)
    back_in_time(block_len - chunk, chunk)
    last = EXTRA + block_len
    up = pltpu.make_async_remote_copy(
        src_ref=ext.at[:, block_len:last],
        dst_ref=ext.at[:, 0:EXTRA],
        send_sem=halo_send.at[0],
        recv_sem=halo_recv.at[0],
        device_id=(blk + 1, me),
        device_id_type=MESH,
    )
    down = pltpu.make_async_remote_copy(
        src_ref=ext.at[:, EXTRA : 2 * EXTRA],
        dst_ref=ext.at[:, last : last + EXTRA],
        send_sem=halo_send.at[1],
        recv_sem=halo_recv.at[1],
        device_id=(blk - 1, me),
        device_id_type=MESH,
    )

    @pl.when(blk < blocks - 1)
    def _():
        up.start()

    @pl.when(blk > 0)
    def _():
        down.start()

    for first in range(chunk, block_len - chunk, chunk):
        back_in_time(first, chunk)

    @pl.when(blk > 0)
    def _():
        up.wait_recv()

    @pl.when(blk == 0)
    def _():
        ext[:, 0:EXTRA] = jnp.zeros((ext.shape[0], EXTRA), jnp.bfloat16)

    @pl.when(blk < blocks - 1)
    def _():
        down.wait_recv()

    @pl.when(blk == blocks - 1)
    def _():
        ext[:, last : last + EXTRA] = jnp.zeros((ext.shape[0], EXTRA), jnp.bfloat16)

    span = block_len + EXTRA
    for r in range(SHIFTS):
        begin = EXTRA - RIM + 1 + r
        moved = ext[:, begin : begin + span]
        rows = slice(r * SUBARRAY, (r + 1) * SUBARRAY)
        for a in range(local_ch // STRIDE):
            shifted[rows, a * span : (a + 1) * span] = moved[a * STRIDE : a * STRIDE + SUBARRAY]

    @pl.loop(0, shifted.shape[1] // chunk)
    def _(n):
        lanes = pl.ds(pl.multiple_of(n * chunk, chunk), chunk)
        sums[:, lanes] = dot_f32(weights[...], shifted[:, lanes])

    @pl.loop(0, slow_count // step)
    def _(n):
        for a in range(local_ch // STRIDE):
            total = None
            for g in range(GROUPS):
                rows = pl.ds(pl.multiple_of(g * slow_count + n * step, step), step)
                begin = a * span + SHIFTS * g
                part = sums[rows, a * span : (a + 1) * span][:, SHIFTS * g : SHIFTS * g + block_len]
                total = part if total is None else total + part
            out_ref[a, pl.ds(pl.multiple_of(n * step, step), step), :] = total.astype(jnp.bfloat16)

    for k in order[:-1]:
        copies[k].wait_send()
        back_copies[k].wait_send()

    @pl.when(blk < blocks - 1)
    def _():
        up.wait_send()

    @pl.when(blk > 0)
    def _():
        down.wait_send()


def fused_body(devices, blocks, record, fk_mask, tap_table, delay_whole, tap_index):
    block_len, local_ch = record.shape
    band_rows, channels = fk_mask.shape
    slow_count = delay_whole.shape[0]
    table_hi, table_lo = time_table(block_len, devices)
    cos_twist, sin_twist = twist_tables(devices, local_ch)
    mix = local_table(local_ch)
    slab = 2 * band_rows
    reach = SUBARRAY - STRIDE
    span = block_len + EXTRA
    subarrays = local_ch // STRIDE
    bf16 = jnp.bfloat16
    vmem = pl.BlockSpec(memory_space=pltpu.VMEM)
    hbm = pl.BlockSpec(memory_space=pltpu.HBM)
    return pl.pallas_call(
        functools.partial(fused, devices, blocks),
        out_shape=pltpu.VMEM((subarrays, slow_count, block_len), bf16),
        in_specs=[vmem] + [hbm] * 10,
        out_specs=vmem,
        scratch_shapes=[
            pltpu.VMEM((block_len, local_ch), jnp.float32),
            pltpu.VMEM((band_rows, channels), jnp.int32),
            pltpu.VMEM((slow_count, SUBARRAY), jnp.int32),
            pltpu.VMEM((slow_count, SUBARRAY), jnp.int32),
            pltpu.VMEM((6 * local_ch, 2 * local_ch), bf16),
            pltpu.VMEM((6 * local_ch, 2 * local_ch), bf16),
            pltpu.VMEM((devices, local_ch), jnp.float32),
            pltpu.VMEM((devices, local_ch), jnp.float32),
            pltpu.VMEM((block_len, block_len), bf16),
            pltpu.VMEM((block_len, block_len), bf16),
            pltpu.VMEM((block_len, 2 * local_ch), bf16),
            pltpu.VMEM((devices, slab, local_ch), bf16),
            pltpu.VMEM((devices, slab, local_ch), bf16),
            pltpu.VMEM((devices * band_rows, 2 * local_ch), jnp.float32),
            pltpu.VMEM((devices * band_rows, local_ch), jnp.float32),
            pltpu.VMEM((devices, slab + band_rows, local_ch), bf16),
            pltpu.VMEM((devices, slab + band_rows, local_ch), bf16),
            pltpu.VMEM((local_ch + reach, block_len), bf16),
            pltpu.VMEM((local_ch + reach, block_len + 2 * EXTRA), bf16),
            pltpu.VMEM((GROUPS * slow_count, SHIFTS * SUBARRAY), bf16),
            pltpu.VMEM((SHIFTS * SUBARRAY, subarrays * span), bf16),
            pltpu.VMEM((GROUPS * slow_count, subarrays * span), jnp.float32),
            pltpu.SemaphoreType.DMA((8,)),
            pltpu.SemaphoreType.DMA((2, devices)),
            pltpu.SemaphoreType.DMA((2, devices)),
            pltpu.SemaphoreType.DMA((2, devices)),
            pltpu.SemaphoreType.DMA((2,)),
            pltpu.SemaphoreType.DMA((2,)),
        ],
        compiler_params=pltpu.CompilerParams(
            collective_id=0, has_side_effects=True, vmem_limit_bytes=60 * 2**20
        ),
    )(
        tap_table,
        record,
        fk_mask,
        delay_whole,
        tap_index,
        jnp.asarray(triple(mix)),
        jnp.asarray(triple(mix.T)),
        jnp.asarray(cos_twist),
        jnp.asarray(sin_twist),
        jnp.asarray(table_hi),
        jnp.asarray(table_lo),
    )


def solution(mesh):
    placed = (P("tm", "chan"), P("chan", None), P(), P(), P())
    devices, blocks = mesh.shape["chan"], mesh.shape["tm"]

    def placed_body(record, *others):
        block_len, local_ch = record.shape
        if local_ch == TILE and block_len // devices == TILE:
            return fused_body(devices, blocks, record, *others)
        return body(record, *others)

    return jax.shard_map(
        placed_body, mesh=mesh, in_specs=placed, out_specs=P("chan", None, "tm"), check_vma=False
    )
```

```python
import functools
import math

import jax
import jax.numpy as jnp
import ml_dtypes
import numpy as np
from jax import lax
from jax.experimental import pallas as pl
from jax.experimental.pallas import tpu as pltpu
from jax.sharding import PartitionSpec as P

SUBARRAY = 128
STRIDE = 64
TAPS = 8
FRACS = 8
LAG = 16
RIM = 20
LAGS = 40
GROUPS = 5
SHIFTS = LAGS // GROUPS


def split_table(table):
    high = table.astype(ml_dtypes.bfloat16)
    low = (table - high.astype(np.float64)).astype(ml_dtypes.bfloat16)
    return high, low


def time_table(block_len, devices):
    half_len = block_len // 2
    freq = np.arange(half_len)
    phase = (freq[:, None] * np.arange(block_len)[None, :] % block_len) * (2.0 * math.pi / block_len)
    both = np.stack([np.cos(phase), -np.sin(phase)])
    both = both.reshape(2, devices, half_len // devices, block_len).transpose(1, 0, 2, 3)
    return split_table(both.reshape(block_len, block_len))


def local_table(local_ch):
    ids = np.arange(local_ch)
    phase = (ids[:, None] * ids[None, :] % local_ch) * (2.0 * math.pi / local_ch)
    c, s = np.cos(phase), np.sin(phase)
    return np.block([[c, -s], [s, c]]).astype(np.float32)


def twist_tables(devices, local_ch):
    phase = np.arange(devices)[:, None] * np.arange(local_ch)[None, :] * (2.0 * math.pi / (devices * local_ch))
    return np.cos(phase).astype(np.float32), np.sin(phase).astype(np.float32)


def small_dft(re, im, sign):
    count = len(re)
    if count == 1:
        return re, im
    even_re, even_im = small_dft(re[0::2], im[0::2], sign)
    odd_re, odd_im = small_dft(re[1::2], im[1::2], sign)
    out_re, out_im = [None] * count, [None] * count
    half = count // 2
    for k in range(half):
        if k == 0:
            tr, ti = odd_re[k], odd_im[k]
        elif 4 * k == count:
            tr, ti = -sign * odd_im[k], sign * odd_re[k]
        else:
            c = math.cos(2.0 * math.pi * k / count)
            s = sign * math.sin(2.0 * math.pi * k / count)
            tr = odd_re[k] * c - odd_im[k] * s
            ti = odd_im[k] * c + odd_re[k] * s
        out_re[k], out_im[k] = even_re[k] + tr, even_im[k] + ti
        out_re[k + half], out_im[k + half] = even_re[k] - tr, even_im[k] - ti
    return out_re, out_im


def flip_wavenumbers(rows_table):
    return jnp.roll(rows_table[:, ::-1], 1, axis=1)


def grouped_weights(tap_table, delay_whole, tap_index):
    table = tap_table.astype(jnp.float32)
    coeffs = []
    for tap_pos in range(TAPS):
        value = jnp.zeros(tap_index.shape, jnp.float32)
        for frac in range(FRACS):
            value = jnp.where(tap_index == frac, table[frac, tap_pos], value)
        coeffs.append(value)
    lag = (
        SHIFTS * jnp.arange(GROUPS, dtype=jnp.int32)[:, None, None, None]
        + jnp.arange(SHIFTS, dtype=jnp.int32)[None, None, :, None]
    )
    tap = lag - (delay_whole + LAG)[None, :, None, :]
    weights = jnp.zeros(tap.shape, jnp.float32)
    for tap_pos in range(TAPS):
        weights = jnp.where(tap == tap_pos, coeffs[tap_pos][None, :, None, :], weights)
    rows = GROUPS * delay_whole.shape[0]
    return weights.astype(jnp.bfloat16).reshape(rows, SHIFTS * delay_whole.shape[1])


def dot_f32(left_op, right_op, precision=None):
    return jnp.dot(left_op, right_op, precision=precision, preferred_element_type=jnp.float32)


def body(record, fk_mask, tap_table, delay_whole, tap_index):
    block_len, local_ch = record.shape
    devices = lax.axis_size("chan")
    band_rows, channels = fk_mask.shape
    slow_count = delay_whole.shape[0]
    table_hi, table_lo = time_table(block_len, devices)
    table_hi, table_lo = jnp.asarray(table_hi), jnp.asarray(table_lo)

    rec_hi = record.astype(jnp.bfloat16)
    rec_lo = (record - rec_hi.astype(jnp.float32)).astype(jnp.bfloat16)
    first = dot_f32(table_hi, jnp.concatenate([rec_hi, rec_lo], axis=1))
    spectrum = first[:, :local_ch] + first[:, local_ch:] + dot_f32(table_lo, rec_hi)
    sent = spectrum.astype(jnp.bfloat16).reshape(devices, 2 * band_rows, local_ch)
    got = lax.all_to_all(sent, "chan", split_axis=0, concat_axis=0, tiled=True)

    own_band = fk_mask.astype(jnp.float32)
    freq = lax.axis_index("chan") * band_rows + jnp.arange(band_rows, dtype=jnp.int32)
    at_zero = (freq == 0)[:, None]
    band = jnp.where(at_zero, own_band * flip_wavenumbers(own_band), own_band)
    scale = jnp.where(at_zero, 1.0, 2.0) / (block_len * channels)
    band = (band * scale).reshape(band_rows, local_ch, devices).transpose(2, 0, 1)
    band = band.reshape(devices * band_rows, local_ch)

    cos_twist, sin_twist = twist_tables(devices, local_ch)
    mix = local_table(local_ch)
    parts = got.astype(jnp.float32)
    re, im = small_dft(
        [parts[d, :band_rows] for d in range(devices)],
        [parts[d, band_rows:] for d in range(devices)],
        -1.0,
    )
    turned = []
    for d in range(devices):
        c, s = cos_twist[d][None], sin_twist[d][None]
        turned.append(jnp.concatenate([re[d] * c + im[d] * s, im[d] * c - re[d] * s], axis=1))
    wave = dot_f32(jnp.concatenate(turned, axis=0), mix, lax.Precision.HIGH)
    kept = wave * jnp.concatenate([band, band], axis=1)
    back = dot_f32(kept, mix.T, lax.Precision.HIGH).reshape(devices, band_rows, 2 * local_ch)
    re, im = [], []
    for d in range(devices):
        c, s = cos_twist[d][None], sin_twist[d][None]
        b_re, b_im = back[d, :, :local_ch], back[d, :, local_ch:]
        re.append(b_re * c - b_im * s)
        im.append(b_im * c + b_re * s)
    re, im = small_dft(re, im, 1.0)
    reach = SUBARRAY - STRIDE
    slabs = []
    for d in range(devices):
        if d + 1 < devices:
            rim = jnp.concatenate([re[d + 1][:, :reach], im[d + 1][:, :reach]], axis=1)
        else:
            rim = jnp.zeros((band_rows, 2 * reach), jnp.float32)
        slabs.append(jnp.concatenate([re[d], im[d], rim], axis=0).astype(jnp.bfloat16))
    back_got = lax.all_to_all(jnp.stack(slabs), "chan", split_axis=0, concat_axis=0, tiled=True)
    own = back_got[:, : 2 * band_rows].reshape(block_len, local_ch)
    rim = back_got[:, 2 * band_rows :].reshape(devices, band_rows, 2, reach)
    rim = rim.transpose(0, 2, 1, 3).reshape(block_len, reach)
    rows = jnp.concatenate([own, rim], axis=1)
    contract = (((0,), (0,)), ((), ()))
    field = lax.dot_general(rows, table_hi, contract, preferred_element_type=jnp.float32)
    field = field + lax.dot_general(rows, table_lo, contract, preferred_element_type=jnp.float32)
    filtered = field.astype(jnp.bfloat16)

    count = lax.axis_size("tm")
    forward = [(i, i + 1) for i in range(count - 1)]
    backward = [(i + 1, i) for i in range(count - 1)]
    low = lax.ppermute(filtered[:, block_len - RIM :], "tm", forward)
    high = lax.ppermute(filtered[:, :RIM], "tm", backward)
    extended = jnp.concatenate([low, filtered, high], axis=1)

    weights = grouped_weights(tap_table, delay_whole, tap_index)
    span = block_len + SHIFTS * (GROUPS - 1)
    shifted = jnp.stack([extended[:, r + 1 : r + 1 + span] for r in range(SHIFTS)])
    beams = []
    for a in range(local_ch // STRIDE):
        chosen = shifted[:, a * STRIDE : a * STRIDE + SUBARRAY].reshape(SHIFTS * SUBARRAY, span)
        sums = dot_f32(weights, chosen).reshape(GROUPS, slow_count, span)
        total = sums[0, :, :block_len]
        for g in range(1, GROUPS):
            total = total + sums[g, :, SHIFTS * g : SHIFTS * g + block_len]
        beams.append(total)
    return jnp.stack(beams).astype(jnp.bfloat16)


TILE = 128
EDGE = 32
PHASE = 8
TURNS = 2 * TILE
MESH = pl.DeviceIdType.MESH


def flipped_bits(number, mask, count):
    result, bit = 0, 1
    while bit < count:
        digit = number // bit % 2
        result = result + (1 - digit if mask // bit % 2 else digit) * bit
        bit *= 2
    return result


def triple(table):
    high, low = split_table(table.astype(np.float64))
    return np.concatenate([high, high, low], axis=0)


def parity_tables(block_len, devices):
    half_len = block_len // 2
    count = half_len // devices // 2
    tables = []
    for parity in range(2):
        freq = np.arange(devices)[:, None] * 2 * count + 2 * np.arange(count)[None, :] + parity
        phase = (freq[:, :, None] * np.arange(half_len) % block_len) * (2.0 * math.pi / block_len)
        tables.append(np.stack([np.cos(phase), -np.sin(phase)], axis=1).reshape(half_len, half_len))
    tables = np.stack(tables)
    ahead = np.concatenate(split_table(tables), axis=2)
    back = np.concatenate(split_table(tables.transpose(0, 2, 1)), axis=2)
    return ahead, back


def split_dot(left_op, right_ref):
    high = left_op.astype(jnp.bfloat16)
    low = (left_op - high.astype(jnp.float32)).astype(jnp.bfloat16)
    return dot_f32(jnp.concatenate([high, low, high], axis=1), right_ref[...])


def fused(
    devices,
    blocks,
    tap_ref,
    rec_hbm,
    mask_hbm,
    delay_hbm,
    index_hbm,
    mix_hbm,
    unmix_hbm,
    cos_hbm,
    sin_hbm,
    ahead_hbm,
    behind_hbm,
    out_ref,
    rec_ref,
    mask_ref,
    delay_ref,
    index_ref,
    mix_ref,
    unmix_ref,
    cos_ref,
    sin_ref,
    ahead,
    behind,
    folded,
    sent,
    got,
    wave,
    band,
    back_sent,
    back_got,
    ext,
    edge_sent,
    edge_got,
    rim_sent,
    rim_got,
    weights,
    shifted,
    load_sem,
    table_sem,
    send_sem,
    recv_sem,
    edge_send,
    edge_recv,
    rim_sem,
):
    me = lax.axis_index("chan")
    blk = lax.axis_index("tm")
    block_len, local_ch = rec_ref.shape
    half_len = block_len // 2
    band_rows, channels = mask_ref.shape
    half_rows = band_rows // 2
    slow_count = delay_ref.shape[0]
    f32, bf16 = jnp.float32, jnp.bfloat16
    is_first, is_last = me == 0, me == devices - 1
    low_blk, high_blk = blk > 0, blk < blocks - 1
    order = list(range(devices - 1, 0, -1))
    peer = {k: flipped_bits(me, k, devices) for k in order}

    def count_of(flag):
        return jnp.where(flag, 1, 0)

    loads = [
        pltpu.make_async_copy(source, target, load_sem.at[place])
        for place, (source, target) in enumerate(
            (
                (rec_hbm, rec_ref),
                (mask_hbm, mask_ref),
                (delay_hbm, delay_ref),
                (index_hbm, index_ref),
                (cos_hbm, cos_ref),
                (sin_hbm, sin_ref),
                (mix_hbm, mix_ref),
                (unmix_hbm, unmix_ref),
            )
        )
    ]
    tables = [
        pltpu.make_async_copy(ahead_hbm.at[0], ahead.at[0], table_sem.at[0]),
        pltpu.make_async_copy(ahead_hbm.at[1], ahead.at[1], table_sem.at[1]),
        pltpu.make_async_copy(behind_hbm, behind, table_sem.at[2]),
    ]
    loads[0].start()
    tables[0].start()

    barrier = pltpu.get_barrier_semaphore()

    def greet(block, shard):
        pl.semaphore_signal(barrier, inc=1, device_id=(block, shard), device_id_type=MESH)

    for k in order:
        greet(blk, peer[k])
    for there, block in ((low_blk, blk - 1), (high_blk, blk + 1)):

        @pl.when(there)
        def _():
            greet(block, me)

        @pl.when(there & (me < devices - 1))
        def _():
            greet(block, me + 1)

    tables[1].start()
    for load in loads[1:]:
        load.start()
    tables[2].start()

    def fold(parity):
        first, second = rec_ref[:half_len], rec_ref[half_len:]
        value = first - second if parity else first + second
        high = value.astype(bf16)
        folded[:half_len, :local_ch] = high
        folded[:half_len, local_ch:] = (value - high.astype(f32)).astype(bf16)
        folded[half_len:, :local_ch] = high
        folded[half_len:, local_ch:] = jnp.zeros_like(high)

    copies = {}
    loads[0].wait()
    for parity in range(2):
        fold(parity)
        tables[parity].wait()
        both = dot_f32(ahead[parity], folded[...])
        part = (both[:, :local_ch] + both[:, local_ch:]).astype(bf16)
        sent[parity] = part.reshape(devices, band_rows, local_ch)
        if parity == 0:
            neighbours = count_of(low_blk) + count_of(high_blk)
            pl.semaphore_wait(barrier, devices - 1 + neighbours * (1 + count_of(me > 0)))
        for k in order:
            copies[parity, k] = pltpu.make_async_remote_copy(
                src_ref=sent.at[parity, peer[k]],
                dst_ref=got.at[parity, me],
                send_sem=send_sem.at[0, parity, k],
                recv_sem=recv_sem.at[0, parity, k],
                device_id=(blk, peer[k]),
                device_id_type=MESH,
            )
            copies[parity, k].start()
        got[parity, me] = sent[parity, me]

    for load in loads[1:]:
        load.wait()
    put_id = lax.broadcasted_iota(jnp.int32, (band_rows, band_rows), 0)
    take_id = lax.broadcasted_iota(jnp.int32, (band_rows, band_rows), 1)
    taken = jnp.where(put_id < half_rows, 2 * put_id, 2 * (put_id - half_rows) + 1)
    sort = jnp.where(take_id == taken, 1.0, 0.0).astype(bf16)
    mask = dot_f32(sort, mask_ref[...].astype(f32).astype(bf16)).astype(bf16)
    wave_id = lax.broadcasted_iota(jnp.int32, (channels, local_ch), 0)
    lane_id = lax.broadcasted_iota(jnp.int32, (channels, local_ch), 1)
    bands = []
    for k1 in range(devices):
        pick = jnp.where(wave_id == lane_id * devices + k1, 1.0, 0.0).astype(bf16)
        bands.append(dot_f32(mask, pick))
    from_id = lax.broadcasted_iota(jnp.int32, (local_ch, local_ch), 0)
    to_id = lax.broadcasted_iota(jnp.int32, (local_ch, local_ch), 1)
    row_id = lax.broadcasted_iota(jnp.int32, (band_rows, local_ch), 0)
    at_zero = (row_id == 0) & is_first
    scale = jnp.where(at_zero, 1.0, 2.0) / (block_len * channels)
    for k1 in range(devices):
        total = from_id + to_id
        if k1 == 0:
            turn = jnp.where((total == local_ch) | (total == 0), 1.0, 0.0)
        else:
            turn = jnp.where(total == local_ch - 1, 1.0, 0.0)
        mirror = dot_f32(bands[(devices - k1) % devices].astype(bf16), turn.astype(bf16))
        own = jnp.where(at_zero, bands[k1] * mirror, bands[k1]) * scale
        for parity in range(2):
            band[parity, k1 * half_rows : (k1 + 1) * half_rows] = own[parity * half_rows : (parity + 1) * half_rows]

    step = 16

    def over_channels(parity):
        for low_row in range(0, half_rows, step):
            re = [got[parity, d, low_row : low_row + step].astype(f32) for d in range(devices)]
            im = [
                got[parity, d, half_rows + low_row : half_rows + low_row + step].astype(f32)
                for d in range(devices)
            ]
            re, im = small_dft(re, im, -1.0)
            for d in range(devices):
                c, s = cos_ref[d : d + 1], sin_ref[d : d + 1]
                rows = slice(d * half_rows + low_row, d * half_rows + low_row + step)
                wave[rows, :local_ch] = re[d] * c + im[d] * s
                wave[rows, local_ch:] = im[d] * c - re[d] * s
        spread = split_dot(wave[...], mix_ref)
        kept = spread * jnp.concatenate([band[parity], band[parity]], axis=1)
        wave[...] = split_dot(kept, unmix_ref)
        for low_row in range(0, half_rows, step):
            re, im = [], []
            for d in range(devices):
                c, s = cos_ref[d : d + 1], sin_ref[d : d + 1]
                rows = slice(d * half_rows + low_row, d * half_rows + low_row + step)
                b_re, b_im = wave[rows, :local_ch], wave[rows, local_ch:]
                re.append(b_re * c - b_im * s)
                im.append(b_im * c + b_re * s)
            re, im = small_dft(re, im, 1.0)
            for d in range(devices):
                back_sent[parity, d, low_row : low_row + step] = re[d].astype(bf16)
                back_sent[parity, d, half_rows + low_row : half_rows + low_row + step] = im[d].astype(bf16)

    back_copies = {}
    for parity in range(2):
        for k in order:
            copies[parity, k].wait_recv()
        over_channels(parity)
        for k in order:
            back_copies[parity, k] = pltpu.make_async_remote_copy(
                src_ref=back_sent.at[parity, peer[k]],
                dst_ref=back_got.at[parity, me],
                send_sem=send_sem.at[1, parity, k],
                recv_sem=recv_sem.at[1, parity, k],
                device_id=(blk, peer[k]),
                device_id_type=MESH,
            )
            back_copies[parity, k].start()
        back_got[parity, me] = back_sent[parity, me]

    tables[2].wait()

    def drain_exchanges():
        for parity in range(2):
            for k in order:
                copies[parity, k].wait_send()
                back_copies[parity, k].wait_send()

    table = tap_ref[...].astype(f32)
    starts = delay_ref[...].astype(f32).T.astype(jnp.int32) + LAG
    index_t = index_ref[...].astype(f32).T.astype(jnp.int32)
    blank = jnp.zeros((PHASE * SUBARRAY, slow_count), bf16)
    weights[LAGS * SUBARRAY :, :slow_count] = blank
    weights[: PHASE * SUBARRAY, slow_count:] = blank
    for first in range(0, SUBARRAY, 32):
        start = starts[first : first + 32]
        index = index_t[first : first + 32]
        coeffs = []
        for tap_pos in range(TAPS):
            value = jnp.zeros(index.shape, f32)
            for frac in range(FRACS):
                value = jnp.where(index == frac, table[frac : frac + 1, tap_pos : tap_pos + 1], value)
            coeffs.append(value)
        for lag in range(LAGS):
            value = jnp.zeros(index.shape, f32)
            for tap_pos in range(TAPS):
                if 0 <= lag - tap_pos <= 2 * LAG:
                    value = jnp.where(start == lag - tap_pos, coeffs[tap_pos], value)
            value = value.astype(bf16)
            for phase in range(2):
                top = (lag + PHASE * phase) * SUBARRAY + first
                weights[top : top + 32, phase * slow_count : (phase + 1) * slow_count] = value
    pieces = []
    for parity in range(2):
        for k in order:
            back_copies[parity, k].wait_recv()
        rows = back_got[parity].reshape(half_len, local_ch)
        pieces.append(dot_f32(behind[parity], jnp.concatenate([rows, rows], axis=0)))
    early, late = pieces[0] + pieces[1], pieces[0] - pieces[1]
    edge_sent[0] = early[:EDGE].astype(bf16)
    edge_sent[1] = late[half_len - EDGE :].astype(bf16)

    def edge_copy(side, beside):
        return pltpu.make_async_remote_copy(
            src_ref=edge_sent.at[side],
            dst_ref=edge_got.at[beside, side],
            send_sem=edge_send.at[beside, side],
            recv_sem=edge_recv.at[beside, side],
            device_id=(blk - 1 + 2 * side, me - beside),
            device_id_type=MESH,
        )

    edges = {(side, beside): edge_copy(side, beside) for side in range(2) for beside in range(2)}
    leaves = (low_blk, high_blk)
    for side in range(2):
        for beside in range(2):

            @pl.when(leaves[side] & (me > 0) if beside else leaves[side])
            def _():
                edges[side, beside].start()

    swapped_early = pltpu.roll(early, STRIDE, 1)
    swapped_late = pltpu.roll(late, STRIDE, 1)
    left = lax.broadcasted_iota(jnp.int32, (half_len, local_ch), 1) < STRIDE
    rim_sent[...] = jnp.where(left, early, swapped_late).astype(bf16)
    rim_copy = pltpu.make_async_remote_copy(
        src_ref=rim_sent,
        dst_ref=rim_got,
        send_sem=rim_sem.at[0],
        recv_sem=rim_sem.at[1],
        device_id=(blk, me - 1),
        device_id_type=MESH,
    )

    @pl.when(me > 0)
    def _():
        rim_copy.start()

    middle, end = EDGE + half_len, EDGE + block_len
    ext[0, EDGE:middle] = early
    ext[0, middle:end] = late
    ext[1, EDGE:middle] = swapped_early
    ext[1, middle:end] = swapped_late

    tops = (end, 0)

    def take_edge(side, beside):
        here = leaves[1 - side]

        @pl.when(here & (me < devices - 1) if beside else here)
        def _():
            edges[side, beside].wait_recv()

        @pl.when(jnp.logical_not(here & (me < devices - 1) if beside else here))
        def _():
            edge_got[beside, side] = jnp.zeros(edge_got.shape[2:], bf16)

    span = shifted.shape[2]
    tiles = span // (2 * PHASE)

    def shift_rows(a):
        for r in range(PHASE):
            begin = EDGE - RIM + 1 + r
            halves = [
                ext[a, begin + place : begin + place + span].reshape(tiles, 2, PHASE, local_ch)
                for place in (0, half_len)
            ]
            for odd in range(2):
                pair = jnp.stack([halves[0][:, odd], halves[1][:, odd]], axis=1)
                shifted[a, odd, :, r * local_ch : (r + 1) * local_ch] = pair.reshape(span, local_ch).astype(bf16)

    depth = PHASE * SUBARRAY

    def beam(a):
        for first in range(0, half_len, TURNS):
            total = None
            for g in range(weights.shape[0] // depth):
                top = first + 2 * PHASE * (g // 2)
                part = dot_f32(shifted[a, g % 2, top : top + TURNS], weights[g * depth : (g + 1) * depth])
                total = part if total is None else total + part
            count = TURNS // (2 * PHASE)
            parts = total.reshape(count, 2, PHASE, 2 * slow_count)
            for half in range(2):
                pair = jnp.stack([parts[:, half, :, :slow_count], parts[:, half, :, slow_count:]], axis=1)
                lanes = half * half_len + first
                out_ref[a, :, lanes : lanes + TURNS] = pair.reshape(TURNS, slow_count).T.astype(bf16)

    for side in range(2):
        take_edge(side, 0)
        ext[0, tops[side] : tops[side] + EDGE] = edge_got[0, side].astype(f32)
    shift_rows(0)
    beam(0)

    for side in range(2):
        take_edge(side, 1)
        own = pltpu.roll(edge_got[0, side].astype(f32), STRIDE, 1)
        other = pltpu.roll(edge_got[1, side].astype(f32), STRIDE, 1)
        ext[1, tops[side] : tops[side] + EDGE] = jnp.where(left[:EDGE], own, other)

    @pl.when(me < devices - 1)
    def _():
        rim_copy.wait_recv()

    @pl.when(is_last)
    def _():
        rim_got[...] = jnp.zeros(rim_got.shape, bf16)

    rim = rim_got[...].astype(f32)
    ext[1, EDGE:middle] = jnp.where(left, ext[1, EDGE:middle], pltpu.roll(rim, STRIDE, 1))
    ext[1, middle:end] = jnp.where(left, ext[1, middle:end], rim)
    shift_rows(1)
    beam(1)

    drain_exchanges()
    for side in range(2):
        for beside in range(2):

            @pl.when(leaves[side] & (me > 0) if beside else leaves[side])
            def _():
                edges[side, beside].wait_send()

    @pl.when(me > 0)
    def _():
        rim_copy.wait_send()


def fused_body(devices, blocks, record, fk_mask, tap_table, delay_whole, tap_index):
    block_len, local_ch = record.shape
    band_rows, channels = fk_mask.shape
    slow_count = delay_whole.shape[0]
    half_len, half_rows = block_len // 2, band_rows // 2
    ahead, behind = parity_tables(block_len, devices)
    cos_twist, sin_twist = twist_tables(devices, local_ch)
    mix = local_table(local_ch)
    subarrays = local_ch // STRIDE
    span = half_len + EDGE
    bf16 = jnp.bfloat16
    vmem = pl.BlockSpec(memory_space=pltpu.VMEM)
    hbm = pl.BlockSpec(memory_space=pltpu.HBM)
    return pl.pallas_call(
        functools.partial(fused, devices, blocks),
        out_shape=pltpu.VMEM((subarrays, slow_count, block_len), bf16),
        in_specs=[vmem] + [hbm] * 10,
        out_specs=vmem,
        scratch_shapes=[
            pltpu.VMEM((block_len, local_ch), jnp.float32),
            pltpu.VMEM((band_rows, channels), jnp.int32),
            pltpu.VMEM((slow_count, SUBARRAY), jnp.int32),
            pltpu.VMEM((slow_count, SUBARRAY), jnp.int32),
            pltpu.VMEM((6 * local_ch, 2 * local_ch), bf16),
            pltpu.VMEM((6 * local_ch, 2 * local_ch), bf16),
            pltpu.VMEM((devices, local_ch), jnp.float32),
            pltpu.VMEM((devices, local_ch), jnp.float32),
            pltpu.VMEM(ahead.shape, bf16),
            pltpu.VMEM(behind.shape, bf16),
            pltpu.VMEM((block_len, 2 * local_ch), bf16),
            pltpu.VMEM((2, devices, band_rows, local_ch), bf16),
            pltpu.VMEM((2, devices, band_rows, local_ch), bf16),
            pltpu.VMEM((devices * half_rows, 2 * local_ch), jnp.float32),
            pltpu.VMEM((2, devices * half_rows, local_ch), jnp.float32),
            pltpu.VMEM((2, devices, band_rows, local_ch), bf16),
            pltpu.VMEM((2, devices, band_rows, local_ch), bf16),
            pltpu.VMEM((subarrays, block_len + 2 * EDGE, local_ch), jnp.float32),
            pltpu.VMEM((2, EDGE, local_ch), bf16),
            pltpu.VMEM((2, 2, EDGE, local_ch), bf16),
            pltpu.VMEM((half_len, local_ch), bf16),
            pltpu.VMEM((half_len, local_ch), bf16),
            pltpu.VMEM(((LAGS + PHASE) * SUBARRAY, 2 * slow_count), bf16),
            pltpu.VMEM((subarrays, 2, span, PHASE * local_ch), bf16),
            pltpu.SemaphoreType.DMA((8,)),
            pltpu.SemaphoreType.DMA((3,)),
            pltpu.SemaphoreType.DMA((2, 2, devices)),
            pltpu.SemaphoreType.DMA((2, 2, devices)),
            pltpu.SemaphoreType.DMA((2, 2)),
            pltpu.SemaphoreType.DMA((2, 2)),
            pltpu.SemaphoreType.DMA((2,)),
        ],
        compiler_params=pltpu.CompilerParams(
            collective_id=0, has_side_effects=True, vmem_limit_bytes=60 * 2**20
        ),
    )(
        tap_table,
        record,
        fk_mask,
        delay_whole,
        tap_index,
        jnp.asarray(triple(mix)),
        jnp.asarray(triple(mix.T)),
        jnp.asarray(cos_twist),
        jnp.asarray(sin_twist),
        jnp.asarray(ahead),
        jnp.asarray(behind),
    )


def solution(mesh):
    placed = (P("tm", "chan"), P("chan", None), P(), P(), P())
    devices, blocks = mesh.shape["chan"], mesh.shape["tm"]

    def placed_body(record, *others):
        block_len, local_ch = record.shape
        if local_ch == TILE and block_len // devices == TILE:
            return fused_body(devices, blocks, record, *others)
        return body(record, *others)

    return jax.shard_map(
        placed_body, mesh=mesh, in_specs=placed, out_specs=P("chan", None, "tm"), check_vma=False
    )
```

```python
import functools
import math

import jax
import jax.numpy as jnp
import ml_dtypes
import numpy as np
from jax import lax
from jax.experimental import pallas as pl
from jax.experimental.pallas import tpu as pltpu
from jax.sharding import PartitionSpec as P

SUBARRAY = 128
STRIDE = 64
TAPS = 8
FRACS = 8
LAG = 16
RIM = 20
LAGS = 40
GROUPS = 5
SHIFTS = LAGS // GROUPS


def split_table(table):
    high = table.astype(ml_dtypes.bfloat16)
    low = (table - high.astype(np.float64)).astype(ml_dtypes.bfloat16)
    return high, low


def time_table(block_len, devices):
    half_len = block_len // 2
    freq = np.arange(half_len)
    phase = (freq[:, None] * np.arange(block_len)[None, :] % block_len) * (2.0 * math.pi / block_len)
    both = np.stack([np.cos(phase), -np.sin(phase)])
    both = both.reshape(2, devices, half_len // devices, block_len).transpose(1, 0, 2, 3)
    return split_table(both.reshape(block_len, block_len))


def local_table(local_ch):
    ids = np.arange(local_ch)
    phase = (ids[:, None] * ids[None, :] % local_ch) * (2.0 * math.pi / local_ch)
    c, s = np.cos(phase), np.sin(phase)
    return np.block([[c, -s], [s, c]]).astype(np.float32)


def twist_tables(devices, local_ch):
    phase = np.arange(devices)[:, None] * np.arange(local_ch)[None, :] * (2.0 * math.pi / (devices * local_ch))
    return np.cos(phase).astype(np.float32), np.sin(phase).astype(np.float32)


def small_dft(re, im, sign):
    count = len(re)
    if count == 1:
        return re, im
    even_re, even_im = small_dft(re[0::2], im[0::2], sign)
    odd_re, odd_im = small_dft(re[1::2], im[1::2], sign)
    out_re, out_im = [None] * count, [None] * count
    half = count // 2
    for k in range(half):
        if k == 0:
            tr, ti = odd_re[k], odd_im[k]
        elif 4 * k == count:
            tr, ti = -sign * odd_im[k], sign * odd_re[k]
        else:
            c = math.cos(2.0 * math.pi * k / count)
            s = sign * math.sin(2.0 * math.pi * k / count)
            tr = odd_re[k] * c - odd_im[k] * s
            ti = odd_im[k] * c + odd_re[k] * s
        out_re[k], out_im[k] = even_re[k] + tr, even_im[k] + ti
        out_re[k + half], out_im[k + half] = even_re[k] - tr, even_im[k] - ti
    return out_re, out_im


def flip_wavenumbers(rows_table):
    return jnp.roll(rows_table[:, ::-1], 1, axis=1)


def grouped_weights(tap_table, delay_whole, tap_index):
    table = tap_table.astype(jnp.float32)
    coeffs = []
    for tap_pos in range(TAPS):
        value = jnp.zeros(tap_index.shape, jnp.float32)
        for frac in range(FRACS):
            value = jnp.where(tap_index == frac, table[frac, tap_pos], value)
        coeffs.append(value)
    lag = (
        SHIFTS * jnp.arange(GROUPS, dtype=jnp.int32)[:, None, None, None]
        + jnp.arange(SHIFTS, dtype=jnp.int32)[None, None, :, None]
    )
    tap = lag - (delay_whole + LAG)[None, :, None, :]
    weights = jnp.zeros(tap.shape, jnp.float32)
    for tap_pos in range(TAPS):
        weights = jnp.where(tap == tap_pos, coeffs[tap_pos][None, :, None, :], weights)
    rows = GROUPS * delay_whole.shape[0]
    return weights.astype(jnp.bfloat16).reshape(rows, SHIFTS * delay_whole.shape[1])


def dot_f32(left_op, right_op, precision=None):
    return jnp.dot(left_op, right_op, precision=precision, preferred_element_type=jnp.float32)


def body(record, fk_mask, tap_table, delay_whole, tap_index):
    block_len, local_ch = record.shape
    devices = lax.axis_size("chan")
    band_rows, channels = fk_mask.shape
    slow_count = delay_whole.shape[0]
    table_hi, table_lo = time_table(block_len, devices)
    table_hi, table_lo = jnp.asarray(table_hi), jnp.asarray(table_lo)

    rec_hi = record.astype(jnp.bfloat16)
    rec_lo = (record - rec_hi.astype(jnp.float32)).astype(jnp.bfloat16)
    first = dot_f32(table_hi, jnp.concatenate([rec_hi, rec_lo], axis=1))
    spectrum = first[:, :local_ch] + first[:, local_ch:] + dot_f32(table_lo, rec_hi)
    sent = spectrum.astype(jnp.bfloat16).reshape(devices, 2 * band_rows, local_ch)
    got = lax.all_to_all(sent, "chan", split_axis=0, concat_axis=0, tiled=True)

    own_band = fk_mask.astype(jnp.float32)
    freq = lax.axis_index("chan") * band_rows + jnp.arange(band_rows, dtype=jnp.int32)
    at_zero = (freq == 0)[:, None]
    band = jnp.where(at_zero, own_band * flip_wavenumbers(own_band), own_band)
    scale = jnp.where(at_zero, 1.0, 2.0) / (block_len * channels)
    band = (band * scale).reshape(band_rows, local_ch, devices).transpose(2, 0, 1)
    band = band.reshape(devices * band_rows, local_ch)

    cos_twist, sin_twist = twist_tables(devices, local_ch)
    mix = local_table(local_ch)
    parts = got.astype(jnp.float32)
    re, im = small_dft(
        [parts[d, :band_rows] for d in range(devices)],
        [parts[d, band_rows:] for d in range(devices)],
        -1.0,
    )
    turned = []
    for d in range(devices):
        c, s = cos_twist[d][None], sin_twist[d][None]
        turned.append(jnp.concatenate([re[d] * c + im[d] * s, im[d] * c - re[d] * s], axis=1))
    wave = dot_f32(jnp.concatenate(turned, axis=0), mix, lax.Precision.HIGH)
    kept = wave * jnp.concatenate([band, band], axis=1)
    back = dot_f32(kept, mix.T, lax.Precision.HIGH).reshape(devices, band_rows, 2 * local_ch)
    re, im = [], []
    for d in range(devices):
        c, s = cos_twist[d][None], sin_twist[d][None]
        b_re, b_im = back[d, :, :local_ch], back[d, :, local_ch:]
        re.append(b_re * c - b_im * s)
        im.append(b_im * c + b_re * s)
    re, im = small_dft(re, im, 1.0)
    reach = SUBARRAY - STRIDE
    slabs = []
    for d in range(devices):
        if d + 1 < devices:
            rim = jnp.concatenate([re[d + 1][:, :reach], im[d + 1][:, :reach]], axis=1)
        else:
            rim = jnp.zeros((band_rows, 2 * reach), jnp.float32)
        slabs.append(jnp.concatenate([re[d], im[d], rim], axis=0).astype(jnp.bfloat16))
    back_got = lax.all_to_all(jnp.stack(slabs), "chan", split_axis=0, concat_axis=0, tiled=True)
    own = back_got[:, : 2 * band_rows].reshape(block_len, local_ch)
    rim = back_got[:, 2 * band_rows :].reshape(devices, band_rows, 2, reach)
    rim = rim.transpose(0, 2, 1, 3).reshape(block_len, reach)
    rows = jnp.concatenate([own, rim], axis=1)
    contract = (((0,), (0,)), ((), ()))
    field = lax.dot_general(rows, table_hi, contract, preferred_element_type=jnp.float32)
    field = field + lax.dot_general(rows, table_lo, contract, preferred_element_type=jnp.float32)
    filtered = field.astype(jnp.bfloat16)

    count = lax.axis_size("tm")
    forward = [(i, i + 1) for i in range(count - 1)]
    backward = [(i + 1, i) for i in range(count - 1)]
    low = lax.ppermute(filtered[:, block_len - RIM :], "tm", forward)
    high = lax.ppermute(filtered[:, :RIM], "tm", backward)
    extended = jnp.concatenate([low, filtered, high], axis=1)

    weights = grouped_weights(tap_table, delay_whole, tap_index)
    span = block_len + SHIFTS * (GROUPS - 1)
    shifted = jnp.stack([extended[:, r + 1 : r + 1 + span] for r in range(SHIFTS)])
    beams = []
    for a in range(local_ch // STRIDE):
        chosen = shifted[:, a * STRIDE : a * STRIDE + SUBARRAY].reshape(SHIFTS * SUBARRAY, span)
        sums = dot_f32(weights, chosen).reshape(GROUPS, slow_count, span)
        total = sums[0, :, :block_len]
        for g in range(1, GROUPS):
            total = total + sums[g, :, SHIFTS * g : SHIFTS * g + block_len]
        beams.append(total)
    return jnp.stack(beams).astype(jnp.bfloat16)


TILE = 128
EDGE = 32
LEAD = 8
PHASE = 8
MESH = pl.DeviceIdType.MESH


def flipped_bits(number, mask, count):
    result, bit = 0, 1
    while bit < count:
        digit = number // bit % 2
        result = result + (1 - digit if mask // bit % 2 else digit) * bit
        bit *= 2
    return result


def triple(table):
    high, low = split_table(table.astype(np.float64))
    return np.concatenate([high, high, low], axis=0)


def parity_tables(block_len, devices):
    half_len = block_len // 2
    count = half_len // devices // 2
    tables = []
    for parity in range(2):
        freq = np.arange(devices)[:, None] * 2 * count + 2 * np.arange(count)[None, :] + parity
        phase = (freq[:, :, None] * np.arange(half_len) % block_len) * (2.0 * math.pi / block_len)
        tables.append(np.stack([np.cos(phase), -np.sin(phase)], axis=1).reshape(half_len, half_len))
    tables = np.stack(tables)
    ahead = np.concatenate(split_table(tables), axis=2)
    back = np.concatenate(split_table(tables.transpose(0, 2, 1)), axis=2)
    return ahead, back


def split_dot(left_op, right_ref):
    high = left_op.astype(jnp.bfloat16)
    low = (left_op - high.astype(jnp.float32)).astype(jnp.bfloat16)
    return dot_f32(jnp.concatenate([high, low, high], axis=1), right_ref[...])


def fused(
    devices,
    blocks,
    tap_hbm,
    rec_hbm,
    mask_hbm,
    delay_hbm,
    index_hbm,
    mix_hbm,
    unmix_hbm,
    cos_hbm,
    sin_hbm,
    ahead_hbm,
    behind_hbm,
    out_ref,
    tap_ref,
    rec_ref,
    mask_ref,
    delay_ref,
    index_ref,
    mix_ref,
    unmix_ref,
    cos_ref,
    sin_ref,
    ahead,
    behind,
    folded,
    sent,
    got,
    wave,
    band,
    back_sent,
    back_got,
    ext,
    edge_sent,
    edge_got,
    rim_sent,
    rim_got,
    weights,
    shifted,
    partial,
    sums,
    load_sem,
    table_sem,
    send_sem,
    recv_sem,
    edge_send,
    edge_recv,
    rim_sem,
):
    me = lax.axis_index("chan")
    blk = lax.axis_index("tm")
    block_len, local_ch = rec_ref.shape
    half_len = block_len // 2
    band_rows, channels = mask_ref.shape
    half_rows = band_rows // 2
    slow_count = delay_ref.shape[0]
    f32, bf16 = jnp.float32, jnp.bfloat16
    is_first, is_last = me == 0, me == devices - 1
    low_blk, high_blk = blk > 0, blk < blocks - 1
    order = list(range(devices - 1, 0, -1))
    peer = {k: flipped_bits(me, k, devices) for k in order}

    def count_of(flag):
        return jnp.where(flag, 1, 0)

    loads = [
        pltpu.make_async_copy(source, target, load_sem.at[place])
        for place, (source, target) in enumerate(
            (
                (rec_hbm, rec_ref),
                (tap_hbm, tap_ref),
                (mask_hbm, mask_ref),
                (delay_hbm, delay_ref),
                (index_hbm, index_ref),
                (cos_hbm, cos_ref),
                (sin_hbm, sin_ref),
                (mix_hbm, mix_ref),
                (unmix_hbm, unmix_ref),
            )
        )
    ]
    tables = [
        pltpu.make_async_copy(ahead_hbm.at[0], ahead.at[0], table_sem.at[0]),
        pltpu.make_async_copy(ahead_hbm.at[1], ahead.at[1], table_sem.at[1]),
        pltpu.make_async_copy(behind_hbm, behind, table_sem.at[2]),
    ]
    loads[0].start()
    tables[0].start()

    barrier = pltpu.get_barrier_semaphore()

    def greet(block, shard):
        pl.semaphore_signal(barrier, inc=1, device_id=(block, shard), device_id_type=MESH)

    for k in order:
        greet(blk, peer[k])
    for there, block in ((low_blk, blk - 1), (high_blk, blk + 1)):

        @pl.when(there)
        def _():
            greet(block, me)

        @pl.when(there & (me < devices - 1))
        def _():
            greet(block, me + 1)

    tables[1].start()
    for load in loads[1:]:
        load.start()
    tables[2].start()

    def fold(parity):
        first, second = rec_ref[:half_len], rec_ref[half_len:]
        value = first - second if parity else first + second
        high = value.astype(bf16)
        folded[:half_len, :local_ch] = high
        folded[:half_len, local_ch:] = (value - high.astype(f32)).astype(bf16)
        folded[half_len:, :local_ch] = high
        folded[half_len:, local_ch:] = jnp.zeros_like(high)

    copies = {}
    loads[0].wait()
    for parity in range(2):
        fold(parity)
        tables[parity].wait()
        both = dot_f32(ahead[parity], folded[...])
        part = (both[:, :local_ch] + both[:, local_ch:]).astype(bf16)
        sent[parity] = part.reshape(devices, band_rows, local_ch)
        if parity == 0:
            neighbours = count_of(low_blk) + count_of(high_blk)
            pl.semaphore_wait(barrier, devices - 1 + neighbours * (1 + count_of(me > 0)))
        for k in order:
            copies[parity, k] = pltpu.make_async_remote_copy(
                src_ref=sent.at[parity, peer[k]],
                dst_ref=got.at[parity, me],
                send_sem=send_sem.at[0, parity, k],
                recv_sem=recv_sem.at[0, parity, k],
                device_id=(blk, peer[k]),
                device_id_type=MESH,
            )
            copies[parity, k].start()
        got[parity, me] = sent[parity, me]

    for load in loads[1:]:
        load.wait()
    put_id = lax.broadcasted_iota(jnp.int32, (band_rows, band_rows), 0)
    take_id = lax.broadcasted_iota(jnp.int32, (band_rows, band_rows), 1)
    taken = jnp.where(put_id < half_rows, 2 * put_id, 2 * (put_id - half_rows) + 1)
    sort = jnp.where(take_id == taken, 1.0, 0.0).astype(bf16)
    mask = dot_f32(sort, mask_ref[...].astype(f32).astype(bf16)).astype(bf16)
    wave_id = lax.broadcasted_iota(jnp.int32, (channels, local_ch), 0)
    lane_id = lax.broadcasted_iota(jnp.int32, (channels, local_ch), 1)
    bands = []
    for k1 in range(devices):
        pick = jnp.where(wave_id == lane_id * devices + k1, 1.0, 0.0).astype(bf16)
        bands.append(dot_f32(mask, pick))
    from_id = lax.broadcasted_iota(jnp.int32, (local_ch, local_ch), 0)
    to_id = lax.broadcasted_iota(jnp.int32, (local_ch, local_ch), 1)
    row_id = lax.broadcasted_iota(jnp.int32, (band_rows, local_ch), 0)
    at_zero = (row_id == 0) & is_first
    scale = jnp.where(at_zero, 1.0, 2.0) / (block_len * channels)
    for k1 in range(devices):
        total = from_id + to_id
        if k1 == 0:
            turn = jnp.where((total == local_ch) | (total == 0), 1.0, 0.0)
        else:
            turn = jnp.where(total == local_ch - 1, 1.0, 0.0)
        mirror = dot_f32(bands[(devices - k1) % devices].astype(bf16), turn.astype(bf16))
        own = jnp.where(at_zero, bands[k1] * mirror, bands[k1]) * scale
        for parity in range(2):
            band[parity, k1 * half_rows : (k1 + 1) * half_rows] = own[parity * half_rows : (parity + 1) * half_rows]

    step = 16

    def over_channels(parity):
        for low_row in range(0, half_rows, step):
            re = [got[parity, d, low_row : low_row + step].astype(f32) for d in range(devices)]
            im = [
                got[parity, d, half_rows + low_row : half_rows + low_row + step].astype(f32)
                for d in range(devices)
            ]
            re, im = small_dft(re, im, -1.0)
            for d in range(devices):
                c, s = cos_ref[d : d + 1], sin_ref[d : d + 1]
                rows = slice(d * half_rows + low_row, d * half_rows + low_row + step)
                wave[rows, :local_ch] = re[d] * c + im[d] * s
                wave[rows, local_ch:] = im[d] * c - re[d] * s
        spread = split_dot(wave[...], mix_ref)
        kept = spread * jnp.concatenate([band[parity], band[parity]], axis=1)
        wave[...] = split_dot(kept, unmix_ref)
        for low_row in range(0, half_rows, step):
            re, im = [], []
            for d in range(devices):
                c, s = cos_ref[d : d + 1], sin_ref[d : d + 1]
                rows = slice(d * half_rows + low_row, d * half_rows + low_row + step)
                b_re, b_im = wave[rows, :local_ch], wave[rows, local_ch:]
                re.append(b_re * c - b_im * s)
                im.append(b_im * c + b_re * s)
            re, im = small_dft(re, im, 1.0)
            for d in range(devices):
                back_sent[parity, d, low_row : low_row + step] = re[d].astype(bf16)
                back_sent[parity, d, half_rows + low_row : half_rows + low_row + step] = im[d].astype(bf16)

    back_copies = {}
    for parity in range(2):
        for k in order:
            copies[parity, k].wait_recv()
        over_channels(parity)
        for k in order:
            back_copies[parity, k] = pltpu.make_async_remote_copy(
                src_ref=back_sent.at[parity, peer[k]],
                dst_ref=back_got.at[parity, me],
                send_sem=send_sem.at[1, parity, k],
                recv_sem=recv_sem.at[1, parity, k],
                device_id=(blk, peer[k]),
                device_id_type=MESH,
            )
            back_copies[parity, k].start()
        back_got[parity, me] = back_sent[parity, me]

    tables[2].wait()

    def drain_exchanges():
        for parity in range(2):
            for k in order:
                copies[parity, k].wait_send()
                back_copies[parity, k].wait_send()

    table = tap_ref[...].astype(f32)
    starts = delay_ref[...].astype(f32).T.astype(jnp.int32) + LAG
    index_t = index_ref[...].astype(f32).T.astype(jnp.int32)
    blank = jnp.zeros((PHASE * STRIDE, slow_count), bf16)
    for part in range(2):
        weights[part, LAGS * STRIDE :, :slow_count] = blank
        weights[part, : PHASE * STRIDE, slow_count:] = blank
    for first in range(0, SUBARRAY, 32):
        start = starts[first : first + 32]
        index = index_t[first : first + 32]
        coeffs = []
        for tap_pos in range(TAPS):
            value = jnp.zeros(index.shape, f32)
            for frac in range(FRACS):
                value = jnp.where(index == frac, table[frac : frac + 1, tap_pos : tap_pos + 1], value)
            coeffs.append(value)
        for lag in range(LAGS):
            value = jnp.zeros(index.shape, f32)
            for tap_pos in range(TAPS):
                if 0 <= lag - tap_pos <= 2 * LAG:
                    value = jnp.where(start == lag - tap_pos, coeffs[tap_pos], value)
            value = value.astype(bf16)
            for phase in range(2):
                part, place = divmod(first, STRIDE)
                top = (lag + PHASE * phase) * STRIDE + place
                weights[part, top : top + 32, phase * slow_count : (phase + 1) * slow_count] = value
    pieces = []
    for parity in range(2):
        for k in order:
            back_copies[parity, k].wait_recv()
        rows = back_got[parity].reshape(half_len, local_ch)
        pieces.append(dot_f32(behind[parity], jnp.concatenate([rows, rows], axis=0)))
    early, late = pieces[0] + pieces[1], pieces[0] - pieces[1]
    edge_sent[0] = early[:EDGE].astype(bf16)
    edge_sent[1] = late[half_len - EDGE :].astype(bf16)

    def edge_copy(side, beside):
        return pltpu.make_async_remote_copy(
            src_ref=edge_sent.at[side],
            dst_ref=edge_got.at[beside, side],
            send_sem=edge_send.at[beside, side],
            recv_sem=edge_recv.at[beside, side],
            device_id=(blk - 1 + 2 * side, me - beside),
            device_id_type=MESH,
        )

    edges = {(side, beside): edge_copy(side, beside) for side in range(2) for beside in range(2)}
    leaves = (low_blk, high_blk)
    for side in range(2):
        for beside in range(2):

            @pl.when(leaves[side] & (me > 0) if beside else leaves[side])
            def _():
                edges[side, beside].start()

    swapped_early = pltpu.roll(early, STRIDE, 1)
    swapped_late = pltpu.roll(late, STRIDE, 1)
    left = lax.broadcasted_iota(jnp.int32, (half_len, local_ch), 1) < STRIDE
    rim_sent[...] = jnp.where(left, early, swapped_late).astype(bf16)
    rim_copy = pltpu.make_async_remote_copy(
        src_ref=rim_sent,
        dst_ref=rim_got,
        send_sem=rim_sem.at[0],
        recv_sem=rim_sem.at[1],
        device_id=(blk, me - 1),
        device_id_type=MESH,
    )

    @pl.when(me > 0)
    def _():
        rim_copy.start()

    top, middle, end = LEAD + EDGE, LEAD + EDGE + half_len, LEAD + EDGE + block_len
    for group, (plain, other) in enumerate((((early, late), (swapped_early, swapped_late)),) * 2):
        low_part, next_part = (other, plain) if group else (plain, other)
        for place, rows in enumerate(((top, middle), (middle, end))):
            ext[group, rows[0] - 1 : rows[1] - 1] = next_part[place]
        for place, rows in enumerate(((top, middle), (middle, end))):
            ext[group, rows[0] : rows[1], :STRIDE] = low_part[place][:, :STRIDE]

    def take_edge(side, beside):
        here = leaves[1 - side]

        @pl.when(here & (me < devices - 1) if beside else here)
        def _():
            edges[side, beside].wait_recv()

        @pl.when(jnp.logical_not(here & (me < devices - 1) if beside else here))
        def _():
            edge_got[beside, side] = jnp.zeros(edge_got.shape[2:], bf16)

    def put_edge(side, beside):
        begin = (end, LEAD)[side]
        plain = edge_got[beside, side].astype(f32)
        other = pltpu.roll(plain, STRIDE, 1)
        for group in ((2,) if beside else (0, 1)):
            low_part, next_part = (other, plain) if group == 1 else (plain, other)
            before = slice(begin - 1, begin - 1 + EDGE)
            ext[group, before] = jnp.where(left[:EDGE], ext[group, before], next_part)
            ext[group, begin : begin + EDGE, :STRIDE] = low_part[:, :STRIDE]

    pairs = PHASE // 2

    def shift_rows(group, row, count):
        for i in range(pairs):
            halves = []
            for place in (0, half_len):
                begin = top - RIM + 1 + 2 * i + row + place
                value = ext[group, begin : begin + count]
                halves.append(value.reshape(count // (2 * PHASE), 2, PHASE, local_ch))
            for odd in range(2):
                pair = jnp.stack([halves[0][:, odd], halves[1][:, odd]], axis=1).reshape(count, local_ch)
                shifted[group, odd, row : row + count, i * local_ch : (i + 1) * local_ch] = pair.astype(bf16)

    steps = weights.shape[1] // (PHASE * STRIDE)
    core = half_len - 2 * EDGE
    inside = ((EDGE, core),)
    outside = ((0, EDGE), (half_len - EDGE, EDGE))

    def operand(chosen):
        columns = []
        for g in range(steps):
            low_row = 2 * PHASE * (g // 2)
            pieces = [
                shifted[group, g % 2, first + low_row : first + low_row + count]
                for group, spans in chosen
                for first, count in spans
            ]
            columns.append(pieces[0] if len(pieces) == 1 else jnp.concatenate(pieces, axis=0))
        return jnp.concatenate(columns, axis=1)

    def keep_sums(a, total, spans):
        taken = 0
        for first, count in spans:
            parts = total[taken : taken + count].reshape(count // (2 * PHASE), 2, PHASE, 2 * slow_count)
            for half in range(2):
                pair = jnp.stack([parts[:, half, :, :slow_count], parts[:, half, :, slow_count:]], axis=1)
                sums[a, half, first : first + count] = pair.reshape(count, slow_count)
            taken += count

    def put(a, first, count):
        for half in range(2):
            lanes = half * half_len + first
            out_ref[a, :, lanes : lanes + count] = sums[a, half, first : first + count].T.astype(bf16)

    first_rows, half_core = EDGE, core // 2
    shift_rows(0, EDGE, half_core + EDGE)
    shift_rows(1, EDGE, half_core + EDGE)
    chunk = ((EDGE, half_core),)
    total = dot_f32(operand([(0, chunk)]), weights[0]) + dot_f32(operand([(1, chunk)]), weights[1])
    shift_rows(0, half_core + 2 * EDGE, half_core)
    keep_sums(0, total, chunk)
    shift_rows(1, half_core + 2 * EDGE, half_core)
    chunk = ((EDGE + half_core, half_core),)
    total = dot_f32(operand([(0, chunk)]), weights[0]) + dot_f32(operand([(1, chunk)]), weights[1])
    keep_sums(0, total, chunk)
    partial[...] = dot_f32(operand([(1, inside)]), weights[0])
    put(0, TILE, half_len - 2 * TILE)

    for beside in range(2):
        for side in range(2):
            take_edge(side, beside)

    @pl.when(me < devices - 1)
    def _():
        rim_copy.wait_recv()

    @pl.when(is_last)
    def _():
        rim_got[...] = jnp.zeros(rim_got.shape, bf16)

    for side in range(2):
        put_edge(side, 0)
    for group in range(2):
        for row in (0, half_len):
            shift_rows(group, row, EDGE)
    around = dot_f32(operand([(0, outside), (1, outside)]), weights[0])
    rim = rim_got[...].astype(f32)
    swapped_rim = pltpu.roll(rim, STRIDE, 1)
    ext[2, top - 1 : middle - 1] = swapped_rim
    ext[2, middle - 1 : end - 1] = rim
    ext[2, top:middle, :STRIDE] = rim[:, :STRIDE]
    ext[2, middle:end, :STRIDE] = swapped_rim[:, :STRIDE]
    for side in range(2):
        put_edge(side, 1)
    shift_rows(2, 0, half_len + EDGE)
    cut = 2 * EDGE
    firsts, lasts = ((EDGE, core // 2),), ((EDGE + core // 2, core // 2),)
    more = dot_f32(operand([(1, outside), (2, outside), (2, firsts)]), weights[1])
    keep_sums(0, around[:cut] + more[:cut], outside)
    keep_sums(1, around[cut:] + more[cut : 2 * cut], outside)
    keep_sums(1, partial[: core // 2] + more[2 * cut :], firsts)
    more = dot_f32(operand([(2, lasts)]), weights[1])
    for first in (0, half_len - TILE):
        put(0, first, TILE)
    put(1, 0, 2 * TILE)
    keep_sums(1, partial[core // 2 :] + more, lasts)
    put(1, 2 * TILE, half_len - 2 * TILE)

    drain_exchanges()
    for side in range(2):
        for beside in range(2):

            @pl.when(leaves[side] & (me > 0) if beside else leaves[side])
            def _():
                edges[side, beside].wait_send()

    @pl.when(me > 0)
    def _():
        rim_copy.wait_send()


def fused_body(devices, blocks, record, fk_mask, tap_table, delay_whole, tap_index):
    block_len, local_ch = record.shape
    band_rows, channels = fk_mask.shape
    slow_count = delay_whole.shape[0]
    half_len, half_rows = block_len // 2, band_rows // 2
    ahead, behind = parity_tables(block_len, devices)
    cos_twist, sin_twist = twist_tables(devices, local_ch)
    mix = local_table(local_ch)
    subarrays = local_ch // STRIDE
    span = half_len + EDGE
    bf16 = jnp.bfloat16
    vmem = pl.BlockSpec(memory_space=pltpu.VMEM)
    hbm = pl.BlockSpec(memory_space=pltpu.HBM)
    return pl.pallas_call(
        functools.partial(fused, devices, blocks),
        out_shape=pltpu.VMEM((subarrays, slow_count, block_len), bf16),
        in_specs=[hbm] * 11,
        out_specs=vmem,
        scratch_shapes=[
            pltpu.VMEM(tap_table.shape, bf16),
            pltpu.VMEM((block_len, local_ch), jnp.float32),
            pltpu.VMEM((band_rows, channels), jnp.int32),
            pltpu.VMEM((slow_count, SUBARRAY), jnp.int32),
            pltpu.VMEM((slow_count, SUBARRAY), jnp.int32),
            pltpu.VMEM((6 * local_ch, 2 * local_ch), bf16),
            pltpu.VMEM((6 * local_ch, 2 * local_ch), bf16),
            pltpu.VMEM((devices, local_ch), jnp.float32),
            pltpu.VMEM((devices, local_ch), jnp.float32),
            pltpu.VMEM(ahead.shape, bf16),
            pltpu.VMEM(behind.shape, bf16),
            pltpu.VMEM((block_len, 2 * local_ch), bf16),
            pltpu.VMEM((2, devices, band_rows, local_ch), bf16),
            pltpu.VMEM((2, devices, band_rows, local_ch), bf16),
            pltpu.VMEM((devices * half_rows, 2 * local_ch), jnp.float32),
            pltpu.VMEM((2, devices * half_rows, local_ch), jnp.float32),
            pltpu.VMEM((2, devices, band_rows, local_ch), bf16),
            pltpu.VMEM((2, devices, band_rows, local_ch), bf16),
            pltpu.VMEM((3, LEAD + block_len + 2 * EDGE, local_ch), jnp.float32),
            pltpu.VMEM((2, EDGE, local_ch), bf16),
            pltpu.VMEM((2, 2, EDGE, local_ch), bf16),
            pltpu.VMEM((half_len, local_ch), bf16),
            pltpu.VMEM((half_len, local_ch), bf16),
            pltpu.VMEM((2, (LAGS + PHASE) * STRIDE, 2 * slow_count), bf16),
            pltpu.VMEM((3, 2, span, PHASE * STRIDE), bf16),
            pltpu.VMEM((half_len - 2 * EDGE, 2 * slow_count), jnp.float32),
            pltpu.VMEM((subarrays, 2, half_len, slow_count), jnp.float32),
            pltpu.SemaphoreType.DMA((9,)),
            pltpu.SemaphoreType.DMA((3,)),
            pltpu.SemaphoreType.DMA((2, 2, devices)),
            pltpu.SemaphoreType.DMA((2, 2, devices)),
            pltpu.SemaphoreType.DMA((2, 2)),
            pltpu.SemaphoreType.DMA((2, 2)),
            pltpu.SemaphoreType.DMA((2,)),
        ],
        compiler_params=pltpu.CompilerParams(
            collective_id=0, has_side_effects=True, vmem_limit_bytes=60 * 2**20
        ),
    )(
        tap_table,
        record,
        fk_mask,
        delay_whole,
        tap_index,
        jnp.asarray(triple(mix)),
        jnp.asarray(triple(mix.T)),
        jnp.asarray(cos_twist),
        jnp.asarray(sin_twist),
        jnp.asarray(ahead),
        jnp.asarray(behind),
    )


def solution(mesh):
    placed = (P("tm", "chan"), P("chan", None), P(), P(), P())
    devices, blocks = mesh.shape["chan"], mesh.shape["tm"]

    def placed_body(record, *others):
        block_len, local_ch = record.shape
        if local_ch == TILE and block_len // devices == TILE:
            return fused_body(devices, blocks, record, *others)
        return body(record, *others)

    return jax.shard_map(
        placed_body, mesh=mesh, in_specs=placed, out_specs=P("chan", None, "tm"), check_vma=False
    )
```

```python
import functools
import math

import jax
import jax.numpy as jnp
import ml_dtypes
import numpy as np
from jax import lax
from jax.experimental import pallas as pl
from jax.experimental.pallas import tpu as pltpu
from jax.sharding import PartitionSpec as P

SUBARRAY = 128
STRIDE = 64
TAPS = 8
FRACS = 8
LAG = 16
RIM = 20
LAGS = 40
GROUPS = 5
SHIFTS = LAGS // GROUPS


def split_table(table):
    high = table.astype(ml_dtypes.bfloat16)
    low = (table - high.astype(np.float64)).astype(ml_dtypes.bfloat16)
    return high, low


def time_table(block_len, devices):
    half_len = block_len // 2
    freq = np.arange(half_len)
    phase = (freq[:, None] * np.arange(block_len)[None, :] % block_len) * (2.0 * math.pi / block_len)
    both = np.stack([np.cos(phase), -np.sin(phase)])
    both = both.reshape(2, devices, half_len // devices, block_len).transpose(1, 0, 2, 3)
    return split_table(both.reshape(block_len, block_len))


def local_table(local_ch):
    ids = np.arange(local_ch)
    phase = (ids[:, None] * ids[None, :] % local_ch) * (2.0 * math.pi / local_ch)
    c, s = np.cos(phase), np.sin(phase)
    return np.block([[c, -s], [s, c]]).astype(np.float32)


def twist_tables(devices, local_ch):
    phase = np.arange(devices)[:, None] * np.arange(local_ch)[None, :] * (2.0 * math.pi / (devices * local_ch))
    return np.cos(phase).astype(np.float32), np.sin(phase).astype(np.float32)


def small_dft(re, im, sign):
    count = len(re)
    if count == 1:
        return re, im
    even_re, even_im = small_dft(re[0::2], im[0::2], sign)
    odd_re, odd_im = small_dft(re[1::2], im[1::2], sign)
    out_re, out_im = [None] * count, [None] * count
    half = count // 2
    for k in range(half):
        if k == 0:
            tr, ti = odd_re[k], odd_im[k]
        elif 4 * k == count:
            tr, ti = -sign * odd_im[k], sign * odd_re[k]
        else:
            c = math.cos(2.0 * math.pi * k / count)
            s = sign * math.sin(2.0 * math.pi * k / count)
            tr = odd_re[k] * c - odd_im[k] * s
            ti = odd_im[k] * c + odd_re[k] * s
        out_re[k], out_im[k] = even_re[k] + tr, even_im[k] + ti
        out_re[k + half], out_im[k + half] = even_re[k] - tr, even_im[k] - ti
    return out_re, out_im


def flip_wavenumbers(rows_table):
    return jnp.roll(rows_table[:, ::-1], 1, axis=1)


def grouped_weights(tap_table, delay_whole, tap_index):
    table = tap_table.astype(jnp.float32)
    coeffs = []
    for tap_pos in range(TAPS):
        value = jnp.zeros(tap_index.shape, jnp.float32)
        for frac in range(FRACS):
            value = jnp.where(tap_index == frac, table[frac, tap_pos], value)
        coeffs.append(value)
    lag = (
        SHIFTS * jnp.arange(GROUPS, dtype=jnp.int32)[:, None, None, None]
        + jnp.arange(SHIFTS, dtype=jnp.int32)[None, None, :, None]
    )
    tap = lag - (delay_whole + LAG)[None, :, None, :]
    weights = jnp.zeros(tap.shape, jnp.float32)
    for tap_pos in range(TAPS):
        weights = jnp.where(tap == tap_pos, coeffs[tap_pos][None, :, None, :], weights)
    rows = GROUPS * delay_whole.shape[0]
    return weights.astype(jnp.bfloat16).reshape(rows, SHIFTS * delay_whole.shape[1])


def dot_f32(left_op, right_op, precision=None):
    return jnp.dot(left_op, right_op, precision=precision, preferred_element_type=jnp.float32)


def body(record, fk_mask, tap_table, delay_whole, tap_index):
    block_len, local_ch = record.shape
    devices = lax.axis_size("chan")
    band_rows, channels = fk_mask.shape
    slow_count = delay_whole.shape[0]
    table_hi, table_lo = time_table(block_len, devices)
    table_hi, table_lo = jnp.asarray(table_hi), jnp.asarray(table_lo)

    rec_hi = record.astype(jnp.bfloat16)
    rec_lo = (record - rec_hi.astype(jnp.float32)).astype(jnp.bfloat16)
    first = dot_f32(table_hi, jnp.concatenate([rec_hi, rec_lo], axis=1))
    spectrum = first[:, :local_ch] + first[:, local_ch:] + dot_f32(table_lo, rec_hi)
    sent = spectrum.astype(jnp.bfloat16).reshape(devices, 2 * band_rows, local_ch)
    got = lax.all_to_all(sent, "chan", split_axis=0, concat_axis=0, tiled=True)

    own_band = fk_mask.astype(jnp.float32)
    freq = lax.axis_index("chan") * band_rows + jnp.arange(band_rows, dtype=jnp.int32)
    at_zero = (freq == 0)[:, None]
    band = jnp.where(at_zero, own_band * flip_wavenumbers(own_band), own_band)
    scale = jnp.where(at_zero, 1.0, 2.0) / (block_len * channels)
    band = (band * scale).reshape(band_rows, local_ch, devices).transpose(2, 0, 1)
    band = band.reshape(devices * band_rows, local_ch)

    cos_twist, sin_twist = twist_tables(devices, local_ch)
    mix = local_table(local_ch)
    parts = got.astype(jnp.float32)
    re, im = small_dft(
        [parts[d, :band_rows] for d in range(devices)],
        [parts[d, band_rows:] for d in range(devices)],
        -1.0,
    )
    turned = []
    for d in range(devices):
        c, s = cos_twist[d][None], sin_twist[d][None]
        turned.append(jnp.concatenate([re[d] * c + im[d] * s, im[d] * c - re[d] * s], axis=1))
    wave = dot_f32(jnp.concatenate(turned, axis=0), mix, lax.Precision.HIGH)
    kept = wave * jnp.concatenate([band, band], axis=1)
    back = dot_f32(kept, mix.T, lax.Precision.HIGH).reshape(devices, band_rows, 2 * local_ch)
    re, im = [], []
    for d in range(devices):
        c, s = cos_twist[d][None], sin_twist[d][None]
        b_re, b_im = back[d, :, :local_ch], back[d, :, local_ch:]
        re.append(b_re * c - b_im * s)
        im.append(b_im * c + b_re * s)
    re, im = small_dft(re, im, 1.0)
    reach = SUBARRAY - STRIDE
    slabs = []
    for d in range(devices):
        if d + 1 < devices:
            rim = jnp.concatenate([re[d + 1][:, :reach], im[d + 1][:, :reach]], axis=1)
        else:
            rim = jnp.zeros((band_rows, 2 * reach), jnp.float32)
        slabs.append(jnp.concatenate([re[d], im[d], rim], axis=0).astype(jnp.bfloat16))
    back_got = lax.all_to_all(jnp.stack(slabs), "chan", split_axis=0, concat_axis=0, tiled=True)
    own = back_got[:, : 2 * band_rows].reshape(block_len, local_ch)
    rim = back_got[:, 2 * band_rows :].reshape(devices, band_rows, 2, reach)
    rim = rim.transpose(0, 2, 1, 3).reshape(block_len, reach)
    rows = jnp.concatenate([own, rim], axis=1)
    contract = (((0,), (0,)), ((), ()))
    field = lax.dot_general(rows, table_hi, contract, preferred_element_type=jnp.float32)
    field = field + lax.dot_general(rows, table_lo, contract, preferred_element_type=jnp.float32)
    filtered = field.astype(jnp.bfloat16)

    count = lax.axis_size("tm")
    forward = [(i, i + 1) for i in range(count - 1)]
    backward = [(i + 1, i) for i in range(count - 1)]
    low = lax.ppermute(filtered[:, block_len - RIM :], "tm", forward)
    high = lax.ppermute(filtered[:, :RIM], "tm", backward)
    extended = jnp.concatenate([low, filtered, high], axis=1)

    weights = grouped_weights(tap_table, delay_whole, tap_index)
    span = block_len + SHIFTS * (GROUPS - 1)
    shifted = jnp.stack([extended[:, r + 1 : r + 1 + span] for r in range(SHIFTS)])
    beams = []
    for a in range(local_ch // STRIDE):
        chosen = shifted[:, a * STRIDE : a * STRIDE + SUBARRAY].reshape(SHIFTS * SUBARRAY, span)
        sums = dot_f32(weights, chosen).reshape(GROUPS, slow_count, span)
        total = sums[0, :, :block_len]
        for g in range(1, GROUPS):
            total = total + sums[g, :, SHIFTS * g : SHIFTS * g + block_len]
        beams.append(total)
    return jnp.stack(beams).astype(jnp.bfloat16)


TILE = 128
EDGE = 32
LEAD = 8
PHASE = 8
MESH = pl.DeviceIdType.MESH


def flipped_bits(number, mask, count):
    result, bit = 0, 1
    while bit < count:
        digit = number // bit % 2
        result = result + (1 - digit if mask // bit % 2 else digit) * bit
        bit *= 2
    return result


def triple(table):
    high, low = split_table(table.astype(np.float64))
    return np.concatenate([high, high, low], axis=0)


def parity_tables(block_len, devices):
    half_len = block_len // 2
    count = half_len // devices // 2
    tables = []
    for parity in range(2):
        freq = np.arange(devices)[:, None] * 2 * count + 2 * np.arange(count)[None, :] + parity
        phase = (freq[:, :, None] * np.arange(half_len) % block_len) * (2.0 * math.pi / block_len)
        tables.append(np.stack([np.cos(phase), -np.sin(phase)], axis=1).reshape(half_len, half_len))
    tables = np.stack(tables)
    ahead = np.concatenate(split_table(tables), axis=2)
    back = np.concatenate(split_table(tables.transpose(0, 2, 1)), axis=2)
    return ahead, back


def split_dot(left_op, right_ref):
    high = left_op.astype(jnp.bfloat16)
    low = (left_op - high.astype(jnp.float32)).astype(jnp.bfloat16)
    return dot_f32(jnp.concatenate([high, low, high], axis=1), right_ref[...])


def fused(
    devices,
    blocks,
    tap_hbm,
    rec_hbm,
    mask_hbm,
    delay_hbm,
    index_hbm,
    mix_hbm,
    unmix_hbm,
    cos_hbm,
    sin_hbm,
    ahead_hbm,
    behind_hbm,
    out_ref,
    tap_ref,
    rec_ref,
    mask_ref,
    delay_ref,
    index_ref,
    mix_ref,
    unmix_ref,
    cos_ref,
    sin_ref,
    ahead,
    behind,
    folded,
    sent,
    got,
    wave,
    band,
    back_sent,
    back_got,
    ext,
    edge_sent,
    edge_got,
    rim_sent,
    rim_got,
    weights,
    shifted,
    partial,
    sums,
    load_sem,
    table_sem,
    send_sem,
    recv_sem,
    edge_send,
    edge_recv,
    rim_sem,
):
    me = lax.axis_index("chan")
    blk = lax.axis_index("tm")
    block_len, local_ch = rec_ref.shape
    half_len = block_len // 2
    band_rows, channels = mask_ref.shape
    half_rows = band_rows // 2
    slow_count = delay_ref.shape[0]
    f32, bf16 = jnp.float32, jnp.bfloat16
    is_first, is_last = me == 0, me == devices - 1
    low_blk, high_blk = blk > 0, blk < blocks - 1
    order = list(range(devices - 1, 0, -1))
    peer = {k: flipped_bits(me, k, devices) for k in order}

    def count_of(flag):
        return jnp.where(flag, 1, 0)

    loads = [
        pltpu.make_async_copy(source, target, load_sem.at[place])
        for place, (source, target) in enumerate(
            (
                (rec_hbm, rec_ref),
                (tap_hbm, tap_ref),
                (mask_hbm, mask_ref),
                (delay_hbm, delay_ref),
                (index_hbm, index_ref),
                (cos_hbm, cos_ref),
                (sin_hbm, sin_ref),
                (mix_hbm, mix_ref),
                (unmix_hbm, unmix_ref),
            )
        )
    ]
    tables = [
        pltpu.make_async_copy(ahead_hbm.at[0], ahead.at[0], table_sem.at[0]),
        pltpu.make_async_copy(ahead_hbm.at[1], ahead.at[1], table_sem.at[1]),
        pltpu.make_async_copy(behind_hbm, behind, table_sem.at[2]),
    ]
    loads[0].start()
    tables[0].start()

    barrier = pltpu.get_barrier_semaphore()

    def greet(block, shard):
        pl.semaphore_signal(barrier, inc=1, device_id=(block, shard), device_id_type=MESH)

    for k in order:
        greet(blk, peer[k])
    for there, block in ((low_blk, blk - 1), (high_blk, blk + 1)):

        @pl.when(there)
        def _():
            greet(block, me)

        @pl.when(there & (me < devices - 1))
        def _():
            greet(block, me + 1)

    tables[1].start()
    for load in loads[1:]:
        load.start()
    tables[2].start()

    def fold(parity):
        first, second = rec_ref[:half_len], rec_ref[half_len:]
        value = first - second if parity else first + second
        high = value.astype(bf16)
        folded[:half_len, :local_ch] = high
        folded[:half_len, local_ch:] = (value - high.astype(f32)).astype(bf16)
        folded[half_len:, :local_ch] = high
        folded[half_len:, local_ch:] = jnp.zeros_like(high)

    copies = {}
    loads[0].wait()
    for parity in range(2):
        fold(parity)
        tables[parity].wait()
        both = dot_f32(ahead[parity], folded[...])
        part = (both[:, :local_ch] + both[:, local_ch:]).astype(bf16)
        sent[parity] = part.reshape(devices, band_rows, local_ch)
        if parity == 0:
            neighbours = count_of(low_blk) + count_of(high_blk)
            pl.semaphore_wait(barrier, devices - 1 + neighbours * (1 + count_of(me > 0)))
        for k in order:
            copies[parity, k] = pltpu.make_async_remote_copy(
                src_ref=sent.at[parity, peer[k]],
                dst_ref=got.at[parity, me],
                send_sem=send_sem.at[0, parity, k],
                recv_sem=recv_sem.at[0, parity, k],
                device_id=(blk, peer[k]),
                device_id_type=MESH,
            )
            copies[parity, k].start()
        got[parity, me] = sent[parity, me]

    for load in loads[1:]:
        load.wait()
    put_id = lax.broadcasted_iota(jnp.int32, (band_rows, band_rows), 0)
    take_id = lax.broadcasted_iota(jnp.int32, (band_rows, band_rows), 1)
    taken = jnp.where(put_id < half_rows, 2 * put_id, 2 * (put_id - half_rows) + 1)
    sort = jnp.where(take_id == taken, 1.0, 0.0).astype(bf16)
    mask = dot_f32(sort, mask_ref[...].astype(f32).astype(bf16)).astype(bf16)
    wave_id = lax.broadcasted_iota(jnp.int32, (channels, local_ch), 0)
    lane_id = lax.broadcasted_iota(jnp.int32, (channels, local_ch), 1)
    bands = []
    for k1 in range(devices):
        pick = jnp.where(wave_id == lane_id * devices + k1, 1.0, 0.0).astype(bf16)
        bands.append(dot_f32(mask, pick))
    from_id = lax.broadcasted_iota(jnp.int32, (local_ch, local_ch), 0)
    to_id = lax.broadcasted_iota(jnp.int32, (local_ch, local_ch), 1)
    row_id = lax.broadcasted_iota(jnp.int32, (band_rows, local_ch), 0)
    at_zero = (row_id == 0) & is_first
    scale = jnp.where(at_zero, 1.0, 2.0) / (block_len * channels)
    for k1 in range(devices):
        total = from_id + to_id
        if k1 == 0:
            turn = jnp.where((total == local_ch) | (total == 0), 1.0, 0.0)
        else:
            turn = jnp.where(total == local_ch - 1, 1.0, 0.0)
        mirror = dot_f32(bands[(devices - k1) % devices].astype(bf16), turn.astype(bf16))
        own = jnp.where(at_zero, bands[k1] * mirror, bands[k1]) * scale
        for parity in range(2):
            band[parity, k1 * half_rows : (k1 + 1) * half_rows] = own[parity * half_rows : (parity + 1) * half_rows]

    step = 16

    def over_channels(parity):
        for low_row in range(0, half_rows, step):
            re = [got[parity, d, low_row : low_row + step].astype(f32) for d in range(devices)]
            im = [
                got[parity, d, half_rows + low_row : half_rows + low_row + step].astype(f32)
                for d in range(devices)
            ]
            re, im = small_dft(re, im, -1.0)
            for d in range(devices):
                c, s = cos_ref[d : d + 1], sin_ref[d : d + 1]
                rows = slice(d * half_rows + low_row, d * half_rows + low_row + step)
                wave[rows, :local_ch] = re[d] * c + im[d] * s
                wave[rows, local_ch:] = im[d] * c - re[d] * s
        spread = split_dot(wave[...], mix_ref)
        kept = spread * jnp.concatenate([band[parity], band[parity]], axis=1)
        wave[...] = split_dot(kept, unmix_ref)
        for low_row in range(0, half_rows, step):
            re, im = [], []
            for d in range(devices):
                c, s = cos_ref[d : d + 1], sin_ref[d : d + 1]
                rows = slice(d * half_rows + low_row, d * half_rows + low_row + step)
                b_re, b_im = wave[rows, :local_ch], wave[rows, local_ch:]
                re.append(b_re * c - b_im * s)
                im.append(b_im * c + b_re * s)
            re, im = small_dft(re, im, 1.0)
            for d in range(devices):
                back_sent[parity, d, low_row : low_row + step] = re[d].astype(bf16)
                back_sent[parity, d, half_rows + low_row : half_rows + low_row + step] = im[d].astype(bf16)

    back_copies = {}
    for parity in range(2):
        for k in order:
            copies[parity, k].wait_recv()
        over_channels(parity)
        for k in order:
            back_copies[parity, k] = pltpu.make_async_remote_copy(
                src_ref=back_sent.at[parity, peer[k]],
                dst_ref=back_got.at[parity, me],
                send_sem=send_sem.at[1, parity, k],
                recv_sem=recv_sem.at[1, parity, k],
                device_id=(blk, peer[k]),
                device_id_type=MESH,
            )
            back_copies[parity, k].start()
        back_got[parity, me] = back_sent[parity, me]

    tables[2].wait()

    def drain_exchanges():
        for parity in range(2):
            for k in order:
                copies[parity, k].wait_send()
                back_copies[parity, k].wait_send()

    table = tap_ref[...].astype(f32)
    starts = delay_ref[...].astype(f32).T.astype(jnp.int32) + LAG
    index_t = index_ref[...].astype(f32).T.astype(jnp.int32)
    blank = jnp.zeros((PHASE * STRIDE, slow_count), bf16)
    for part in range(2):
        weights[part, LAGS * STRIDE :, :slow_count] = blank
        weights[part, : PHASE * STRIDE, slow_count:] = blank
    for first in range(0, SUBARRAY, 32):
        start = starts[first : first + 32]
        index = index_t[first : first + 32]
        coeffs = []
        for tap_pos in range(TAPS):
            value = jnp.zeros(index.shape, f32)
            for frac in range(FRACS):
                value = jnp.where(index == frac, table[frac : frac + 1, tap_pos : tap_pos + 1], value)
            coeffs.append(value)
        for lag in range(LAGS):
            value = jnp.zeros(index.shape, f32)
            for tap_pos in range(TAPS):
                if 0 <= lag - tap_pos <= 2 * LAG:
                    value = jnp.where(start == lag - tap_pos, coeffs[tap_pos], value)
            value = value.astype(bf16)
            for phase in range(2):
                part, place = divmod(first, STRIDE)
                top = (lag + PHASE * phase) * STRIDE + place
                weights[part, top : top + 32, phase * slow_count : (phase + 1) * slow_count] = value
    for parity in range(2):
        for k in order:
            back_copies[parity, k].wait_recv()
        rows = back_got[parity].reshape(half_len, local_ch)
        if parity == 0:
            even = dot_f32(behind[0], jnp.concatenate([rows, rows], axis=0))
    at_edge = jnp.concatenate([behind[1, :EDGE, :half_len], behind[1, half_len - EDGE :, :half_len]], axis=0)
    odd_edge = dot_f32(at_edge, rows)
    edge_sent[0] = (even[:EDGE] + odd_edge[:EDGE]).astype(bf16)
    edge_sent[1] = (even[half_len - EDGE :] - odd_edge[EDGE:]).astype(bf16)

    def edge_copy(side, beside):
        return pltpu.make_async_remote_copy(
            src_ref=edge_sent.at[side],
            dst_ref=edge_got.at[beside, side],
            send_sem=edge_send.at[beside, side],
            recv_sem=edge_recv.at[beside, side],
            device_id=(blk - 1 + 2 * side, me - beside),
            device_id_type=MESH,
        )

    edges = {(side, beside): edge_copy(side, beside) for side in range(2) for beside in range(2)}
    leaves = (low_blk, high_blk)
    for side in range(2):
        for beside in range(2):

            @pl.when(leaves[side] & (me > 0) if beside else leaves[side])
            def _():
                edges[side, beside].start()

    quarter = half_len // 2
    left = lax.broadcasted_iota(jnp.int32, (quarter, local_ch), 1) < STRIDE
    rim_copies, fields = [], []
    for first in (0, quarter):
        odd = dot_f32(behind[1, first : first + quarter, :half_len], rows)
        some = even[first : first + quarter]
        field = [some + odd, some - odd]
        field += [pltpu.roll(part, STRIDE, 1) for part in field]
        fields.append(field)
        rim_sent[first : first + quarter] = jnp.where(left, field[0], field[3]).astype(bf16)
        copy = pltpu.make_async_remote_copy(
            src_ref=rim_sent.at[first : first + quarter],
            dst_ref=rim_got.at[first : first + quarter],
            send_sem=rim_sem.at[0, len(rim_copies)],
            recv_sem=rim_sem.at[1, len(rim_copies)],
            device_id=(blk, me - 1),
            device_id_type=MESH,
        )
        rim_copies.append(copy)

        @pl.when(me > 0)
        def _():
            copy.start()

    early, late, swapped_early, swapped_late = [jnp.concatenate(parts, axis=0) for parts in zip(*fields)]
    top, middle, end = LEAD + EDGE, LEAD + EDGE + half_len, LEAD + EDGE + block_len
    for group, (plain, other) in enumerate((((early, late), (swapped_early, swapped_late)),) * 2):
        low_part, next_part = (other, plain) if group else (plain, other)
        for place, rows in enumerate(((top, middle), (middle, end))):
            ext[group, rows[0] - 1 : rows[1] - 1] = next_part[place]
        for place, rows in enumerate(((top, middle), (middle, end))):
            ext[group, rows[0] : rows[1], :STRIDE] = low_part[place][:, :STRIDE]

    def take_edge(side, beside):
        here = leaves[1 - side]

        @pl.when(here & (me < devices - 1) if beside else here)
        def _():
            edges[side, beside].wait_recv()

        @pl.when(jnp.logical_not(here & (me < devices - 1) if beside else here))
        def _():
            edge_got[beside, side] = jnp.zeros(edge_got.shape[2:], bf16)

    def put_edge(side, beside):
        begin = (end, LEAD)[side]
        plain = edge_got[beside, side].astype(f32)
        other = pltpu.roll(plain, STRIDE, 1)
        for group in ((2,) if beside else (0, 1)):
            low_part, next_part = (other, plain) if group == 1 else (plain, other)
            before = slice(begin - 1, begin - 1 + EDGE)
            ext[group, before] = jnp.where(left[:EDGE], ext[group, before], next_part)
            ext[group, begin : begin + EDGE, :STRIDE] = low_part[:, :STRIDE]

    pairs = PHASE // 2

    def shift_rows(group, row, count):
        for i in range(pairs):
            halves = []
            for place in (0, half_len):
                begin = top - RIM + 1 + 2 * i + row + place
                value = ext[group, begin : begin + count]
                halves.append(value.reshape(count // (2 * PHASE), 2, PHASE, local_ch))
            for odd in range(2):
                pair = jnp.stack([halves[0][:, odd], halves[1][:, odd]], axis=1).reshape(count, local_ch)
                shifted[group, odd, row : row + count, i * local_ch : (i + 1) * local_ch] = pair.astype(bf16)

    steps = weights.shape[1] // (PHASE * STRIDE)
    core = half_len - 2 * EDGE
    inside = ((EDGE, core),)
    outside = ((0, EDGE), (half_len - EDGE, EDGE))

    def operand(chosen):
        columns = []
        for g in range(steps):
            low_row = 2 * PHASE * (g // 2)
            pieces = [
                shifted[group, g % 2, first + low_row : first + low_row + count]
                for group, spans in chosen
                for first, count in spans
            ]
            columns.append(pieces[0] if len(pieces) == 1 else jnp.concatenate(pieces, axis=0))
        return jnp.concatenate(columns, axis=1)

    def keep_sums(a, total, spans):
        taken = 0
        for first, count in spans:
            parts = total[taken : taken + count].reshape(count // (2 * PHASE), 2, PHASE, 2 * slow_count)
            for half in range(2):
                pair = jnp.stack([parts[:, half, :, :slow_count], parts[:, half, :, slow_count:]], axis=1)
                sums[a, half, first : first + count] = pair.reshape(count, slow_count)
            taken += count

    def put(a, first, count):
        for half in range(2):
            lanes = half * half_len + first
            out_ref[a, :, lanes : lanes + count] = sums[a, half, first : first + count].T.astype(bf16)

    half_core = core // 2
    shift_rows(0, EDGE, half_core + EDGE)
    shift_rows(1, EDGE, half_core + EDGE)
    chunk = ((EDGE, half_core),)
    total = dot_f32(operand([(0, chunk)]), weights[0]) + dot_f32(operand([(1, chunk)]), weights[1])
    shift_rows(0, half_core + 2 * EDGE, half_core)
    keep_sums(0, total, chunk)
    shift_rows(1, half_core + 2 * EDGE, half_core)
    chunk = ((EDGE + half_core, half_core),)
    total = dot_f32(operand([(0, chunk)]), weights[0]) + dot_f32(operand([(1, chunk)]), weights[1])
    keep_sums(0, total, chunk)
    partial[...] = dot_f32(operand([(1, inside)]), weights[0])
    put(0, TILE, half_len - 2 * TILE)

    for beside in range(2):
        for side in range(2):
            take_edge(side, beside)

    @pl.when(me < devices - 1)
    def _():
        for copy in rim_copies:
            copy.wait_recv()

    @pl.when(is_last)
    def _():
        rim_got[...] = jnp.zeros(rim_got.shape, bf16)

    for side in range(2):
        put_edge(side, 0)
    for group in range(2):
        for row in (0, half_len):
            shift_rows(group, row, EDGE)
    around = dot_f32(operand([(0, outside), (1, outside)]), weights[0])
    rim = rim_got[...].astype(f32)
    swapped_rim = pltpu.roll(rim, STRIDE, 1)
    ext[2, top - 1 : middle - 1] = swapped_rim
    ext[2, middle - 1 : end - 1] = rim
    ext[2, top:middle, :STRIDE] = rim[:, :STRIDE]
    ext[2, middle:end, :STRIDE] = swapped_rim[:, :STRIDE]
    for side in range(2):
        put_edge(side, 1)
    shift_rows(2, 0, half_len + EDGE)
    cut = 2 * EDGE
    many = half_len - TILE - EDGE
    firsts, lasts = ((EDGE, many),), ((EDGE + many, core - many),)
    more = dot_f32(operand([(1, outside), (2, outside), (2, firsts)]), weights[1])
    keep_sums(0, around[:cut] + more[:cut], outside)
    keep_sums(1, around[cut:] + more[cut : 2 * cut], outside)
    keep_sums(1, partial[:many] + more[2 * cut :], firsts)
    more = dot_f32(operand([(2, lasts)]), weights[1])
    for first in (0, half_len - TILE):
        put(0, first, TILE)
    put(1, 0, half_len - TILE)
    keep_sums(1, partial[many:] + more, lasts)
    put(1, half_len - TILE, TILE)

    drain_exchanges()
    for side in range(2):
        for beside in range(2):

            @pl.when(leaves[side] & (me > 0) if beside else leaves[side])
            def _():
                edges[side, beside].wait_send()

    @pl.when(me > 0)
    def _():
        for copy in rim_copies:
            copy.wait_send()


def fused_body(devices, blocks, record, fk_mask, tap_table, delay_whole, tap_index):
    block_len, local_ch = record.shape
    band_rows, channels = fk_mask.shape
    slow_count = delay_whole.shape[0]
    half_len, half_rows = block_len // 2, band_rows // 2
    ahead, behind = parity_tables(block_len, devices)
    cos_twist, sin_twist = twist_tables(devices, local_ch)
    mix = local_table(local_ch)
    subarrays = local_ch // STRIDE
    span = half_len + EDGE
    bf16 = jnp.bfloat16
    vmem = pl.BlockSpec(memory_space=pltpu.VMEM)
    hbm = pl.BlockSpec(memory_space=pltpu.HBM)
    return pl.pallas_call(
        functools.partial(fused, devices, blocks),
        out_shape=pltpu.VMEM((subarrays, slow_count, block_len), bf16),
        in_specs=[hbm] * 11,
        out_specs=vmem,
        scratch_shapes=[
            pltpu.VMEM(tap_table.shape, bf16),
            pltpu.VMEM((block_len, local_ch), jnp.float32),
            pltpu.VMEM((band_rows, channels), jnp.int32),
            pltpu.VMEM((slow_count, SUBARRAY), jnp.int32),
            pltpu.VMEM((slow_count, SUBARRAY), jnp.int32),
            pltpu.VMEM((6 * local_ch, 2 * local_ch), bf16),
            pltpu.VMEM((6 * local_ch, 2 * local_ch), bf16),
            pltpu.VMEM((devices, local_ch), jnp.float32),
            pltpu.VMEM((devices, local_ch), jnp.float32),
            pltpu.VMEM(ahead.shape, bf16),
            pltpu.VMEM(behind.shape, bf16),
            pltpu.VMEM((block_len, 2 * local_ch), bf16),
            pltpu.VMEM((2, devices, band_rows, local_ch), bf16),
            pltpu.VMEM((2, devices, band_rows, local_ch), bf16),
            pltpu.VMEM((devices * half_rows, 2 * local_ch), jnp.float32),
            pltpu.VMEM((2, devices * half_rows, local_ch), jnp.float32),
            pltpu.VMEM((2, devices, band_rows, local_ch), bf16),
            pltpu.VMEM((2, devices, band_rows, local_ch), bf16),
            pltpu.VMEM((3, LEAD + block_len + 2 * EDGE, local_ch), jnp.float32),
            pltpu.VMEM((2, EDGE, local_ch), bf16),
            pltpu.VMEM((2, 2, EDGE, local_ch), bf16),
            pltpu.VMEM((half_len, local_ch), bf16),
            pltpu.VMEM((half_len, local_ch), bf16),
            pltpu.VMEM((2, (LAGS + PHASE) * STRIDE, 2 * slow_count), bf16),
            pltpu.VMEM((3, 2, span, PHASE * STRIDE), bf16),
            pltpu.VMEM((half_len - 2 * EDGE, 2 * slow_count), jnp.float32),
            pltpu.VMEM((subarrays, 2, half_len, slow_count), jnp.float32),
            pltpu.SemaphoreType.DMA((9,)),
            pltpu.SemaphoreType.DMA((3,)),
            pltpu.SemaphoreType.DMA((2, 2, devices)),
            pltpu.SemaphoreType.DMA((2, 2, devices)),
            pltpu.SemaphoreType.DMA((2, 2)),
            pltpu.SemaphoreType.DMA((2, 2)),
            pltpu.SemaphoreType.DMA((2, 2)),
        ],
        compiler_params=pltpu.CompilerParams(
            collective_id=0, has_side_effects=True, vmem_limit_bytes=60 * 2**20
        ),
    )(
        tap_table,
        record,
        fk_mask,
        delay_whole,
        tap_index,
        jnp.asarray(triple(mix)),
        jnp.asarray(triple(mix.T)),
        jnp.asarray(cos_twist),
        jnp.asarray(sin_twist),
        jnp.asarray(ahead),
        jnp.asarray(behind),
    )


def solution(mesh):
    placed = (P("tm", "chan"), P("chan", None), P(), P(), P())
    devices, blocks = mesh.shape["chan"], mesh.shape["tm"]

    def placed_body(record, *others):
        block_len, local_ch = record.shape
        if local_ch == TILE and block_len // devices == TILE:
            return fused_body(devices, blocks, record, *others)
        return body(record, *others)

    return jax.shard_map(
        placed_body, mesh=mesh, in_specs=placed, out_specs=P("chan", None, "tm"), check_vma=False
    )
```

```python
import functools
import math

import jax
import jax.numpy as jnp
import ml_dtypes
import numpy as np
from jax import lax
from jax.experimental import pallas as pl
from jax.experimental.pallas import tpu as pltpu
from jax.sharding import PartitionSpec as P

SUBARRAY = 128
STRIDE = 64
TAPS = 8
FRACS = 8
LAG = 16
RIM = 20
LAGS = 40
GROUPS = 5
SHIFTS = LAGS // GROUPS


def split_table(table):
    high = table.astype(ml_dtypes.bfloat16)
    low = (table - high.astype(np.float64)).astype(ml_dtypes.bfloat16)
    return high, low


def time_table(block_len, devices):
    half_len = block_len // 2
    freq = np.arange(half_len)
    phase = (freq[:, None] * np.arange(block_len)[None, :] % block_len) * (2.0 * math.pi / block_len)
    both = np.stack([np.cos(phase), -np.sin(phase)])
    both = both.reshape(2, devices, half_len // devices, block_len).transpose(1, 0, 2, 3)
    return split_table(both.reshape(block_len, block_len))


def local_table(local_ch):
    ids = np.arange(local_ch)
    phase = (ids[:, None] * ids[None, :] % local_ch) * (2.0 * math.pi / local_ch)
    c, s = np.cos(phase), np.sin(phase)
    return np.block([[c, -s], [s, c]]).astype(np.float32)


def twist_tables(devices, local_ch):
    phase = np.arange(devices)[:, None] * np.arange(local_ch)[None, :] * (2.0 * math.pi / (devices * local_ch))
    return np.cos(phase).astype(np.float32), np.sin(phase).astype(np.float32)


def small_dft(re, im, sign):
    count = len(re)
    if count == 1:
        return re, im
    even_re, even_im = small_dft(re[0::2], im[0::2], sign)
    odd_re, odd_im = small_dft(re[1::2], im[1::2], sign)
    out_re, out_im = [None] * count, [None] * count
    half = count // 2
    for k in range(half):
        if k == 0:
            tr, ti = odd_re[k], odd_im[k]
        elif 4 * k == count:
            tr, ti = -sign * odd_im[k], sign * odd_re[k]
        else:
            c = math.cos(2.0 * math.pi * k / count)
            s = sign * math.sin(2.0 * math.pi * k / count)
            tr = odd_re[k] * c - odd_im[k] * s
            ti = odd_im[k] * c + odd_re[k] * s
        out_re[k], out_im[k] = even_re[k] + tr, even_im[k] + ti
        out_re[k + half], out_im[k + half] = even_re[k] - tr, even_im[k] - ti
    return out_re, out_im


def flip_wavenumbers(rows_table):
    return jnp.roll(rows_table[:, ::-1], 1, axis=1)


def grouped_weights(tap_table, delay_whole, tap_index):
    table = tap_table.astype(jnp.float32)
    coeffs = []
    for tap_pos in range(TAPS):
        value = jnp.zeros(tap_index.shape, jnp.float32)
        for frac in range(FRACS):
            value = jnp.where(tap_index == frac, table[frac, tap_pos], value)
        coeffs.append(value)
    lag = (
        SHIFTS * jnp.arange(GROUPS, dtype=jnp.int32)[:, None, None, None]
        + jnp.arange(SHIFTS, dtype=jnp.int32)[None, None, :, None]
    )
    tap = lag - (delay_whole + LAG)[None, :, None, :]
    weights = jnp.zeros(tap.shape, jnp.float32)
    for tap_pos in range(TAPS):
        weights = jnp.where(tap == tap_pos, coeffs[tap_pos][None, :, None, :], weights)
    rows = GROUPS * delay_whole.shape[0]
    return weights.astype(jnp.bfloat16).reshape(rows, SHIFTS * delay_whole.shape[1])


def dot_f32(left_op, right_op, precision=None):
    return jnp.dot(left_op, right_op, precision=precision, preferred_element_type=jnp.float32)


def body(record, fk_mask, tap_table, delay_whole, tap_index):
    block_len, local_ch = record.shape
    devices = lax.axis_size("chan")
    band_rows, channels = fk_mask.shape
    slow_count = delay_whole.shape[0]
    table_hi, table_lo = time_table(block_len, devices)
    table_hi, table_lo = jnp.asarray(table_hi), jnp.asarray(table_lo)

    rec_hi = record.astype(jnp.bfloat16)
    rec_lo = (record - rec_hi.astype(jnp.float32)).astype(jnp.bfloat16)
    first = dot_f32(table_hi, jnp.concatenate([rec_hi, rec_lo], axis=1))
    spectrum = first[:, :local_ch] + first[:, local_ch:] + dot_f32(table_lo, rec_hi)
    sent = spectrum.astype(jnp.bfloat16).reshape(devices, 2 * band_rows, local_ch)
    got = lax.all_to_all(sent, "chan", split_axis=0, concat_axis=0, tiled=True)

    own_band = fk_mask.astype(jnp.float32)
    freq = lax.axis_index("chan") * band_rows + jnp.arange(band_rows, dtype=jnp.int32)
    at_zero = (freq == 0)[:, None]
    band = jnp.where(at_zero, own_band * flip_wavenumbers(own_band), own_band)
    scale = jnp.where(at_zero, 1.0, 2.0) / (block_len * channels)
    band = (band * scale).reshape(band_rows, local_ch, devices).transpose(2, 0, 1)
    band = band.reshape(devices * band_rows, local_ch)

    cos_twist, sin_twist = twist_tables(devices, local_ch)
    mix = local_table(local_ch)
    parts = got.astype(jnp.float32)
    re, im = small_dft(
        [parts[d, :band_rows] for d in range(devices)],
        [parts[d, band_rows:] for d in range(devices)],
        -1.0,
    )
    turned = []
    for d in range(devices):
        c, s = cos_twist[d][None], sin_twist[d][None]
        turned.append(jnp.concatenate([re[d] * c + im[d] * s, im[d] * c - re[d] * s], axis=1))
    wave = dot_f32(jnp.concatenate(turned, axis=0), mix, lax.Precision.HIGH)
    kept = wave * jnp.concatenate([band, band], axis=1)
    back = dot_f32(kept, mix.T, lax.Precision.HIGH).reshape(devices, band_rows, 2 * local_ch)
    re, im = [], []
    for d in range(devices):
        c, s = cos_twist[d][None], sin_twist[d][None]
        b_re, b_im = back[d, :, :local_ch], back[d, :, local_ch:]
        re.append(b_re * c - b_im * s)
        im.append(b_im * c + b_re * s)
    re, im = small_dft(re, im, 1.0)
    reach = SUBARRAY - STRIDE
    slabs = []
    for d in range(devices):
        if d + 1 < devices:
            rim = jnp.concatenate([re[d + 1][:, :reach], im[d + 1][:, :reach]], axis=1)
        else:
            rim = jnp.zeros((band_rows, 2 * reach), jnp.float32)
        slabs.append(jnp.concatenate([re[d], im[d], rim], axis=0).astype(jnp.bfloat16))
    back_got = lax.all_to_all(jnp.stack(slabs), "chan", split_axis=0, concat_axis=0, tiled=True)
    own = back_got[:, : 2 * band_rows].reshape(block_len, local_ch)
    rim = back_got[:, 2 * band_rows :].reshape(devices, band_rows, 2, reach)
    rim = rim.transpose(0, 2, 1, 3).reshape(block_len, reach)
    rows = jnp.concatenate([own, rim], axis=1)
    contract = (((0,), (0,)), ((), ()))
    field = lax.dot_general(rows, table_hi, contract, preferred_element_type=jnp.float32)
    field = field + lax.dot_general(rows, table_lo, contract, preferred_element_type=jnp.float32)
    filtered = field.astype(jnp.bfloat16)

    count = lax.axis_size("tm")
    forward = [(i, i + 1) for i in range(count - 1)]
    backward = [(i + 1, i) for i in range(count - 1)]
    low = lax.ppermute(filtered[:, block_len - RIM :], "tm", forward)
    high = lax.ppermute(filtered[:, :RIM], "tm", backward)
    extended = jnp.concatenate([low, filtered, high], axis=1)

    weights = grouped_weights(tap_table, delay_whole, tap_index)
    span = block_len + SHIFTS * (GROUPS - 1)
    shifted = jnp.stack([extended[:, r + 1 : r + 1 + span] for r in range(SHIFTS)])
    beams = []
    for a in range(local_ch // STRIDE):
        chosen = shifted[:, a * STRIDE : a * STRIDE + SUBARRAY].reshape(SHIFTS * SUBARRAY, span)
        sums = dot_f32(weights, chosen).reshape(GROUPS, slow_count, span)
        total = sums[0, :, :block_len]
        for g in range(1, GROUPS):
            total = total + sums[g, :, SHIFTS * g : SHIFTS * g + block_len]
        beams.append(total)
    return jnp.stack(beams).astype(jnp.bfloat16)


TILE = 128
EDGE = 32
LEAD = 8
PHASE = 8
MESH = pl.DeviceIdType.MESH


def flipped_bits(number, mask, count):
    result, bit = 0, 1
    while bit < count:
        digit = number // bit % 2
        result = result + (1 - digit if mask // bit % 2 else digit) * bit
        bit *= 2
    return result


def triple(table):
    high, low = split_table(table.astype(np.float64))
    return np.concatenate([high, high, low], axis=0)


def parity_tables(block_len, devices):
    half_len = block_len // 2
    count = half_len // devices // 2
    tables = []
    for parity in range(2):
        freq = np.arange(devices)[:, None] * 2 * count + 2 * np.arange(count)[None, :] + parity
        phase = (freq[:, :, None] * np.arange(half_len) % block_len) * (2.0 * math.pi / block_len)
        tables.append(np.stack([np.cos(phase), -np.sin(phase)], axis=1).reshape(half_len, half_len))
    tables = np.stack(tables)
    ahead = np.concatenate(split_table(tables), axis=2)
    back = np.concatenate(split_table(tables.transpose(0, 2, 1)), axis=2)
    return ahead, back


def split_dot(left_op, right_ref):
    high = left_op.astype(jnp.bfloat16)
    low = (left_op - high.astype(jnp.float32)).astype(jnp.bfloat16)
    return dot_f32(jnp.concatenate([high, low, high], axis=1), right_ref[...])


def fused(
    devices,
    blocks,
    tap_hbm,
    rec_hbm,
    mask_hbm,
    delay_hbm,
    index_hbm,
    mix_hbm,
    unmix_hbm,
    cos_hbm,
    sin_hbm,
    ahead_hbm,
    behind_hbm,
    out_ref,
    tap_ref,
    rec_ref,
    mask_ref,
    delay_ref,
    index_ref,
    mix_ref,
    unmix_ref,
    cos_ref,
    sin_ref,
    ahead,
    behind,
    folded,
    sent,
    got,
    wave,
    band,
    back_sent,
    back_got,
    ext,
    edge_sent,
    edge_got,
    rim_sent,
    rim_got,
    weights,
    shifted,
    partial,
    sums,
    load_sem,
    table_sem,
    send_sem,
    recv_sem,
    edge_send,
    edge_recv,
    rim_sem,
):
    me = lax.axis_index("chan")
    blk = lax.axis_index("tm")
    block_len, local_ch = rec_ref.shape
    half_len = block_len // 2
    band_rows, channels = mask_ref.shape
    half_rows = band_rows // 2
    slow_count = delay_ref.shape[0]
    f32, bf16 = jnp.float32, jnp.bfloat16
    is_first, is_last = me == 0, me == devices - 1
    low_blk, high_blk = blk > 0, blk < blocks - 1
    order = list(range(devices - 1, 0, -1))
    peer = {k: flipped_bits(me, k, devices) for k in order}

    def count_of(flag):
        return jnp.where(flag, 1, 0)

    loads = [
        pltpu.make_async_copy(source, target, load_sem.at[place])
        for place, (source, target) in enumerate(
            (
                (rec_hbm, rec_ref),
                (tap_hbm, tap_ref),
                (mask_hbm, mask_ref),
                (delay_hbm, delay_ref),
                (index_hbm, index_ref),
                (cos_hbm, cos_ref),
                (sin_hbm, sin_ref),
                (mix_hbm, mix_ref),
                (unmix_hbm, unmix_ref),
            )
        )
    ]
    tables = [
        pltpu.make_async_copy(ahead_hbm.at[0], ahead.at[0], table_sem.at[0]),
        pltpu.make_async_copy(ahead_hbm.at[1], ahead.at[1], table_sem.at[1]),
        pltpu.make_async_copy(behind_hbm, behind, table_sem.at[2]),
    ]
    loads[0].start()
    tables[0].start()

    barrier = pltpu.get_barrier_semaphore()

    def greet(block, shard):
        pl.semaphore_signal(barrier, inc=1, device_id=(block, shard), device_id_type=MESH)

    for k in order:
        greet(blk, peer[k])
    for there, block in ((low_blk, blk - 1), (high_blk, blk + 1)):

        @pl.when(there)
        def _():
            greet(block, me)

        @pl.when(there & (me < devices - 1))
        def _():
            greet(block, me + 1)

    tables[1].start()
    for load in loads[1:]:
        load.start()
    tables[2].start()

    def fold(parity):
        first, second = rec_ref[:half_len], rec_ref[half_len:]
        value = first - second if parity else first + second
        high = value.astype(bf16)
        folded[:half_len, :local_ch] = high
        folded[:half_len, local_ch:] = (value - high.astype(f32)).astype(bf16)
        folded[half_len:, :local_ch] = high
        folded[half_len:, local_ch:] = jnp.zeros_like(high)

    copies = {}
    loads[0].wait()
    for parity in range(2):
        fold(parity)
        tables[parity].wait()
        both = dot_f32(ahead[parity], folded[...])
        part = (both[:, :local_ch] + both[:, local_ch:]).astype(bf16)
        sent[parity] = part.reshape(devices, band_rows, local_ch)
        if parity == 0:
            neighbours = count_of(low_blk) + count_of(high_blk)
            pl.semaphore_wait(barrier, devices - 1 + neighbours * (1 + count_of(me > 0)))
        for k in order:
            copies[parity, k] = pltpu.make_async_remote_copy(
                src_ref=sent.at[parity, peer[k]],
                dst_ref=got.at[parity, me],
                send_sem=send_sem.at[0, parity, k],
                recv_sem=recv_sem.at[0, parity, k],
                device_id=(blk, peer[k]),
                device_id_type=MESH,
            )
            copies[parity, k].start()
        got[parity, me] = sent[parity, me]

    for load in loads[1:]:
        load.wait()
    put_id = lax.broadcasted_iota(jnp.int32, (band_rows, band_rows), 0)
    take_id = lax.broadcasted_iota(jnp.int32, (band_rows, band_rows), 1)
    taken = jnp.where(put_id < half_rows, 2 * put_id, 2 * (put_id - half_rows) + 1)
    sort = jnp.where(take_id == taken, 1.0, 0.0).astype(bf16)
    mask = dot_f32(sort, mask_ref[...].astype(f32).astype(bf16)).astype(bf16)
    wave_id = lax.broadcasted_iota(jnp.int32, (channels, local_ch), 0)
    lane_id = lax.broadcasted_iota(jnp.int32, (channels, local_ch), 1)
    bands = []
    for k1 in range(devices):
        pick = jnp.where(wave_id == lane_id * devices + k1, 1.0, 0.0).astype(bf16)
        bands.append(dot_f32(mask, pick))
    from_id = lax.broadcasted_iota(jnp.int32, (local_ch, local_ch), 0)
    to_id = lax.broadcasted_iota(jnp.int32, (local_ch, local_ch), 1)
    row_id = lax.broadcasted_iota(jnp.int32, (band_rows, local_ch), 0)
    at_zero = (row_id == 0) & is_first
    scale = jnp.where(at_zero, 1.0, 2.0) / (block_len * channels)
    for k1 in range(devices):
        total = from_id + to_id
        if k1 == 0:
            turn = jnp.where((total == local_ch) | (total == 0), 1.0, 0.0)
        else:
            turn = jnp.where(total == local_ch - 1, 1.0, 0.0)
        mirror = dot_f32(bands[(devices - k1) % devices].astype(bf16), turn.astype(bf16))
        own = jnp.where(at_zero, bands[k1] * mirror, bands[k1]) * scale
        for parity in range(2):
            band[parity, k1 * half_rows : (k1 + 1) * half_rows] = own[parity * half_rows : (parity + 1) * half_rows]

    step = 16

    def over_channels(parity):
        for low_row in range(0, half_rows, step):
            re = [got[parity, d, low_row : low_row + step].astype(f32) for d in range(devices)]
            im = [
                got[parity, d, half_rows + low_row : half_rows + low_row + step].astype(f32)
                for d in range(devices)
            ]
            re, im = small_dft(re, im, -1.0)
            for d in range(devices):
                c, s = cos_ref[d : d + 1], sin_ref[d : d + 1]
                rows = slice(d * half_rows + low_row, d * half_rows + low_row + step)
                wave[rows, :local_ch] = re[d] * c + im[d] * s
                wave[rows, local_ch:] = im[d] * c - re[d] * s
        spread = split_dot(wave[...], mix_ref)
        kept = spread * jnp.concatenate([band[parity], band[parity]], axis=1)
        wave[...] = split_dot(kept, unmix_ref)
        for low_row in range(0, half_rows, step):
            re, im = [], []
            for d in range(devices):
                c, s = cos_ref[d : d + 1], sin_ref[d : d + 1]
                rows = slice(d * half_rows + low_row, d * half_rows + low_row + step)
                b_re, b_im = wave[rows, :local_ch], wave[rows, local_ch:]
                re.append(b_re * c - b_im * s)
                im.append(b_im * c + b_re * s)
            re, im = small_dft(re, im, 1.0)
            for d in range(devices):
                back_sent[parity, d, low_row : low_row + step] = re[d].astype(bf16)
                back_sent[parity, d, half_rows + low_row : half_rows + low_row + step] = im[d].astype(bf16)

    back_copies = {}
    for parity in range(2):
        for k in order:
            copies[parity, k].wait_recv()
        over_channels(parity)
        for k in order:
            back_copies[parity, k] = pltpu.make_async_remote_copy(
                src_ref=back_sent.at[parity, peer[k]],
                dst_ref=back_got.at[parity, me],
                send_sem=send_sem.at[1, parity, k],
                recv_sem=recv_sem.at[1, parity, k],
                device_id=(blk, peer[k]),
                device_id_type=MESH,
            )
            back_copies[parity, k].start()
        back_got[parity, me] = back_sent[parity, me]

    tables[2].wait()

    def drain_exchanges():
        for parity in range(2):
            for k in order:
                copies[parity, k].wait_send()
                back_copies[parity, k].wait_send()

    table = tap_ref[...].astype(f32)
    starts = delay_ref[...].astype(f32).T.astype(jnp.int32) + LAG
    index_t = index_ref[...].astype(f32).T.astype(jnp.int32)
    blank = jnp.zeros((PHASE * STRIDE, slow_count), bf16)
    for part in range(2):
        weights[part, LAGS * STRIDE :, :slow_count] = blank
        weights[part, : PHASE * STRIDE, slow_count:] = blank
    for first in range(0, SUBARRAY, 32):
        start = starts[first : first + 32]
        index = index_t[first : first + 32]
        coeffs = []
        for tap_pos in range(TAPS):
            value = jnp.zeros(index.shape, f32)
            for frac in range(FRACS):
                value = jnp.where(index == frac, table[frac : frac + 1, tap_pos : tap_pos + 1], value)
            coeffs.append(value)
        for lag in range(LAGS):
            value = jnp.zeros(index.shape, f32)
            for tap_pos in range(TAPS):
                if 0 <= lag - tap_pos <= 2 * LAG:
                    value = jnp.where(start == lag - tap_pos, coeffs[tap_pos], value)
            value = value.astype(bf16)
            for phase in range(2):
                part, place = divmod(first, STRIDE)
                top = (lag + PHASE * phase) * STRIDE + place
                weights[part, top : top + 32, phase * slow_count : (phase + 1) * slow_count] = value
    for parity in range(2):
        for k in order:
            back_copies[parity, k].wait_recv()
        rows = back_got[parity].reshape(half_len, local_ch)
        if parity == 0:
            even = dot_f32(behind[0], jnp.concatenate([rows, rows], axis=0))
    def edge_copy(side, beside):
        return pltpu.make_async_remote_copy(
            src_ref=edge_sent.at[side],
            dst_ref=edge_got.at[beside, side],
            send_sem=edge_send.at[beside, side],
            recv_sem=edge_recv.at[beside, side],
            device_id=(blk - 1 + 2 * side, me - beside),
            device_id_type=MESH,
        )

    edges = {(side, beside): edge_copy(side, beside) for side in range(2) for beside in range(2)}
    leaves = (low_blk, high_blk)
    quarter = half_len // 2
    left = lax.broadcasted_iota(jnp.int32, (quarter, local_ch), 1) < STRIDE
    rim_copies, fields = [], []
    for first in (0, quarter):
        odd = dot_f32(behind[1, first : first + quarter, :half_len], rows)
        some = even[first : first + quarter]
        field = [some + odd, some - odd]
        field += [pltpu.roll(part, STRIDE, 1) for part in field]
        fields.append(field)
        rim_sent[first : first + quarter] = jnp.where(left, field[0], field[3]).astype(bf16)
        copy = pltpu.make_async_remote_copy(
            src_ref=rim_sent.at[first : first + quarter],
            dst_ref=rim_got.at[first : first + quarter],
            send_sem=rim_sem.at[0, len(rim_copies)],
            recv_sem=rim_sem.at[1, len(rim_copies)],
            device_id=(blk, me - 1),
            device_id_type=MESH,
        )
        rim_copies.append(copy)

        @pl.when(me > 0)
        def _():
            copy.start()

    early, late, swapped_early, swapped_late = [jnp.concatenate(parts, axis=0) for parts in zip(*fields)]
    edge_sent[0] = early[:EDGE].astype(bf16)
    edge_sent[1] = late[half_len - EDGE :].astype(bf16)
    for side in range(2):
        for beside in range(2):

            @pl.when(leaves[side] & (me > 0) if beside else leaves[side])
            def _():
                edges[side, beside].start()

    top, middle, end = LEAD + EDGE, LEAD + EDGE + half_len, LEAD + EDGE + block_len
    for group, (plain, other) in enumerate((((early, late), (swapped_early, swapped_late)),) * 2):
        low_part, next_part = (other, plain) if group else (plain, other)
        for place, rows in enumerate(((top, middle), (middle, end))):
            ext[group, rows[0] - 1 : rows[1] - 1] = next_part[place]
        for place, rows in enumerate(((top, middle), (middle, end))):
            ext[group, rows[0] : rows[1], :STRIDE] = low_part[place][:, :STRIDE]

    def take_edge(side, beside):
        here = leaves[1 - side]

        @pl.when(here & (me < devices - 1) if beside else here)
        def _():
            edges[side, beside].wait_recv()

        @pl.when(jnp.logical_not(here & (me < devices - 1) if beside else here))
        def _():
            edge_got[beside, side] = jnp.zeros(edge_got.shape[2:], bf16)

    def put_edge(side, beside):
        begin = (end, LEAD)[side]
        plain = edge_got[beside, side].astype(f32)
        other = pltpu.roll(plain, STRIDE, 1)
        for group in ((2,) if beside else (0, 1)):
            low_part, next_part = (other, plain) if group == 1 else (plain, other)
            before = slice(begin - 1, begin - 1 + EDGE)
            ext[group, before] = jnp.where(left[:EDGE], ext[group, before], next_part)
            ext[group, begin : begin + EDGE, :STRIDE] = low_part[:, :STRIDE]

    pairs = PHASE // 2

    def shift_rows(group, row, count):
        for i in range(pairs):
            halves = []
            for place in (0, half_len):
                begin = top - RIM + 1 + 2 * i + row + place
                value = ext[group, begin : begin + count]
                halves.append(value.reshape(count // (2 * PHASE), 2, PHASE, local_ch))
            for odd in range(2):
                pair = jnp.stack([halves[0][:, odd], halves[1][:, odd]], axis=1).reshape(count, local_ch)
                shifted[group, odd, row : row + count, i * local_ch : (i + 1) * local_ch] = pair.astype(bf16)

    steps = weights.shape[1] // (PHASE * STRIDE)
    core = half_len - 2 * EDGE
    inside = ((EDGE, core),)
    outside = ((0, EDGE), (half_len - EDGE, EDGE))

    def operand(chosen):
        columns = []
        for g in range(steps):
            low_row = 2 * PHASE * (g // 2)
            pieces = [
                shifted[group, g % 2, first + low_row : first + low_row + count]
                for group, spans in chosen
                for first, count in spans
            ]
            columns.append(pieces[0] if len(pieces) == 1 else jnp.concatenate(pieces, axis=0))
        return jnp.concatenate(columns, axis=1)

    def keep_sums(a, total, spans):
        taken = 0
        for first, count in spans:
            parts = total[taken : taken + count].reshape(count // (2 * PHASE), 2, PHASE, 2 * slow_count)
            for half in range(2):
                pair = jnp.stack([parts[:, half, :, :slow_count], parts[:, half, :, slow_count:]], axis=1)
                sums[a, half, first : first + count] = pair.reshape(count, slow_count)
            taken += count

    def put(a, first, count):
        for half in range(2):
            lanes = half * half_len + first
            out_ref[a, :, lanes : lanes + count] = sums[a, half, first : first + count].T.astype(bf16)

    half_core = core // 2
    shift_rows(0, EDGE, half_core + EDGE)
    shift_rows(1, EDGE, half_core + EDGE)
    chunk = ((EDGE, half_core),)
    total = dot_f32(operand([(0, chunk)]), weights[0]) + dot_f32(operand([(1, chunk)]), weights[1])
    shift_rows(0, half_core + 2 * EDGE, half_core)
    keep_sums(0, total, chunk)
    shift_rows(1, half_core + 2 * EDGE, half_core)
    chunk = ((EDGE + half_core, half_core),)
    total = dot_f32(operand([(0, chunk)]), weights[0]) + dot_f32(operand([(1, chunk)]), weights[1])
    keep_sums(0, total, chunk)
    partial[...] = dot_f32(operand([(1, inside)]), weights[0])
    put(0, TILE, half_len - 2 * TILE)

    for beside in range(2):
        for side in range(2):
            take_edge(side, beside)

    @pl.when(me < devices - 1)
    def _():
        for copy in rim_copies:
            copy.wait_recv()

    @pl.when(is_last)
    def _():
        rim_got[...] = jnp.zeros(rim_got.shape, bf16)

    for side in range(2):
        put_edge(side, 0)
    for group in range(2):
        for row in (0, half_len):
            shift_rows(group, row, EDGE)
    around = dot_f32(operand([(0, outside), (1, outside)]), weights[0])
    rim = rim_got[...].astype(f32)
    swapped_rim = pltpu.roll(rim, STRIDE, 1)
    ext[2, top - 1 : middle - 1] = swapped_rim
    ext[2, middle - 1 : end - 1] = rim
    ext[2, top:middle, :STRIDE] = rim[:, :STRIDE]
    ext[2, middle:end, :STRIDE] = swapped_rim[:, :STRIDE]
    for side in range(2):
        put_edge(side, 1)
    shift_rows(2, 0, half_len - TILE + 2 * EDGE)
    shift_rows(2, half_len - EDGE, 2 * EDGE)
    cut = 2 * EDGE
    many = half_len - TILE - EDGE
    firsts, lasts = ((EDGE, many),), ((EDGE + many, core - many),)
    more = dot_f32(operand([(1, outside), (2, outside), (2, firsts)]), weights[1])
    shift_rows(2, half_len - TILE + 2 * EDGE, TILE - 3 * EDGE)
    keep_sums(0, around[:cut] + more[:cut], outside)
    keep_sums(1, around[cut:] + more[cut : 2 * cut], outside)
    keep_sums(1, partial[:many] + more[2 * cut :], firsts)
    more = dot_f32(operand([(2, lasts)]), weights[1])
    for first in (0, half_len - TILE):
        put(0, first, TILE)
    put(1, 0, half_len - TILE)
    keep_sums(1, partial[many:] + more, lasts)
    put(1, half_len - TILE, TILE)

    drain_exchanges()
    for side in range(2):
        for beside in range(2):

            @pl.when(leaves[side] & (me > 0) if beside else leaves[side])
            def _():
                edges[side, beside].wait_send()

    @pl.when(me > 0)
    def _():
        for copy in rim_copies:
            copy.wait_send()


def fused_body(devices, blocks, record, fk_mask, tap_table, delay_whole, tap_index):
    block_len, local_ch = record.shape
    band_rows, channels = fk_mask.shape
    slow_count = delay_whole.shape[0]
    half_len, half_rows = block_len // 2, band_rows // 2
    ahead, behind = parity_tables(block_len, devices)
    cos_twist, sin_twist = twist_tables(devices, local_ch)
    mix = local_table(local_ch)
    subarrays = local_ch // STRIDE
    span = half_len + EDGE
    bf16 = jnp.bfloat16
    vmem = pl.BlockSpec(memory_space=pltpu.VMEM)
    hbm = pl.BlockSpec(memory_space=pltpu.HBM)
    return pl.pallas_call(
        functools.partial(fused, devices, blocks),
        out_shape=pltpu.VMEM((subarrays, slow_count, block_len), bf16),
        in_specs=[hbm] * 11,
        out_specs=vmem,
        scratch_shapes=[
            pltpu.VMEM(tap_table.shape, bf16),
            pltpu.VMEM((block_len, local_ch), jnp.float32),
            pltpu.VMEM((band_rows, channels), jnp.int32),
            pltpu.VMEM((slow_count, SUBARRAY), jnp.int32),
            pltpu.VMEM((slow_count, SUBARRAY), jnp.int32),
            pltpu.VMEM((6 * local_ch, 2 * local_ch), bf16),
            pltpu.VMEM((6 * local_ch, 2 * local_ch), bf16),
            pltpu.VMEM((devices, local_ch), jnp.float32),
            pltpu.VMEM((devices, local_ch), jnp.float32),
            pltpu.VMEM(ahead.shape, bf16),
            pltpu.VMEM(behind.shape, bf16),
            pltpu.VMEM((block_len, 2 * local_ch), bf16),
            pltpu.VMEM((2, devices, band_rows, local_ch), bf16),
            pltpu.VMEM((2, devices, band_rows, local_ch), bf16),
            pltpu.VMEM((devices * half_rows, 2 * local_ch), jnp.float32),
            pltpu.VMEM((2, devices * half_rows, local_ch), jnp.float32),
            pltpu.VMEM((2, devices, band_rows, local_ch), bf16),
            pltpu.VMEM((2, devices, band_rows, local_ch), bf16),
            pltpu.VMEM((3, LEAD + block_len + 2 * EDGE, local_ch), jnp.float32),
            pltpu.VMEM((2, EDGE, local_ch), bf16),
            pltpu.VMEM((2, 2, EDGE, local_ch), bf16),
            pltpu.VMEM((half_len, local_ch), bf16),
            pltpu.VMEM((half_len, local_ch), bf16),
            pltpu.VMEM((2, (LAGS + PHASE) * STRIDE, 2 * slow_count), bf16),
            pltpu.VMEM((3, 2, span, PHASE * STRIDE), bf16),
            pltpu.VMEM((half_len - 2 * EDGE, 2 * slow_count), jnp.float32),
            pltpu.VMEM((subarrays, 2, half_len, slow_count), jnp.float32),
            pltpu.SemaphoreType.DMA((9,)),
            pltpu.SemaphoreType.DMA((3,)),
            pltpu.SemaphoreType.DMA((2, 2, devices)),
            pltpu.SemaphoreType.DMA((2, 2, devices)),
            pltpu.SemaphoreType.DMA((2, 2)),
            pltpu.SemaphoreType.DMA((2, 2)),
            pltpu.SemaphoreType.DMA((2, 2)),
        ],
        compiler_params=pltpu.CompilerParams(
            collective_id=0, has_side_effects=True, vmem_limit_bytes=60 * 2**20
        ),
    )(
        tap_table,
        record,
        fk_mask,
        delay_whole,
        tap_index,
        jnp.asarray(triple(mix)),
        jnp.asarray(triple(mix.T)),
        jnp.asarray(cos_twist),
        jnp.asarray(sin_twist),
        jnp.asarray(ahead),
        jnp.asarray(behind),
    )


def solution(mesh):
    placed = (P("tm", "chan"), P("chan", None), P(), P(), P())
    devices, blocks = mesh.shape["chan"], mesh.shape["tm"]

    def placed_body(record, *others):
        block_len, local_ch = record.shape
        if local_ch == TILE and block_len // devices == TILE:
            return fused_body(devices, blocks, record, *others)
        return body(record, *others)

    return jax.shard_map(
        placed_body, mesh=mesh, in_specs=placed, out_specs=P("chan", None, "tm"), check_vma=False
    )
```

```python
import functools
import math

import jax
import jax.numpy as jnp
import ml_dtypes
import numpy as np
from jax import lax
from jax.experimental import pallas as pl
from jax.experimental.pallas import tpu as pltpu
from jax.sharding import PartitionSpec as P

SUBARRAY = 128
STRIDE = 64
TAPS = 8
FRACS = 8
LAG = 16
RIM = 20
LAGS = 40
GROUPS = 5
SHIFTS = LAGS // GROUPS


def split_table(table):
    high = table.astype(ml_dtypes.bfloat16)
    low = (table - high.astype(np.float64)).astype(ml_dtypes.bfloat16)
    return high, low


def time_table(block_len, devices):
    half_len = block_len // 2
    freq = np.arange(half_len)
    phase = (freq[:, None] * np.arange(block_len)[None, :] % block_len) * (2.0 * math.pi / block_len)
    both = np.stack([np.cos(phase), -np.sin(phase)])
    both = both.reshape(2, devices, half_len // devices, block_len).transpose(1, 0, 2, 3)
    return split_table(both.reshape(block_len, block_len))


def local_table(local_ch):
    ids = np.arange(local_ch)
    phase = (ids[:, None] * ids[None, :] % local_ch) * (2.0 * math.pi / local_ch)
    c, s = np.cos(phase), np.sin(phase)
    return np.block([[c, -s], [s, c]]).astype(np.float32)


def twist_tables(devices, local_ch):
    phase = np.arange(devices)[:, None] * np.arange(local_ch)[None, :] * (2.0 * math.pi / (devices * local_ch))
    return np.cos(phase).astype(np.float32), np.sin(phase).astype(np.float32)


def small_dft(re, im, sign):
    count = len(re)
    if count == 1:
        return re, im
    even_re, even_im = small_dft(re[0::2], im[0::2], sign)
    odd_re, odd_im = small_dft(re[1::2], im[1::2], sign)
    out_re, out_im = [None] * count, [None] * count
    half = count // 2
    for k in range(half):
        if k == 0:
            tr, ti = odd_re[k], odd_im[k]
        elif 4 * k == count:
            tr, ti = -sign * odd_im[k], sign * odd_re[k]
        else:
            c = math.cos(2.0 * math.pi * k / count)
            s = sign * math.sin(2.0 * math.pi * k / count)
            tr = odd_re[k] * c - odd_im[k] * s
            ti = odd_im[k] * c + odd_re[k] * s
        out_re[k], out_im[k] = even_re[k] + tr, even_im[k] + ti
        out_re[k + half], out_im[k + half] = even_re[k] - tr, even_im[k] - ti
    return out_re, out_im


def flip_wavenumbers(rows_table):
    return jnp.roll(rows_table[:, ::-1], 1, axis=1)


def grouped_weights(tap_table, delay_whole, tap_index):
    table = tap_table.astype(jnp.float32)
    coeffs = []
    for tap_pos in range(TAPS):
        value = jnp.zeros(tap_index.shape, jnp.float32)
        for frac in range(FRACS):
            value = jnp.where(tap_index == frac, table[frac, tap_pos], value)
        coeffs.append(value)
    lag = (
        SHIFTS * jnp.arange(GROUPS, dtype=jnp.int32)[:, None, None, None]
        + jnp.arange(SHIFTS, dtype=jnp.int32)[None, None, :, None]
    )
    tap = lag - (delay_whole + LAG)[None, :, None, :]
    weights = jnp.zeros(tap.shape, jnp.float32)
    for tap_pos in range(TAPS):
        weights = jnp.where(tap == tap_pos, coeffs[tap_pos][None, :, None, :], weights)
    rows = GROUPS * delay_whole.shape[0]
    return weights.astype(jnp.bfloat16).reshape(rows, SHIFTS * delay_whole.shape[1])


def dot_f32(left_op, right_op, precision=None):
    return jnp.dot(left_op, right_op, precision=precision, preferred_element_type=jnp.float32)


def body(record, fk_mask, tap_table, delay_whole, tap_index):
    block_len, local_ch = record.shape
    devices = lax.axis_size("chan")
    band_rows, channels = fk_mask.shape
    slow_count = delay_whole.shape[0]
    table_hi, table_lo = time_table(block_len, devices)
    table_hi, table_lo = jnp.asarray(table_hi), jnp.asarray(table_lo)

    rec_hi = record.astype(jnp.bfloat16)
    rec_lo = (record - rec_hi.astype(jnp.float32)).astype(jnp.bfloat16)
    first = dot_f32(table_hi, jnp.concatenate([rec_hi, rec_lo], axis=1))
    spectrum = first[:, :local_ch] + first[:, local_ch:] + dot_f32(table_lo, rec_hi)
    sent = spectrum.astype(jnp.bfloat16).reshape(devices, 2 * band_rows, local_ch)
    got = lax.all_to_all(sent, "chan", split_axis=0, concat_axis=0, tiled=True)

    own_band = fk_mask.astype(jnp.float32)
    freq = lax.axis_index("chan") * band_rows + jnp.arange(band_rows, dtype=jnp.int32)
    at_zero = (freq == 0)[:, None]
    band = jnp.where(at_zero, own_band * flip_wavenumbers(own_band), own_band)
    scale = jnp.where(at_zero, 1.0, 2.0) / (block_len * channels)
    band = (band * scale).reshape(band_rows, local_ch, devices).transpose(2, 0, 1)
    band = band.reshape(devices * band_rows, local_ch)

    cos_twist, sin_twist = twist_tables(devices, local_ch)
    mix = local_table(local_ch)
    parts = got.astype(jnp.float32)
    re, im = small_dft(
        [parts[d, :band_rows] for d in range(devices)],
        [parts[d, band_rows:] for d in range(devices)],
        -1.0,
    )
    turned = []
    for d in range(devices):
        c, s = cos_twist[d][None], sin_twist[d][None]
        turned.append(jnp.concatenate([re[d] * c + im[d] * s, im[d] * c - re[d] * s], axis=1))
    wave = dot_f32(jnp.concatenate(turned, axis=0), mix, lax.Precision.HIGH)
    kept = wave * jnp.concatenate([band, band], axis=1)
    back = dot_f32(kept, mix.T, lax.Precision.HIGH).reshape(devices, band_rows, 2 * local_ch)
    re, im = [], []
    for d in range(devices):
        c, s = cos_twist[d][None], sin_twist[d][None]
        b_re, b_im = back[d, :, :local_ch], back[d, :, local_ch:]
        re.append(b_re * c - b_im * s)
        im.append(b_im * c + b_re * s)
    re, im = small_dft(re, im, 1.0)
    reach = SUBARRAY - STRIDE
    slabs = []
    for d in range(devices):
        if d + 1 < devices:
            rim = jnp.concatenate([re[d + 1][:, :reach], im[d + 1][:, :reach]], axis=1)
        else:
            rim = jnp.zeros((band_rows, 2 * reach), jnp.float32)
        slabs.append(jnp.concatenate([re[d], im[d], rim], axis=0).astype(jnp.bfloat16))
    back_got = lax.all_to_all(jnp.stack(slabs), "chan", split_axis=0, concat_axis=0, tiled=True)
    own = back_got[:, : 2 * band_rows].reshape(block_len, local_ch)
    rim = back_got[:, 2 * band_rows :].reshape(devices, band_rows, 2, reach)
    rim = rim.transpose(0, 2, 1, 3).reshape(block_len, reach)
    rows = jnp.concatenate([own, rim], axis=1)
    contract = (((0,), (0,)), ((), ()))
    field = lax.dot_general(rows, table_hi, contract, preferred_element_type=jnp.float32)
    field = field + lax.dot_general(rows, table_lo, contract, preferred_element_type=jnp.float32)
    filtered = field.astype(jnp.bfloat16)

    count = lax.axis_size("tm")
    forward = [(i, i + 1) for i in range(count - 1)]
    backward = [(i + 1, i) for i in range(count - 1)]
    low = lax.ppermute(filtered[:, block_len - RIM :], "tm", forward)
    high = lax.ppermute(filtered[:, :RIM], "tm", backward)
    extended = jnp.concatenate([low, filtered, high], axis=1)

    weights = grouped_weights(tap_table, delay_whole, tap_index)
    span = block_len + SHIFTS * (GROUPS - 1)
    shifted = jnp.stack([extended[:, r + 1 : r + 1 + span] for r in range(SHIFTS)])
    beams = []
    for a in range(local_ch // STRIDE):
        chosen = shifted[:, a * STRIDE : a * STRIDE + SUBARRAY].reshape(SHIFTS * SUBARRAY, span)
        sums = dot_f32(weights, chosen).reshape(GROUPS, slow_count, span)
        total = sums[0, :, :block_len]
        for g in range(1, GROUPS):
            total = total + sums[g, :, SHIFTS * g : SHIFTS * g + block_len]
        beams.append(total)
    return jnp.stack(beams).astype(jnp.bfloat16)


TILE = 128
EDGE = 32
LEAD = 8
PHASE = 8
MESH = pl.DeviceIdType.MESH


def flipped_bits(number, mask, count):
    result, bit = 0, 1
    while bit < count:
        digit = number // bit % 2
        result = result + (1 - digit if mask // bit % 2 else digit) * bit
        bit *= 2
    return result


def triple(table):
    high, low = split_table(table.astype(np.float64))
    return np.concatenate([high, high, low], axis=0)


def parity_tables(block_len, devices):
    half_len = block_len // 2
    count = half_len // devices // 2
    tables = []
    for parity in range(2):
        freq = np.arange(devices)[:, None] * 2 * count + 2 * np.arange(count)[None, :] + parity
        phase = (freq[:, :, None] * np.arange(half_len) % block_len) * (2.0 * math.pi / block_len)
        tables.append(np.stack([np.cos(phase), -np.sin(phase)], axis=1).reshape(half_len, half_len))
    tables = np.stack(tables)
    ahead = np.concatenate(split_table(tables), axis=2)
    back = np.concatenate(split_table(tables.transpose(0, 2, 1)), axis=2)
    return ahead, back


def split_dot(left_op, right_ref):
    high = left_op.astype(jnp.bfloat16)
    low = (left_op - high.astype(jnp.float32)).astype(jnp.bfloat16)
    return dot_f32(jnp.concatenate([high, low, high], axis=1), right_ref[...])


def fused(
    devices,
    blocks,
    tap_hbm,
    rec_hbm,
    mask_hbm,
    delay_hbm,
    index_hbm,
    mix_hbm,
    unmix_hbm,
    cos_hbm,
    sin_hbm,
    ahead_hbm,
    behind_hbm,
    out_ref,
    tap_ref,
    rec_ref,
    mask_ref,
    delay_ref,
    index_ref,
    mix_ref,
    unmix_ref,
    cos_ref,
    sin_ref,
    ahead,
    behind,
    folded,
    sent,
    got,
    wave,
    band,
    back_sent,
    back_got,
    ext,
    edge_sent,
    edge_got,
    rim_sent,
    rim_got,
    weights,
    shifted,
    partial,
    sums,
    load_sem,
    table_sem,
    send_sem,
    recv_sem,
    edge_send,
    edge_recv,
    rim_sem,
):
    me = lax.axis_index("chan")
    blk = lax.axis_index("tm")
    block_len, local_ch = rec_ref.shape
    half_len = block_len // 2
    band_rows, channels = mask_ref.shape
    half_rows = band_rows // 2
    slow_count = delay_ref.shape[0]
    f32, bf16 = jnp.float32, jnp.bfloat16
    is_first, is_last = me == 0, me == devices - 1
    low_blk, high_blk = blk > 0, blk < blocks - 1
    order = list(range(devices - 1, 0, -1))
    peer = {k: flipped_bits(me, k, devices) for k in order}

    def count_of(flag):
        return jnp.where(flag, 1, 0)

    loads = [
        pltpu.make_async_copy(source, target, load_sem.at[place])
        for place, (source, target) in enumerate(
            (
                (rec_hbm, rec_ref),
                (tap_hbm, tap_ref),
                (mask_hbm, mask_ref),
                (delay_hbm, delay_ref),
                (index_hbm, index_ref),
                (cos_hbm, cos_ref),
                (sin_hbm, sin_ref),
                (mix_hbm, mix_ref),
                (unmix_hbm, unmix_ref),
            )
        )
    ]
    tables = [
        pltpu.make_async_copy(ahead_hbm.at[0], ahead.at[0], table_sem.at[0]),
        pltpu.make_async_copy(ahead_hbm.at[1], ahead.at[1], table_sem.at[1]),
        pltpu.make_async_copy(behind_hbm, behind, table_sem.at[2]),
    ]
    loads[0].start()
    tables[0].start()

    barrier = pltpu.get_barrier_semaphore()

    def greet(block, shard):
        pl.semaphore_signal(barrier, inc=1, device_id=(block, shard), device_id_type=MESH)

    for k in order:
        greet(blk, peer[k])
    for there, block in ((low_blk, blk - 1), (high_blk, blk + 1)):

        @pl.when(there)
        def _():
            greet(block, me)

        @pl.when(there & (me < devices - 1))
        def _():
            greet(block, me + 1)

    tables[1].start()
    for load in loads[1:]:
        load.start()
    tables[2].start()

    def fold(parity):
        first, second = rec_ref[:half_len], rec_ref[half_len:]
        value = first - second if parity else first + second
        high = value.astype(bf16)
        folded[:half_len, :local_ch] = high
        folded[:half_len, local_ch:] = (value - high.astype(f32)).astype(bf16)

    copies = {}
    loads[0].wait()
    for parity in range(2):
        fold(parity)
        tables[parity].wait()
        both = dot_f32(ahead[parity, :, :half_len], folded[...])
        low = dot_f32(ahead[parity, :, half_len:], folded[:, :local_ch])
        part = (both[:, :local_ch] + both[:, local_ch:] + low).astype(bf16)
        sent[parity] = part.reshape(devices, band_rows, local_ch)
        if parity == 0:
            neighbours = count_of(low_blk) + count_of(high_blk)
            pl.semaphore_wait(barrier, devices - 1 + neighbours * (1 + count_of(me > 0)))
        for k in order:
            copies[parity, k] = pltpu.make_async_remote_copy(
                src_ref=sent.at[parity, peer[k]],
                dst_ref=got.at[parity, me],
                send_sem=send_sem.at[0, parity, k],
                recv_sem=recv_sem.at[0, parity, k],
                device_id=(blk, peer[k]),
                device_id_type=MESH,
            )
            copies[parity, k].start()
        got[parity, me] = sent[parity, me]

    for load in loads[1:]:
        load.wait()
    put_id = lax.broadcasted_iota(jnp.int32, (band_rows, band_rows), 0)
    take_id = lax.broadcasted_iota(jnp.int32, (band_rows, band_rows), 1)
    taken = jnp.where(put_id < half_rows, 2 * put_id, 2 * (put_id - half_rows) + 1)
    sort = jnp.where(take_id == taken, 1.0, 0.0).astype(bf16)
    mask = dot_f32(sort, mask_ref[...].astype(f32).astype(bf16)).astype(bf16)
    wave_id = lax.broadcasted_iota(jnp.int32, (channels, local_ch), 0)
    lane_id = lax.broadcasted_iota(jnp.int32, (channels, local_ch), 1)
    bands = []
    for k1 in range(devices):
        pick = jnp.where(wave_id == lane_id * devices + k1, 1.0, 0.0).astype(bf16)
        bands.append(dot_f32(mask, pick))
    from_id = lax.broadcasted_iota(jnp.int32, (local_ch, local_ch), 0)
    to_id = lax.broadcasted_iota(jnp.int32, (local_ch, local_ch), 1)
    row_id = lax.broadcasted_iota(jnp.int32, (band_rows, local_ch), 0)
    at_zero = (row_id == 0) & is_first
    scale = jnp.where(at_zero, 1.0, 2.0) / (block_len * channels)
    for k1 in range(devices):
        total = from_id + to_id
        if k1 == 0:
            turn = jnp.where((total == local_ch) | (total == 0), 1.0, 0.0)
        else:
            turn = jnp.where(total == local_ch - 1, 1.0, 0.0)
        mirror = dot_f32(bands[(devices - k1) % devices].astype(bf16), turn.astype(bf16))
        own = jnp.where(at_zero, bands[k1] * mirror, bands[k1]) * scale
        for parity in range(2):
            band[parity, k1 * half_rows : (k1 + 1) * half_rows] = own[parity * half_rows : (parity + 1) * half_rows]

    step = 16

    def over_channels(parity):
        for low_row in range(0, half_rows, step):
            re = [got[parity, d, low_row : low_row + step].astype(f32) for d in range(devices)]
            im = [
                got[parity, d, half_rows + low_row : half_rows + low_row + step].astype(f32)
                for d in range(devices)
            ]
            re, im = small_dft(re, im, -1.0)
            for d in range(devices):
                c, s = cos_ref[d : d + 1], sin_ref[d : d + 1]
                rows = slice(d * half_rows + low_row, d * half_rows + low_row + step)
                wave[rows, :local_ch] = re[d] * c + im[d] * s
                wave[rows, local_ch:] = im[d] * c - re[d] * s
        spread = split_dot(wave[...], mix_ref)
        kept = spread * jnp.concatenate([band[parity], band[parity]], axis=1)
        wave[...] = split_dot(kept, unmix_ref)
        for low_row in range(0, half_rows, step):
            re, im = [], []
            for d in range(devices):
                c, s = cos_ref[d : d + 1], sin_ref[d : d + 1]
                rows = slice(d * half_rows + low_row, d * half_rows + low_row + step)
                b_re, b_im = wave[rows, :local_ch], wave[rows, local_ch:]
                re.append(b_re * c - b_im * s)
                im.append(b_im * c + b_re * s)
            re, im = small_dft(re, im, 1.0)
            for d in range(devices):
                back_sent[parity, d, low_row : low_row + step] = re[d].astype(bf16)
                back_sent[parity, d, half_rows + low_row : half_rows + low_row + step] = im[d].astype(bf16)

    back_copies = {}
    for parity in range(2):
        for k in order:
            copies[parity, k].wait_recv()
        over_channels(parity)
        for k in order:
            back_copies[parity, k] = pltpu.make_async_remote_copy(
                src_ref=back_sent.at[parity, peer[k]],
                dst_ref=back_got.at[parity, me],
                send_sem=send_sem.at[1, parity, k],
                recv_sem=recv_sem.at[1, parity, k],
                device_id=(blk, peer[k]),
                device_id_type=MESH,
            )
            back_copies[parity, k].start()
        back_got[parity, me] = back_sent[parity, me]

    tables[2].wait()

    def drain_exchanges():
        for parity in range(2):
            for k in order:
                copies[parity, k].wait_send()
                back_copies[parity, k].wait_send()

    table = tap_ref[...].astype(f32)
    starts = delay_ref[...].astype(f32).T.astype(jnp.int32) + LAG
    index_t = index_ref[...].astype(f32).T.astype(jnp.int32)
    blank = jnp.zeros((PHASE * STRIDE, slow_count), bf16)
    for part in range(2):
        weights[part, LAGS * STRIDE :, :slow_count] = blank
        weights[part, : PHASE * STRIDE, slow_count:] = blank
    for first in range(0, SUBARRAY, 32):
        start = starts[first : first + 32]
        index = index_t[first : first + 32]
        coeffs = []
        for tap_pos in range(TAPS):
            value = jnp.zeros(index.shape, f32)
            for frac in range(FRACS):
                value = jnp.where(index == frac, table[frac : frac + 1, tap_pos : tap_pos + 1], value)
            coeffs.append(value)
        for lag in range(LAGS):
            value = jnp.zeros(index.shape, f32)
            for tap_pos in range(TAPS):
                if 0 <= lag - tap_pos <= 2 * LAG:
                    value = jnp.where(start == lag - tap_pos, coeffs[tap_pos], value)
            value = value.astype(bf16)
            for phase in range(2):
                part, place = divmod(first, STRIDE)
                top = (lag + PHASE * phase) * STRIDE + place
                weights[part, top : top + 32, phase * slow_count : (phase + 1) * slow_count] = value
    for parity in range(2):
        for k in order:
            back_copies[parity, k].wait_recv()
        rows = back_got[parity].reshape(half_len, local_ch)
        if parity == 0:
            even = dot_f32(behind[0], jnp.concatenate([rows, rows], axis=0))
    at_edge = jnp.concatenate([behind[1, :EDGE, :half_len], behind[1, half_len - EDGE :, :half_len]], axis=0)
    odd_edge = dot_f32(at_edge, rows)
    edge_sent[0] = (even[:EDGE] + odd_edge[:EDGE]).astype(bf16)
    edge_sent[1] = (even[half_len - EDGE :] - odd_edge[EDGE:]).astype(bf16)

    def edge_copy(side, beside):
        return pltpu.make_async_remote_copy(
            src_ref=edge_sent.at[side],
            dst_ref=edge_got.at[beside, side],
            send_sem=edge_send.at[beside, side],
            recv_sem=edge_recv.at[beside, side],
            device_id=(blk - 1 + 2 * side, me - beside),
            device_id_type=MESH,
        )

    edges = {(side, beside): edge_copy(side, beside) for side in range(2) for beside in range(2)}
    leaves = (low_blk, high_blk)
    for side in range(2):
        for beside in range(2):

            @pl.when(leaves[side] & (me > 0) if beside else leaves[side])
            def _():
                edges[side, beside].start()

    quarter = half_len // 2
    left = lax.broadcasted_iota(jnp.int32, (quarter, local_ch), 1) < STRIDE
    rim_copies, fields = [], []
    for first in (0, quarter):
        odd = dot_f32(behind[1, first : first + quarter, :half_len], rows)
        some = even[first : first + quarter]
        field = [some + odd, some - odd]
        field += [pltpu.roll(part, STRIDE, 1) for part in field]
        fields.append(field)
        rim_sent[first : first + quarter] = jnp.where(left, field[0], field[3]).astype(bf16)
        copy = pltpu.make_async_remote_copy(
            src_ref=rim_sent.at[first : first + quarter],
            dst_ref=rim_got.at[first : first + quarter],
            send_sem=rim_sem.at[0, len(rim_copies)],
            recv_sem=rim_sem.at[1, len(rim_copies)],
            device_id=(blk, me - 1),
            device_id_type=MESH,
        )
        rim_copies.append(copy)

        @pl.when(me > 0)
        def _():
            copy.start()

    early, late, swapped_early, swapped_late = [jnp.concatenate(parts, axis=0) for parts in zip(*fields)]
    top, middle, end = LEAD + EDGE, LEAD + EDGE + half_len, LEAD + EDGE + block_len
    for group, (plain, other) in enumerate((((early, late), (swapped_early, swapped_late)),) * 2):
        low_part, next_part = (other, plain) if group else (plain, other)
        for place, rows in enumerate(((top, middle), (middle, end))):
            ext[group, rows[0] - 1 : rows[1] - 1] = next_part[place]
        for place, rows in enumerate(((top, middle), (middle, end))):
            ext[group, rows[0] : rows[1], :STRIDE] = low_part[place][:, :STRIDE]

    def take_edge(side, beside):
        here = leaves[1 - side]

        @pl.when(here & (me < devices - 1) if beside else here)
        def _():
            edges[side, beside].wait_recv()

        @pl.when(jnp.logical_not(here & (me < devices - 1) if beside else here))
        def _():
            edge_got[beside, side] = jnp.zeros(edge_got.shape[2:], bf16)

    def put_edge(side, beside):
        begin = (end, LEAD)[side]
        plain = edge_got[beside, side].astype(f32)
        other = pltpu.roll(plain, STRIDE, 1)
        for group in ((2,) if beside else (0, 1)):
            low_part, next_part = (other, plain) if group == 1 else (plain, other)
            before = slice(begin - 1, begin - 1 + EDGE)
            ext[group, before] = jnp.where(left[:EDGE], ext[group, before], next_part)
            ext[group, begin : begin + EDGE, :STRIDE] = low_part[:, :STRIDE]

    pairs = PHASE // 2

    def shift_rows(group, row, count):
        for i in range(pairs):
            halves = []
            for place in (0, half_len):
                begin = top - RIM + 1 + 2 * i + row + place
                value = ext[group, begin : begin + count]
                halves.append(value.reshape(count // (2 * PHASE), 2, PHASE, local_ch))
            for odd in range(2):
                pair = jnp.stack([halves[0][:, odd], halves[1][:, odd]], axis=1).reshape(count, local_ch)
                shifted[group, odd, row : row + count, i * local_ch : (i + 1) * local_ch] = pair.astype(bf16)

    steps = weights.shape[1] // (PHASE * STRIDE)
    core = half_len - 2 * EDGE
    inside = ((EDGE, core),)
    outside = ((0, EDGE), (half_len - EDGE, EDGE))

    def operand(chosen):
        columns = []
        for g in range(steps):
            low_row = 2 * PHASE * (g // 2)
            pieces = [
                shifted[group, g % 2, first + low_row : first + low_row + count]
                for group, spans in chosen
                for first, count in spans
            ]
            columns.append(pieces[0] if len(pieces) == 1 else jnp.concatenate(pieces, axis=0))
        return jnp.concatenate(columns, axis=1)

    def keep_sums(a, total, spans):
        taken = 0
        for first, count in spans:
            parts = total[taken : taken + count].reshape(count // (2 * PHASE), 2, PHASE, 2 * slow_count)
            for half in range(2):
                pair = jnp.stack([parts[:, half, :, :slow_count], parts[:, half, :, slow_count:]], axis=1)
                sums[a, half, first : first + count] = pair.reshape(count, slow_count)
            taken += count

    def put(a, first, count):
        for half in range(2):
            lanes = half * half_len + first
            out_ref[a, :, lanes : lanes + count] = sums[a, half, first : first + count].T.astype(bf16)

    half_core = core // 2
    shift_rows(0, EDGE, half_core + EDGE)
    shift_rows(1, EDGE, half_core + EDGE)
    chunk = ((EDGE, half_core),)
    total = dot_f32(operand([(0, chunk)]), weights[0]) + dot_f32(operand([(1, chunk)]), weights[1])
    shift_rows(0, half_core + 2 * EDGE, half_core)
    keep_sums(0, total, chunk)
    shift_rows(1, half_core + 2 * EDGE, half_core)
    chunk = ((EDGE + half_core, half_core),)
    total = dot_f32(operand([(0, chunk)]), weights[0]) + dot_f32(operand([(1, chunk)]), weights[1])
    keep_sums(0, total, chunk)
    partial[...] = dot_f32(operand([(1, inside)]), weights[0])
    put(0, TILE, half_len - 2 * TILE)

    for beside in range(2):
        for side in range(2):
            take_edge(side, beside)

    @pl.when(me < devices - 1)
    def _():
        for copy in rim_copies:
            copy.wait_recv()

    @pl.when(is_last)
    def _():
        rim_got[...] = jnp.zeros(rim_got.shape, bf16)

    for side in range(2):
        put_edge(side, 0)
    for group in range(2):
        for row in (0, half_len):
            shift_rows(group, row, EDGE)
    around = dot_f32(operand([(0, outside), (1, outside)]), weights[0])
    rim = rim_got[...].astype(f32)
    swapped_rim = pltpu.roll(rim, STRIDE, 1)
    ext[2, top - 1 : middle - 1] = swapped_rim
    ext[2, middle - 1 : end - 1] = rim
    ext[2, top:middle, :STRIDE] = rim[:, :STRIDE]
    ext[2, middle:end, :STRIDE] = swapped_rim[:, :STRIDE]
    for side in range(2):
        put_edge(side, 1)
    shift_rows(2, 0, half_len + EDGE)
    cut = 2 * EDGE
    many = half_len - TILE - EDGE
    firsts, lasts = ((EDGE, many),), ((EDGE + many, core - many),)
    more = dot_f32(operand([(1, outside), (2, outside), (2, firsts)]), weights[1])
    keep_sums(0, around[:cut] + more[:cut], outside)
    keep_sums(1, around[cut:] + more[cut : 2 * cut], outside)
    keep_sums(1, partial[:many] + more[2 * cut :], firsts)
    more = dot_f32(operand([(2, lasts)]), weights[1])
    for first in (0, half_len - TILE):
        put(0, first, TILE)
    put(1, 0, half_len - TILE)
    keep_sums(1, partial[many:] + more, lasts)
    put(1, half_len - TILE, TILE)

    drain_exchanges()
    for side in range(2):
        for beside in range(2):

            @pl.when(leaves[side] & (me > 0) if beside else leaves[side])
            def _():
                edges[side, beside].wait_send()

    @pl.when(me > 0)
    def _():
        for copy in rim_copies:
            copy.wait_send()


def fused_body(devices, blocks, record, fk_mask, tap_table, delay_whole, tap_index):
    block_len, local_ch = record.shape
    band_rows, channels = fk_mask.shape
    slow_count = delay_whole.shape[0]
    half_len, half_rows = block_len // 2, band_rows // 2
    ahead, behind = parity_tables(block_len, devices)
    cos_twist, sin_twist = twist_tables(devices, local_ch)
    mix = local_table(local_ch)
    subarrays = local_ch // STRIDE
    span = half_len + EDGE
    bf16 = jnp.bfloat16
    vmem = pl.BlockSpec(memory_space=pltpu.VMEM)
    hbm = pl.BlockSpec(memory_space=pltpu.HBM)
    return pl.pallas_call(
        functools.partial(fused, devices, blocks),
        out_shape=pltpu.VMEM((subarrays, slow_count, block_len), bf16),
        in_specs=[hbm] * 11,
        out_specs=vmem,
        scratch_shapes=[
            pltpu.VMEM(tap_table.shape, bf16),
            pltpu.VMEM((block_len, local_ch), jnp.float32),
            pltpu.VMEM((band_rows, channels), jnp.int32),
            pltpu.VMEM((slow_count, SUBARRAY), jnp.int32),
            pltpu.VMEM((slow_count, SUBARRAY), jnp.int32),
            pltpu.VMEM((6 * local_ch, 2 * local_ch), bf16),
            pltpu.VMEM((6 * local_ch, 2 * local_ch), bf16),
            pltpu.VMEM((devices, local_ch), jnp.float32),
            pltpu.VMEM((devices, local_ch), jnp.float32),
            pltpu.VMEM(ahead.shape, bf16),
            pltpu.VMEM(behind.shape, bf16),
            pltpu.VMEM((half_len, 2 * local_ch), bf16),
            pltpu.VMEM((2, devices, band_rows, local_ch), bf16),
            pltpu.VMEM((2, devices, band_rows, local_ch), bf16),
            pltpu.VMEM((devices * half_rows, 2 * local_ch), jnp.float32),
            pltpu.VMEM((2, devices * half_rows, local_ch), jnp.float32),
            pltpu.VMEM((2, devices, band_rows, local_ch), bf16),
            pltpu.VMEM((2, devices, band_rows, local_ch), bf16),
            pltpu.VMEM((3, LEAD + block_len + 2 * EDGE, local_ch), jnp.float32),
            pltpu.VMEM((2, EDGE, local_ch), bf16),
            pltpu.VMEM((2, 2, EDGE, local_ch), bf16),
            pltpu.VMEM((half_len, local_ch), bf16),
            pltpu.VMEM((half_len, local_ch), bf16),
            pltpu.VMEM((2, (LAGS + PHASE) * STRIDE, 2 * slow_count), bf16),
            pltpu.VMEM((3, 2, span, PHASE * STRIDE), bf16),
            pltpu.VMEM((half_len - 2 * EDGE, 2 * slow_count), jnp.float32),
            pltpu.VMEM((subarrays, 2, half_len, slow_count), jnp.float32),
            pltpu.SemaphoreType.DMA((9,)),
            pltpu.SemaphoreType.DMA((3,)),
            pltpu.SemaphoreType.DMA((2, 2, devices)),
            pltpu.SemaphoreType.DMA((2, 2, devices)),
            pltpu.SemaphoreType.DMA((2, 2)),
            pltpu.SemaphoreType.DMA((2, 2)),
            pltpu.SemaphoreType.DMA((2, 2)),
        ],
        compiler_params=pltpu.CompilerParams(
            collective_id=0, has_side_effects=True, vmem_limit_bytes=60 * 2**20
        ),
    )(
        tap_table,
        record,
        fk_mask,
        delay_whole,
        tap_index,
        jnp.asarray(triple(mix)),
        jnp.asarray(triple(mix.T)),
        jnp.asarray(cos_twist),
        jnp.asarray(sin_twist),
        jnp.asarray(ahead),
        jnp.asarray(behind),
    )


def solution(mesh):
    placed = (P("tm", "chan"), P("chan", None), P(), P(), P())
    devices, blocks = mesh.shape["chan"], mesh.shape["tm"]

    def placed_body(record, *others):
        block_len, local_ch = record.shape
        if local_ch == TILE and block_len // devices == TILE:
            return fused_body(devices, blocks, record, *others)
        return body(record, *others)

    return jax.shard_map(
        placed_body, mesh=mesh, in_specs=placed, out_specs=P("chan", None, "tm"), check_vma=False
    )
```

```python
import functools
import math

import jax
import jax.numpy as jnp
import ml_dtypes
import numpy as np
from jax import lax
from jax.experimental import pallas as pl
from jax.experimental.pallas import tpu as pltpu
from jax.sharding import PartitionSpec as P

SUBARRAY = 128
STRIDE = 64
TAPS = 8
FRACS = 8
LAG = 16
RIM = 20
LAGS = 40
GROUPS = 5
SHIFTS = LAGS // GROUPS


def split_table(table):
    high = table.astype(ml_dtypes.bfloat16)
    low = (table - high.astype(np.float64)).astype(ml_dtypes.bfloat16)
    return high, low


def time_table(block_len, devices):
    half_len = block_len // 2
    freq = np.arange(half_len)
    phase = (freq[:, None] * np.arange(block_len)[None, :] % block_len) * (2.0 * math.pi / block_len)
    both = np.stack([np.cos(phase), -np.sin(phase)])
    both = both.reshape(2, devices, half_len // devices, block_len).transpose(1, 0, 2, 3)
    return split_table(both.reshape(block_len, block_len))


def local_table(local_ch):
    ids = np.arange(local_ch)
    phase = (ids[:, None] * ids[None, :] % local_ch) * (2.0 * math.pi / local_ch)
    c, s = np.cos(phase), np.sin(phase)
    return np.block([[c, -s], [s, c]]).astype(np.float32)


def twist_tables(devices, local_ch):
    phase = np.arange(devices)[:, None] * np.arange(local_ch)[None, :] * (2.0 * math.pi / (devices * local_ch))
    return np.cos(phase).astype(np.float32), np.sin(phase).astype(np.float32)


def small_dft(re, im, sign):
    count = len(re)
    if count == 1:
        return re, im
    even_re, even_im = small_dft(re[0::2], im[0::2], sign)
    odd_re, odd_im = small_dft(re[1::2], im[1::2], sign)
    out_re, out_im = [None] * count, [None] * count
    half = count // 2
    for k in range(half):
        if k == 0:
            tr, ti = odd_re[k], odd_im[k]
        elif 4 * k == count:
            tr, ti = -sign * odd_im[k], sign * odd_re[k]
        else:
            c = math.cos(2.0 * math.pi * k / count)
            s = sign * math.sin(2.0 * math.pi * k / count)
            tr = odd_re[k] * c - odd_im[k] * s
            ti = odd_im[k] * c + odd_re[k] * s
        out_re[k], out_im[k] = even_re[k] + tr, even_im[k] + ti
        out_re[k + half], out_im[k + half] = even_re[k] - tr, even_im[k] - ti
    return out_re, out_im


def flip_wavenumbers(rows_table):
    return jnp.roll(rows_table[:, ::-1], 1, axis=1)


def grouped_weights(tap_table, delay_whole, tap_index):
    table = tap_table.astype(jnp.float32)
    coeffs = []
    for tap_pos in range(TAPS):
        value = jnp.zeros(tap_index.shape, jnp.float32)
        for frac in range(FRACS):
            value = jnp.where(tap_index == frac, table[frac, tap_pos], value)
        coeffs.append(value)
    lag = (
        SHIFTS * jnp.arange(GROUPS, dtype=jnp.int32)[:, None, None, None]
        + jnp.arange(SHIFTS, dtype=jnp.int32)[None, None, :, None]
    )
    tap = lag - (delay_whole + LAG)[None, :, None, :]
    weights = jnp.zeros(tap.shape, jnp.float32)
    for tap_pos in range(TAPS):
        weights = jnp.where(tap == tap_pos, coeffs[tap_pos][None, :, None, :], weights)
    rows = GROUPS * delay_whole.shape[0]
    return weights.astype(jnp.bfloat16).reshape(rows, SHIFTS * delay_whole.shape[1])


def dot_f32(left_op, right_op, precision=None):
    return jnp.dot(left_op, right_op, precision=precision, preferred_element_type=jnp.float32)


def body(record, fk_mask, tap_table, delay_whole, tap_index):
    block_len, local_ch = record.shape
    devices = lax.axis_size("chan")
    band_rows, channels = fk_mask.shape
    slow_count = delay_whole.shape[0]
    table_hi, table_lo = time_table(block_len, devices)
    table_hi, table_lo = jnp.asarray(table_hi), jnp.asarray(table_lo)

    rec_hi = record.astype(jnp.bfloat16)
    rec_lo = (record - rec_hi.astype(jnp.float32)).astype(jnp.bfloat16)
    first = dot_f32(table_hi, jnp.concatenate([rec_hi, rec_lo], axis=1))
    spectrum = first[:, :local_ch] + first[:, local_ch:] + dot_f32(table_lo, rec_hi)
    sent = spectrum.astype(jnp.bfloat16).reshape(devices, 2 * band_rows, local_ch)
    got = lax.all_to_all(sent, "chan", split_axis=0, concat_axis=0, tiled=True)

    own_band = fk_mask.astype(jnp.float32)
    freq = lax.axis_index("chan") * band_rows + jnp.arange(band_rows, dtype=jnp.int32)
    at_zero = (freq == 0)[:, None]
    band = jnp.where(at_zero, own_band * flip_wavenumbers(own_band), own_band)
    scale = jnp.where(at_zero, 1.0, 2.0) / (block_len * channels)
    band = (band * scale).reshape(band_rows, local_ch, devices).transpose(2, 0, 1)
    band = band.reshape(devices * band_rows, local_ch)

    cos_twist, sin_twist = twist_tables(devices, local_ch)
    mix = local_table(local_ch)
    parts = got.astype(jnp.float32)
    re, im = small_dft(
        [parts[d, :band_rows] for d in range(devices)],
        [parts[d, band_rows:] for d in range(devices)],
        -1.0,
    )
    turned = []
    for d in range(devices):
        c, s = cos_twist[d][None], sin_twist[d][None]
        turned.append(jnp.concatenate([re[d] * c + im[d] * s, im[d] * c - re[d] * s], axis=1))
    wave = dot_f32(jnp.concatenate(turned, axis=0), mix, lax.Precision.HIGH)
    kept = wave * jnp.concatenate([band, band], axis=1)
    back = dot_f32(kept, mix.T, lax.Precision.HIGH).reshape(devices, band_rows, 2 * local_ch)
    re, im = [], []
    for d in range(devices):
        c, s = cos_twist[d][None], sin_twist[d][None]
        b_re, b_im = back[d, :, :local_ch], back[d, :, local_ch:]
        re.append(b_re * c - b_im * s)
        im.append(b_im * c + b_re * s)
    re, im = small_dft(re, im, 1.0)
    reach = SUBARRAY - STRIDE
    slabs = []
    for d in range(devices):
        if d + 1 < devices:
            rim = jnp.concatenate([re[d + 1][:, :reach], im[d + 1][:, :reach]], axis=1)
        else:
            rim = jnp.zeros((band_rows, 2 * reach), jnp.float32)
        slabs.append(jnp.concatenate([re[d], im[d], rim], axis=0).astype(jnp.bfloat16))
    back_got = lax.all_to_all(jnp.stack(slabs), "chan", split_axis=0, concat_axis=0, tiled=True)
    own = back_got[:, : 2 * band_rows].reshape(block_len, local_ch)
    rim = back_got[:, 2 * band_rows :].reshape(devices, band_rows, 2, reach)
    rim = rim.transpose(0, 2, 1, 3).reshape(block_len, reach)
    rows = jnp.concatenate([own, rim], axis=1)
    contract = (((0,), (0,)), ((), ()))
    field = lax.dot_general(rows, table_hi, contract, preferred_element_type=jnp.float32)
    field = field + lax.dot_general(rows, table_lo, contract, preferred_element_type=jnp.float32)
    filtered = field.astype(jnp.bfloat16)

    count = lax.axis_size("tm")
    forward = [(i, i + 1) for i in range(count - 1)]
    backward = [(i + 1, i) for i in range(count - 1)]
    low = lax.ppermute(filtered[:, block_len - RIM :], "tm", forward)
    high = lax.ppermute(filtered[:, :RIM], "tm", backward)
    extended = jnp.concatenate([low, filtered, high], axis=1)

    weights = grouped_weights(tap_table, delay_whole, tap_index)
    span = block_len + SHIFTS * (GROUPS - 1)
    shifted = jnp.stack([extended[:, r + 1 : r + 1 + span] for r in range(SHIFTS)])
    beams = []
    for a in range(local_ch // STRIDE):
        chosen = shifted[:, a * STRIDE : a * STRIDE + SUBARRAY].reshape(SHIFTS * SUBARRAY, span)
        sums = dot_f32(weights, chosen).reshape(GROUPS, slow_count, span)
        total = sums[0, :, :block_len]
        for g in range(1, GROUPS):
            total = total + sums[g, :, SHIFTS * g : SHIFTS * g + block_len]
        beams.append(total)
    return jnp.stack(beams).astype(jnp.bfloat16)


TILE = 128
EDGE = 32
LEAD = 8
PHASE = 8
MESH = pl.DeviceIdType.MESH


def flipped_bits(number, mask, count):
    result, bit = 0, 1
    while bit < count:
        digit = number // bit % 2
        result = result + (1 - digit if mask // bit % 2 else digit) * bit
        bit *= 2
    return result


def triple(table):
    high, low = split_table(table.astype(np.float64))
    return np.concatenate([high, high, low], axis=0)


def parity_tables(block_len, devices):
    half_len = block_len // 2
    count = half_len // devices // 2
    tables = []
    for parity in range(2):
        freq = np.arange(devices)[:, None] * 2 * count + 2 * np.arange(count)[None, :] + parity
        phase = (freq[:, :, None] * np.arange(half_len) % block_len) * (2.0 * math.pi / block_len)
        tables.append(np.stack([np.cos(phase), -np.sin(phase)], axis=1).reshape(half_len, half_len))
    tables = np.stack(tables)
    ahead = np.concatenate(split_table(tables), axis=2)
    back = np.concatenate(split_table(tables.transpose(0, 2, 1)), axis=2)
    return ahead, back


def split_dot(left_op, right_ref):
    high = left_op.astype(jnp.bfloat16)
    low = (left_op - high.astype(jnp.float32)).astype(jnp.bfloat16)
    return dot_f32(jnp.concatenate([high, low, high], axis=1), right_ref[...])


def fused(
    devices,
    blocks,
    tap_hbm,
    rec_hbm,
    mask_hbm,
    delay_hbm,
    index_hbm,
    mix_hbm,
    unmix_hbm,
    cos_hbm,
    sin_hbm,
    ahead_hbm,
    behind_hbm,
    out_ref,
    tap_ref,
    rec_ref,
    mask_ref,
    delay_ref,
    index_ref,
    mix_ref,
    unmix_ref,
    cos_ref,
    sin_ref,
    ahead,
    behind,
    folded,
    sent,
    got,
    wave,
    band,
    back_sent,
    back_got,
    ext,
    edge_sent,
    edge_got,
    rim_sent,
    rim_got,
    weights,
    shifted,
    partial,
    sums,
    load_sem,
    table_sem,
    send_sem,
    recv_sem,
    edge_send,
    edge_recv,
    rim_sem,
):
    me = lax.axis_index("chan")
    blk = lax.axis_index("tm")
    block_len, local_ch = rec_ref.shape
    half_len = block_len // 2
    band_rows, channels = mask_ref.shape
    half_rows = band_rows // 2
    slow_count = delay_ref.shape[0]
    f32, bf16 = jnp.float32, jnp.bfloat16
    is_first, is_last = me == 0, me == devices - 1
    low_blk, high_blk = blk > 0, blk < blocks - 1
    order = list(range(devices - 1, 0, -1))
    peer = {k: flipped_bits(me, k, devices) for k in order}

    def count_of(flag):
        return jnp.where(flag, 1, 0)

    loads = [
        pltpu.make_async_copy(source, target, load_sem.at[place])
        for place, (source, target) in enumerate(
            (
                (rec_hbm, rec_ref),
                (tap_hbm, tap_ref),
                (mask_hbm, mask_ref),
                (delay_hbm, delay_ref),
                (index_hbm, index_ref),
                (cos_hbm, cos_ref),
                (sin_hbm, sin_ref),
                (mix_hbm, mix_ref),
                (unmix_hbm, unmix_ref),
            )
        )
    ]
    tables = [
        pltpu.make_async_copy(ahead_hbm.at[0], ahead.at[0], table_sem.at[0]),
        pltpu.make_async_copy(ahead_hbm.at[1], ahead.at[1], table_sem.at[1]),
        pltpu.make_async_copy(behind_hbm, behind, table_sem.at[2]),
    ]
    loads[0].start()
    tables[0].start()

    barrier = pltpu.get_barrier_semaphore()

    def greet(block, shard):
        pl.semaphore_signal(barrier, inc=1, device_id=(block, shard), device_id_type=MESH)

    for k in order:
        greet(blk, peer[k])
    for there, block in ((low_blk, blk - 1), (high_blk, blk + 1)):

        @pl.when(there)
        def _():
            greet(block, me)

        @pl.when(there & (me < devices - 1))
        def _():
            greet(block, me + 1)

    tables[1].start()
    for load in loads[1:]:
        load.start()
    tables[2].start()

    def fold(parity):
        first, second = rec_ref[:half_len], rec_ref[half_len:]
        value = first - second if parity else first + second
        high = value.astype(bf16)
        folded[:half_len, :local_ch] = high
        folded[:half_len, local_ch:] = (value - high.astype(f32)).astype(bf16)
        folded[half_len:, :local_ch] = high
        folded[half_len:, local_ch:] = jnp.zeros_like(high)

    copies = {}
    loads[0].wait()
    for parity in range(2):
        fold(parity)
        tables[parity].wait()
        both = dot_f32(ahead[parity], folded[...])
        part = (both[:, :local_ch] + both[:, local_ch:]).astype(bf16)
        sent[parity] = part.reshape(devices, band_rows, local_ch)
        if parity == 0:
            neighbours = count_of(low_blk) + count_of(high_blk)
            pl.semaphore_wait(barrier, devices - 1 + neighbours * (1 + count_of(me > 0)))
        for k in order:
            copies[parity, k] = pltpu.make_async_remote_copy(
                src_ref=sent.at[parity, peer[k]],
                dst_ref=got.at[parity, me],
                send_sem=send_sem.at[0, parity, k],
                recv_sem=recv_sem.at[0, parity, k],
                device_id=(blk, peer[k]),
                device_id_type=MESH,
            )
            copies[parity, k].start()
        got[parity, me] = sent[parity, me]

    for load in loads[1:]:
        load.wait()
    put_id = lax.broadcasted_iota(jnp.int32, (band_rows, band_rows), 0)
    take_id = lax.broadcasted_iota(jnp.int32, (band_rows, band_rows), 1)
    taken = jnp.where(put_id < half_rows, 2 * put_id, 2 * (put_id - half_rows) + 1)
    sort = jnp.where(take_id == taken, 1.0, 0.0).astype(bf16)
    mask = dot_f32(sort, mask_ref[...].astype(f32).astype(bf16)).astype(bf16)
    wave_id = lax.broadcasted_iota(jnp.int32, (channels, local_ch), 0)
    lane_id = lax.broadcasted_iota(jnp.int32, (channels, local_ch), 1)
    bands = []
    for k1 in range(devices):
        pick = jnp.where(wave_id == lane_id * devices + k1, 1.0, 0.0).astype(bf16)
        bands.append(dot_f32(mask, pick))
    from_id = lax.broadcasted_iota(jnp.int32, (local_ch, local_ch), 0)
    to_id = lax.broadcasted_iota(jnp.int32, (local_ch, local_ch), 1)
    row_id = lax.broadcasted_iota(jnp.int32, (band_rows, local_ch), 0)
    at_zero = (row_id == 0) & is_first
    scale = jnp.where(at_zero, 1.0, 2.0) / (block_len * channels)
    for k1 in range(devices):
        total = from_id + to_id
        if k1 == 0:
            turn = jnp.where((total == local_ch) | (total == 0), 1.0, 0.0)
        else:
            turn = jnp.where(total == local_ch - 1, 1.0, 0.0)
        mirror = dot_f32(bands[(devices - k1) % devices].astype(bf16), turn.astype(bf16))
        own = jnp.where(at_zero, bands[k1] * mirror, bands[k1]) * scale
        for parity in range(2):
            band[parity, k1 * half_rows : (k1 + 1) * half_rows] = own[parity * half_rows : (parity + 1) * half_rows]

    step = 16

    def over_channels(parity):
        for low_row in range(0, half_rows, step):
            re = [got[parity, d, low_row : low_row + step].astype(f32) for d in range(devices)]
            im = [
                got[parity, d, half_rows + low_row : half_rows + low_row + step].astype(f32)
                for d in range(devices)
            ]
            re, im = small_dft(re, im, -1.0)
            for d in range(devices):
                c, s = cos_ref[d : d + 1], sin_ref[d : d + 1]
                rows = slice(d * half_rows + low_row, d * half_rows + low_row + step)
                wave[rows, :local_ch] = re[d] * c + im[d] * s
                wave[rows, local_ch:] = im[d] * c - re[d] * s
        spread = split_dot(wave[...], mix_ref)
        kept = spread * jnp.concatenate([band[parity], band[parity]], axis=1)
        wave[...] = split_dot(kept, unmix_ref)
        for low_row in range(0, half_rows, step):
            re, im = [], []
            for d in range(devices):
                c, s = cos_ref[d : d + 1], sin_ref[d : d + 1]
                rows = slice(d * half_rows + low_row, d * half_rows + low_row + step)
                b_re, b_im = wave[rows, :local_ch], wave[rows, local_ch:]
                re.append(b_re * c - b_im * s)
                im.append(b_im * c + b_re * s)
            re, im = small_dft(re, im, 1.0)
            for d in range(devices):
                back_sent[parity, d, low_row : low_row + step] = re[d].astype(bf16)
                back_sent[parity, d, half_rows + low_row : half_rows + low_row + step] = im[d].astype(bf16)

    back_copies = {}
    for parity in range(2):
        for k in order:
            copies[parity, k].wait_recv()
        over_channels(parity)
        for k in order:
            back_copies[parity, k] = pltpu.make_async_remote_copy(
                src_ref=back_sent.at[parity, peer[k]],
                dst_ref=back_got.at[parity, me],
                send_sem=send_sem.at[1, parity, k],
                recv_sem=recv_sem.at[1, parity, k],
                device_id=(blk, peer[k]),
                device_id_type=MESH,
            )
            back_copies[parity, k].start()
        back_got[parity, me] = back_sent[parity, me]

    tables[2].wait()

    def drain_exchanges():
        for parity in range(2):
            for k in order:
                copies[parity, k].wait_send()
                back_copies[parity, k].wait_send()

    table = tap_ref[...].astype(f32)
    starts = delay_ref[...].astype(f32).T.astype(jnp.int32) + LAG
    index_t = index_ref[...].astype(f32).T.astype(jnp.int32)
    blank = jnp.zeros((PHASE * STRIDE, slow_count), bf16)
    for part in range(2):
        weights[part, LAGS * STRIDE :, :slow_count] = blank
        weights[part, : PHASE * STRIDE, slow_count:] = blank
    for first in range(0, SUBARRAY, 32):
        start = starts[first : first + 32]
        index = index_t[first : first + 32]
        coeffs = []
        for tap_pos in range(TAPS):
            value = jnp.zeros(index.shape, f32)
            for frac in range(FRACS):
                value = jnp.where(index == frac, table[frac : frac + 1, tap_pos : tap_pos + 1], value)
            coeffs.append(value)
        for lag in range(LAGS):
            value = jnp.zeros(index.shape, f32)
            for tap_pos in range(TAPS):
                if 0 <= lag - tap_pos <= 2 * LAG:
                    value = jnp.where(start == lag - tap_pos, coeffs[tap_pos], value)
            value = value.astype(bf16)
            for phase in range(2):
                part, place = divmod(first, STRIDE)
                top = (lag + PHASE * phase) * STRIDE + place
                weights[part, top : top + 32, phase * slow_count : (phase + 1) * slow_count] = value
    for parity in range(2):
        for k in order:
            back_copies[parity, k].wait_recv()
        rows = back_got[parity].reshape(half_len, local_ch)
        if parity == 0:
            even = dot_f32(behind[0], jnp.concatenate([rows, rows], axis=0))
    at_edge = jnp.concatenate([behind[1, :EDGE, :half_len], behind[1, half_len - EDGE :, :half_len]], axis=0)
    odd_edge = dot_f32(at_edge, rows)
    edge_sent[0] = (even[:EDGE] + odd_edge[:EDGE]).astype(bf16)
    edge_sent[1] = (even[half_len - EDGE :] - odd_edge[EDGE:]).astype(bf16)

    def edge_copy(side, beside):
        return pltpu.make_async_remote_copy(
            src_ref=edge_sent.at[side],
            dst_ref=edge_got.at[beside, side],
            send_sem=edge_send.at[beside, side],
            recv_sem=edge_recv.at[beside, side],
            device_id=(blk - 1 + 2 * side, me - beside),
            device_id_type=MESH,
        )

    edges = {(side, beside): edge_copy(side, beside) for side in range(2) for beside in range(2)}
    leaves = (low_blk, high_blk)
    for side in range(2):
        for beside in range(2):

            @pl.when(leaves[side] & (me > 0) if beside else leaves[side])
            def _():
                edges[side, beside].start()

    quarter = half_len // 2
    left = lax.broadcasted_iota(jnp.int32, (quarter, local_ch), 1) < STRIDE
    rim_copies, fields = [], []
    for first in (0, quarter):
        odd = dot_f32(behind[1, first : first + quarter, :half_len], rows)
        some = even[first : first + quarter]
        field = [some + odd, some - odd]
        field += [pltpu.roll(part, STRIDE, 1) for part in field]
        fields.append(field)
        rim_sent[first : first + quarter] = jnp.where(left, field[0], field[3]).astype(bf16)
        copy = pltpu.make_async_remote_copy(
            src_ref=rim_sent.at[first : first + quarter],
            dst_ref=rim_got.at[first : first + quarter],
            send_sem=rim_sem.at[0, len(rim_copies)],
            recv_sem=rim_sem.at[1, len(rim_copies)],
            device_id=(blk, me - 1),
            device_id_type=MESH,
        )
        rim_copies.append(copy)

        @pl.when(me > 0)
        def _():
            copy.start()

    early, late, swapped_early, swapped_late = [jnp.concatenate(parts, axis=0) for parts in zip(*fields)]
    top, middle, end = LEAD + EDGE, LEAD + EDGE + half_len, LEAD + EDGE + block_len
    for group, (plain, other) in enumerate((((early, late), (swapped_early, swapped_late)),) * 2):
        low_part, next_part = (other, plain) if group else (plain, other)
        for place, rows in enumerate(((top, middle), (middle, end))):
            ext[group, rows[0] - 1 : rows[1] - 1] = next_part[place]
        for place, rows in enumerate(((top, middle), (middle, end))):
            ext[group, rows[0] : rows[1], :STRIDE] = low_part[place][:, :STRIDE]

    def take_edge(side, beside):
        here = leaves[1 - side]

        @pl.when(here & (me < devices - 1) if beside else here)
        def _():
            edges[side, beside].wait_recv()

        @pl.when(jnp.logical_not(here & (me < devices - 1) if beside else here))
        def _():
            edge_got[beside, side] = jnp.zeros(edge_got.shape[2:], bf16)

    def put_edge(side, beside):
        begin = (end, LEAD)[side]
        plain = edge_got[beside, side].astype(f32)
        other = pltpu.roll(plain, STRIDE, 1)
        for group in ((2,) if beside else (0, 1)):
            low_part, next_part = (other, plain) if group == 1 else (plain, other)
            before = slice(begin - 1, begin - 1 + EDGE)
            ext[group, before] = jnp.where(left[:EDGE], ext[group, before], next_part)
            ext[group, begin : begin + EDGE, :STRIDE] = low_part[:, :STRIDE]

    pairs = PHASE // 2

    def shift_rows(group, row, count):
        for i in range(pairs):
            halves = []
            for place in (0, half_len):
                begin = top - RIM + 1 + 2 * i + row + place
                value = ext[group, begin : begin + count]
                halves.append(value.reshape(count // (2 * PHASE), 2, PHASE, local_ch))
            for odd in range(2):
                pair = jnp.stack([halves[0][:, odd], halves[1][:, odd]], axis=1).reshape(count, local_ch)
                shifted[group, odd, row : row + count, i * local_ch : (i + 1) * local_ch] = pair.astype(bf16)

    steps = weights.shape[1] // (PHASE * STRIDE)
    core = half_len - 2 * EDGE
    inside = ((EDGE, core),)
    outside = ((0, EDGE), (half_len - EDGE, EDGE))

    def operand(chosen):
        columns = []
        for g in range(steps):
            low_row = 2 * PHASE * (g // 2)
            pieces = [
                shifted[group, g % 2, first + low_row : first + low_row + count]
                for group, spans in chosen
                for first, count in spans
            ]
            columns.append(pieces[0] if len(pieces) == 1 else jnp.concatenate(pieces, axis=0))
        return jnp.concatenate(columns, axis=1)

    def keep_sums(a, total, spans):
        taken = 0
        for first, count in spans:
            parts = total[taken : taken + count].reshape(count // (2 * PHASE), 2, PHASE, 2 * slow_count)
            for half in range(2):
                pair = jnp.stack([parts[:, half, :, :slow_count], parts[:, half, :, slow_count:]], axis=1)
                sums[a, half, first : first + count] = pair.reshape(count, slow_count)
            taken += count

    def put(a, first, count):
        for half in range(2):
            lanes = half * half_len + first
            out_ref[a, :, lanes : lanes + count] = sums[a, half, first : first + count].T.astype(bf16)

    half_core = core // 2
    shift_rows(0, EDGE, half_core + EDGE)
    shift_rows(1, EDGE, half_core + EDGE)
    chunk = ((EDGE, half_core),)
    total = dot_f32(operand([(0, chunk)]), weights[0]) + dot_f32(operand([(1, chunk)]), weights[1])
    shift_rows(0, half_core + 2 * EDGE, half_core)
    keep_sums(0, total, chunk)
    shift_rows(1, half_core + 2 * EDGE, half_core)
    chunk = ((EDGE + half_core, half_core),)
    total = dot_f32(operand([(0, chunk)]), weights[0]) + dot_f32(operand([(1, chunk)]), weights[1])
    keep_sums(0, total, chunk)
    partial[...] = dot_f32(operand([(1, inside)]), weights[0])
    put(0, TILE, half_len - 2 * TILE)

    for beside in range(2):
        for side in range(2):
            take_edge(side, beside)

    @pl.when(me < devices - 1)
    def _():
        for copy in rim_copies:
            copy.wait_recv()

    @pl.when(is_last)
    def _():
        rim_got[...] = jnp.zeros(rim_got.shape, bf16)

    for side in range(2):
        put_edge(side, 0)
    for group in range(2):
        for row in (0, half_len):
            shift_rows(group, row, EDGE)
    around = dot_f32(operand([(0, outside), (1, outside)]), weights[0])
    rim = rim_got[...].astype(f32)
    swapped_rim = pltpu.roll(rim, STRIDE, 1)
    ext[2, top - 1 : middle - 1] = swapped_rim
    ext[2, middle - 1 : end - 1] = rim
    ext[2, top:middle, :STRIDE] = rim[:, :STRIDE]
    ext[2, middle:end, :STRIDE] = swapped_rim[:, :STRIDE]
    for side in range(2):
        put_edge(side, 1)
    shift_rows(2, 0, half_len - TILE + 2 * EDGE)
    shift_rows(2, half_len - EDGE, 2 * EDGE)
    cut = 2 * EDGE
    many = half_len - TILE - EDGE
    firsts, lasts = ((EDGE, many),), ((EDGE + many, core - many),)
    more = dot_f32(operand([(1, outside), (2, outside), (2, firsts)]), weights[1])
    shift_rows(2, half_len - TILE + 2 * EDGE, TILE - 3 * EDGE)
    keep_sums(0, around[:cut] + more[:cut], outside)
    keep_sums(1, around[cut:] + more[cut : 2 * cut], outside)
    keep_sums(1, partial[:many] + more[2 * cut :], firsts)
    more = dot_f32(operand([(2, lasts)]), weights[1])
    for first in (0, half_len - TILE):
        put(0, first, TILE)
    put(1, 0, half_len - TILE)
    keep_sums(1, partial[many:] + more, lasts)
    put(1, half_len - TILE, TILE)

    drain_exchanges()
    for side in range(2):
        for beside in range(2):

            @pl.when(leaves[side] & (me > 0) if beside else leaves[side])
            def _():
                edges[side, beside].wait_send()

    @pl.when(me > 0)
    def _():
        for copy in rim_copies:
            copy.wait_send()


def fused_body(devices, blocks, record, fk_mask, tap_table, delay_whole, tap_index):
    block_len, local_ch = record.shape
    band_rows, channels = fk_mask.shape
    slow_count = delay_whole.shape[0]
    half_len, half_rows = block_len // 2, band_rows // 2
    ahead, behind = parity_tables(block_len, devices)
    cos_twist, sin_twist = twist_tables(devices, local_ch)
    mix = local_table(local_ch)
    subarrays = local_ch // STRIDE
    span = half_len + EDGE
    bf16 = jnp.bfloat16
    vmem = pl.BlockSpec(memory_space=pltpu.VMEM)
    hbm = pl.BlockSpec(memory_space=pltpu.HBM)
    return pl.pallas_call(
        functools.partial(fused, devices, blocks),
        out_shape=pltpu.VMEM((subarrays, slow_count, block_len), bf16),
        in_specs=[hbm] * 11,
        out_specs=vmem,
        scratch_shapes=[
            pltpu.VMEM(tap_table.shape, bf16),
            pltpu.VMEM((block_len, local_ch), jnp.float32),
            pltpu.VMEM((band_rows, channels), jnp.int32),
            pltpu.VMEM((slow_count, SUBARRAY), jnp.int32),
            pltpu.VMEM((slow_count, SUBARRAY), jnp.int32),
            pltpu.VMEM((6 * local_ch, 2 * local_ch), bf16),
            pltpu.VMEM((6 * local_ch, 2 * local_ch), bf16),
            pltpu.VMEM((devices, local_ch), jnp.float32),
            pltpu.VMEM((devices, local_ch), jnp.float32),
            pltpu.VMEM(ahead.shape, bf16),
            pltpu.VMEM(behind.shape, bf16),
            pltpu.VMEM((block_len, 2 * local_ch), bf16),
            pltpu.VMEM((2, devices, band_rows, local_ch), bf16),
            pltpu.VMEM((2, devices, band_rows, local_ch), bf16),
            pltpu.VMEM((devices * half_rows, 2 * local_ch), jnp.float32),
            pltpu.VMEM((2, devices * half_rows, local_ch), jnp.float32),
            pltpu.VMEM((2, devices, band_rows, local_ch), bf16),
            pltpu.VMEM((2, devices, band_rows, local_ch), bf16),
            pltpu.VMEM((3, LEAD + block_len + 2 * EDGE, local_ch), jnp.float32),
            pltpu.VMEM((2, EDGE, local_ch), bf16),
            pltpu.VMEM((2, 2, EDGE, local_ch), bf16),
            pltpu.VMEM((half_len, local_ch), bf16),
            pltpu.VMEM((half_len, local_ch), bf16),
            pltpu.VMEM((2, (LAGS + PHASE) * STRIDE, 2 * slow_count), bf16),
            pltpu.VMEM((3, 2, span, PHASE * STRIDE), bf16),
            pltpu.VMEM((half_len - 2 * EDGE, 2 * slow_count), jnp.float32),
            pltpu.VMEM((subarrays, 2, half_len, slow_count), jnp.float32),
            pltpu.SemaphoreType.DMA((9,)),
            pltpu.SemaphoreType.DMA((3,)),
            pltpu.SemaphoreType.DMA((2, 2, devices)),
            pltpu.SemaphoreType.DMA((2, 2, devices)),
            pltpu.SemaphoreType.DMA((2, 2)),
            pltpu.SemaphoreType.DMA((2, 2)),
            pltpu.SemaphoreType.DMA((2, 2)),
        ],
        compiler_params=pltpu.CompilerParams(
            collective_id=0, has_side_effects=True, vmem_limit_bytes=60 * 2**20
        ),
    )(
        tap_table,
        record,
        fk_mask,
        delay_whole,
        tap_index,
        jnp.asarray(triple(mix)),
        jnp.asarray(triple(mix.T)),
        jnp.asarray(cos_twist),
        jnp.asarray(sin_twist),
        jnp.asarray(ahead),
        jnp.asarray(behind),
    )


def solution(mesh):
    placed = (P("tm", "chan"), P("chan", None), P(), P(), P())
    devices, blocks = mesh.shape["chan"], mesh.shape["tm"]

    def placed_body(record, *others):
        block_len, local_ch = record.shape
        if local_ch == TILE and block_len // devices == TILE:
            return fused_body(devices, blocks, record, *others)
        return body(record, *others)

    return jax.shard_map(
        placed_body, mesh=mesh, in_specs=placed, out_specs=P("chan", None, "tm"), check_vma=False
    )
```
